32 devices in a mesh: dp: 8 (over z, x), pipe: 4 (over y, core).
Axes of the slice: x: 2, y: 2, z: 4, core: 2. Of those that a mesh axis runs over, the one named last changes fastest.
Arguments:
- inputs: bfloat16 [2, 9216, 768], P(None, 'dp'), may hold values from -6 to 6
- out_grad: bfloat16 [2, 9216, 768], P(None, 'dp'), may hold values from -6 to 6
- page_side: int32 [2, 8], P(None, 'dp'), may hold values from 14 to 32, as said below
- norm_gain: float32 [4, 768], P('pipe'), may hold values from 0.25 to 1.75
- norm_shift: float32 [4, 768], P('pipe'), may hold values from -3 to 3
- layer_scale: float32 [4, 768], P('pipe'), may hold values from 0.5 to 2
- w_first: bfloat16 [4, 768, 3072], P('pipe'), may hold values from -0.21875 to 0.21875
- w_half: bfloat16 [4, 1536, 768], P('pipe'), may hold values from -0.109375 to 0.109375
- rel_table: float32 [2, 12, 2, 65], replicated, may hold values from -5 to 5
Outputs:
- section_out: bfloat16 [4, 2, 9216, 768], P('pipe', None, 'dp')
- section_in_grad: float32 [4, 2, 9216, 768], P('pipe', None, 'dp')
- g_first: float32 [4, 768, 3072], P('pipe', 'dp')
- g_half: float32 [4, 1536, 768], P('pipe', 'dp')
- g_gain: float32 [4, 768], P('pipe', 'dp')
- g_shift: float32 [4, 768], P('pipe', 'dp')
- g_scale: float32 [4, 768], P('pipe', 'dp')
- g_table: float32 [2, 12, 2, 65], replicated
The draws below stay inside these ranges and needn't reach their ends.
Inputs may be any that keep to these rules, and one draw needn't show every extreme that they name: `page_side`: each entry is 14, 24 or 32; each value occurs in every draw.
All inputs are finite; a program needn't handle non-finite values.
Results may differ from the reference program's by a relative error of at most 0.018.
Values may be sent and summed in bfloat16 or wider, within the bound.
No kernel may reach another device: no remote copies, remote signals or barrier semaphores. Data moves between devices by JAX's collectives and lax.ppermute only.
A program may use at most 256 MiB of HBM per device.

```python
import math
import jax
import jax.numpy as jnp
from jax import lax

D = 768
HEADS = 12
HEAD = 64
FF = 3072
LAYERS = 2
SECTIONS = 4
MICRO = 2
SLOT = 1152
SIDE_S = 14
SIDE_M = 24
SIDE_L = 32
TABLE = 65
DATA = 8
ROWS = 9216


def draw_page_side(key, part):
    key = jax.random.fold_in(key, 7)
    first_key, second_key, third_key = jax.random.split(key, 3)
    side_list = jnp.array([SIDE_S, SIDE_M, SIDE_L], dtype=jnp.int32)
    picked = jax.random.randint(first_key, (MICRO, DATA), 0, 3)
    drawn = side_list[picked]
    large_dev = jax.random.randint(second_key, (), 0, DATA)
    small_dev = jax.random.randint(third_key, (), 0, DATA)
    columns = jnp.arange(DATA)
    drawn = drawn.at[0].set(jnp.where(columns == large_dev, SIDE_L, drawn[0]))
    drawn = drawn.at[MICRO - 1].set(jnp.where(columns == small_dev, SIDE_S, drawn[MICRO - 1]))
    drawn = drawn.at[MICRO - 1].set(jnp.where(columns == (small_dev + 1) % DATA, SIDE_M, drawn[MICRO - 1]))
    return drawn.astype(jnp.int32)


def shard_levels(key, dims, cuts, low, top_value):
    loudness, own = 1.0, jax.random.fold_in(key, 6)
    for position, parts in cuts:
        draws = jnp.exp(jax.random.uniform(jax.random.fold_in(own, position), (parts,), jnp.float32, low / len(cuts), top_value / len(cuts)))
        loudness = loudness * jnp.repeat(draws, dims[position] // parts).reshape([-1 if axis == position else 1 for axis in range(len(dims))])
    return loudness


def scatter_about(key, dims, width, limit, cuts=(), kind=jnp.bfloat16):
    values = width * jax.random.normal(key, dims, jnp.float32)
    if cuts:
        values = values * shard_levels(key, dims, cuts, -0.22, 0.18)
    return jnp.clip(values, -limit, limit).astype(kind)


def setup_inputs(seed: int = 0) -> dict:
    key_of = jax.random.split(jax.random.key(seed), 10)
    return {
        "inputs": scatter_about(key_of[0], (MICRO, ROWS, D), 1.0, 6.0, ((1, 8),)),
        "out_grad": scatter_about(key_of[1], (MICRO, ROWS, D), 1.0, 6.0, ((1, 8),)),
        "page_side": draw_page_side(jax.random.fold_in(key_of[9], 71), 0),
        "norm_gain": jnp.clip(1.0 + 0.15 * jax.random.normal(key_of[3], (SECTIONS, D), jnp.float32), 0.25, 1.75),
        "norm_shift": scatter_about(key_of[4], (SECTIONS, D), 0.5, 3.0, ((0, 4),), jnp.float32),
        "layer_scale": jnp.clip(jnp.exp(math.log(2.0) - 1.3862944 * jax.random.uniform(key_of[5], (SECTIONS, D), jnp.float32) ** shard_levels(key_of[5], (SECTIONS, D), ((0, 4),), -0.2, 0.2)), 0.5, 2.0),
        "w_first": scatter_about(key_of[6], (SECTIONS, D, FF), D ** -0.5, 0.21875, ((0, 4),)),
        "w_half": scatter_about(key_of[7], (SECTIONS, FF // 2, D), FF ** -0.5, 0.109375, ((0, 4),)),
        "rel_table": scatter_about(key_of[8], (LAYERS, HEADS, 2, TABLE), 1.0, 5.0, (), jnp.float32),
    }


@jax.custom_vjp
def low(v):
    return lax.optimization_barrier(v.astype(jnp.bfloat16)).astype(jnp.float32)

@jax.custom_vjp
def low_back(v):
    return v

def low_keep(v):
    return (low(v), None)

def low_pass(kept, grad):
    return (grad,)

def back_keep(v):
    return (v, None)

def back_low(kept, grad):
    return (low(grad),)
low.defvjp(low_keep, low_pass)
low_back.defvjp(back_keep, back_low)
EPSILON = 1e-06
MASKED = -1e+30
HIGHEST = lax.Precision.HIGHEST

def layer_norm(row_vals, gain_vec, shift_vec):
    row_mean = lax.optimization_barrier(jnp.mean(row_vals, axis=-1, keepdims=True))
    centered = row_vals - row_mean
    variance = lax.optimization_barrier(jnp.mean(centered * centered, axis=-1, keepdims=True))
    return centered * lax.rsqrt(variance + EPSILON) * gain_vec + shift_vec

def slot_layout(grid_side):
    row_ids = jnp.arange(SLOT, dtype=jnp.int32)
    page_len = grid_side * grid_side + 1
    page_count = SLOT // page_len
    page_of = jnp.minimum(row_ids // page_len, page_count)
    offset = row_ids - page_of * page_len
    patch_id = jnp.maximum(offset - 1, 0)
    inside = page_of < page_count
    class_row = offset == 0
    coord_y = jnp.where(inside, jnp.where(class_row, SIDE_L, patch_id // grid_side), 0).astype(jnp.int32)
    coord_x = jnp.where(inside, jnp.where(class_row, SIDE_L, patch_id % grid_side), 0).astype(jnp.int32)
    same_page = page_of[:, None] == page_of[None, :]
    return (same_page, coord_y, coord_x)

def attention_branch(normed, section_w, layer_table, layout):
    same_page, coord_y, coord_x = layout
    normed_low = low(normed)
    project = low(low_back(jnp.dot(normed_low, section_w[:, :3 * D], precision=HIGHEST)))
    queries = project[:, :D].reshape(SLOT, HEADS, HEAD)
    key_rows = project[:, D:2 * D].reshape(SLOT, HEADS, HEAD)
    values = project[:, 2 * D:].reshape(SLOT, HEADS, HEAD)
    diff_y = (coord_y[:, None] - coord_y[None, :] + SIDE_L).astype(jnp.int32)
    diff_x = (coord_x[:, None] - coord_x[None, :] + SIDE_L).astype(jnp.int32)
    bias = layer_table[:, 0][:, diff_y] + layer_table[:, 1][:, diff_x]
    raw_scores = jnp.einsum('qhd,khd->hqk', queries, key_rows, precision=HIGHEST) * HEAD ** (-0.5) + bias
    raw_scores = low_back(raw_scores)
    raw_scores = jnp.where(same_page[None], raw_scores, MASKED)
    attn_probs = low(jax.nn.softmax(raw_scores, axis=-1))
    context = jnp.einsum('hqk,khd->qhd', attn_probs, values, precision=HIGHEST).reshape(SLOT, D)
    context = low(low_back(context))
    return low_back(jnp.dot(context, section_w[:, 3 * D:], precision=HIGHEST))

def mlp_branch(normed, section_w, down_w):
    normed_low = low(normed)
    pre_act = low_back(jnp.dot(normed_low, section_w, precision=HIGHEST))
    hidden = low(jax.nn.gelu(pre_act, approximate=True))
    return low_back(jnp.dot(hidden, down_w, precision=HIGHEST))

def run_sections(params_in, slot_in, probe_in, grid_side):
    gain_all, shift_all, scale_all, first_all, half_all, table_all = params_in
    layout = slot_layout(grid_side)
    current = slot_in + probe_in[0]
    results = []
    for section_id in range(SECTIONS):
        normed = layer_norm(current, gain_all[section_id], shift_all[section_id])
        if section_id % 2 == 0:
            branch = attention_branch(normed, first_all[section_id], table_all[section_id // 2], layout)
        else:
            down_w = jnp.concatenate([half_all[section_id - 1], half_all[section_id]], axis=0)
            branch = mlp_branch(normed, first_all[section_id], down_w)
        result = low(current + scale_all[section_id] * branch)
        results.append(result)
        if section_id + 1 < SECTIONS:
            current = low_back(result) + probe_in[section_id + 1]
    return jnp.stack(results)

def reference(inputs, out_grad, page_side, norm_gain, norm_shift, layer_scale, w_first, w_half, rel_table):
    params = (norm_gain, norm_shift, layer_scale, w_first.astype(jnp.float32), w_half.astype(jnp.float32), rel_table)
    slots_in = inputs.astype(jnp.float32).reshape(MICRO * DATA, SLOT, D)
    slots_grad = out_grad.astype(jnp.float32).reshape(MICRO * DATA, SLOT, D)
    sides = page_side.reshape(MICRO * DATA)

    def slot_step(totals, slot_item):
        slot_in, slot_grad, grid_side = slot_item
        probes = jnp.zeros((SECTIONS, SLOT, D), jnp.float32)
        results, back_fn = jax.vjp(lambda params_in, probe_in: run_sections(params_in, slot_in, probe_in, grid_side), params, probes)
        cotangent = jnp.zeros_like(results).at[SECTIONS - 1].set(slot_grad)
        param_grads, probe_grads = back_fn(cotangent)
        totals = jax.tree.map(lambda acc_val, new_val: acc_val + new_val, totals, param_grads)
        return (totals, (results, probe_grads))
    start = jax.tree.map(jnp.zeros_like, params)
    totals, (results, probe_grads) = lax.scan(slot_step, start, (slots_in, slots_grad, sides))
    section_out = results.reshape(MICRO, DATA, SECTIONS, SLOT, D).transpose(2, 0, 1, 3, 4).reshape(SECTIONS, MICRO, ROWS, D)
    section_in_grad = probe_grads.reshape(MICRO, DATA, SECTIONS, SLOT, D).transpose(2, 0, 1, 3, 4).reshape(SECTIONS, MICRO, ROWS, D)
    g_gain, g_shift, g_scale, g_first, g_half, g_table = totals
    return (section_out.astype(jnp.bfloat16), section_in_grad, g_first, g_half, g_gain, g_shift, g_scale, g_table)
```

```python
from functools import partial

import jax
import jax.numpy as jnp
import numpy as np
from jax import lax
from jax.experimental import pallas as pl
from jax.experimental.pallas import tpu as pltpu
from jax.sharding import PartitionSpec as P

SIDE_L = 32
CELLS = SIDE_L + 1
HEAD = 64
PAIR = 2 * HEAD
PAGES = 8
STATIC = 192
LSE_AT = 4 * CELLS + PAGES
MASKED = 1e30
EPSILON = 1e-06
LOG2E = 1.4426950408889634
LN2 = 0.6931471805599453
BF = jnp.bfloat16
F32 = jnp.float32
NT = (((1,), (1,)), ((), ()))
TN = (((0,), (0,)), ((), ()))


def dot(a, b):
    return jnp.dot(a, b, preferred_element_type=F32)


def dot_nt(a, b):
    return lax.dot_general(a, b, NT, preferred_element_type=F32)


def dot_tn(a, b):
    return lax.dot_general(a, b, TN, preferred_element_type=F32)


def geometry(grid_side, row_ids, slot_rows):
    page_len = grid_side * grid_side + 1
    page_count = slot_rows // page_len
    page_of = jnp.minimum(row_ids // page_len, page_count)
    offset = row_ids - page_of * page_len
    patch_id = jnp.maximum(offset - 1, 0)
    inside = page_of < page_count
    class_row = offset == 0
    coord_y = jnp.where(inside, jnp.where(class_row, SIDE_L, patch_id // grid_side), 0)
    coord_x = jnp.where(inside, jnp.where(class_row, SIDE_L, patch_id % grid_side), 0)
    return page_of, coord_y, coord_x


def doubled(cols):
    return jnp.concatenate([cols[..., :HEAD], cols], axis=-1)


def row_features(page_of, coord_y, coord_x):
    lane = jnp.arange(128, dtype=jnp.int32)[None, :]
    hot = (lane == coord_y[:, None]) | (lane == CELLS + coord_x[:, None])
    hot = hot | (lane == 2 * CELLS + page_of[:, None])
    return hot.astype(BF)


def key_features(page_of, coord_y, coord_x):
    lane = jnp.arange(STATIC, dtype=jnp.int32)[None, :]
    at_y = SIDE_L - coord_y[:, None]
    at_x = SIDE_L - coord_x[:, None] + CELLS
    hot = (lane == at_y) | (lane == at_x)
    hot = hot | (lane == at_y + 2 * CELLS) | (lane == at_x + 2 * CELLS)
    hot = hot | (lane == 4 * CELLS + page_of[:, None])
    hot = hot | ((lane >= LSE_AT) & (lane < LSE_AT + 3))
    return doubled(hot.astype(BF))


def table_maps(rel_table):
    layers, heads = rel_table.shape[:2]
    scaled = rel_table * LOG2E
    hankel = jnp.stack([scaled[..., a : a + CELLS] for a in range(CELLS)], axis=-2)
    high = hankel.astype(BF)
    rest = (hankel - high.astype(F32)).astype(BF)
    none = jnp.zeros((layers, heads, CELLS, CELLS), BF)
    far = np.zeros((PAGES, PAGES), np.float32)
    far[:] = -MASKED
    np.fill_diagonal(far, 0.0)
    y_rows = jnp.concatenate([high[:, :, 0], none, rest[:, :, 0], none], axis=-1)
    x_rows = jnp.concatenate([none, high[:, :, 1], none, rest[:, :, 1]], axis=-1)
    grid_rows = jnp.concatenate([y_rows, x_rows], axis=-2)
    grid_rows = jnp.pad(grid_rows, ((0, 0), (0, 0), (0, 128 - 2 * CELLS), (0, STATIC - 4 * CELLS)))
    page_rows = np.zeros((128, STATIC), np.float32)
    page_rows[2 * CELLS : 2 * CELLS + PAGES, 4 * CELLS : 4 * CELLS + PAGES] = far
    return doubled(grid_rows + jnp.asarray(page_rows, BF))


def split3(value):
    high = value.astype(BF).astype(F32)
    middle = (value - high).astype(BF).astype(F32)
    return high, middle, value - high - middle


def lanes_of(rows):
    return lax.broadcasted_iota(jnp.int32, (rows, PAIR), 1)


def attn_fwd_kernel(hot_ref, map_ref, q_ref, ko_ref, kp_ref, vo_ref, vp_ref, key_ref, o_ref, qx_ref, kx_ref, vx_ref):
    rows = q_ref.shape[0]
    chunk = rows // 3
    kx_ref[:, PAIR:] = key_ref[:, PAIR:]
    lane_k = lanes_of(rows)
    lane_c = lanes_of(chunk)
    outs = []
    for head in range(2):
        mine_k = (lane_k < HEAD) if head == 0 else (lane_k >= HEAD)
        one_at = HEAD if head == 0 else 0
        for part, (k_ref, v_ref) in enumerate(((ko_ref, vo_ref), (kp_ref, vp_ref))):
            at = pl.ds(part * rows, rows)
            kx_ref[at, :PAIR] = jnp.where(mine_k, k_ref[...], key_ref[at, :PAIR])
            vx_ref[at, :] = jnp.where(mine_k, v_ref[...], jnp.where(lane_k == one_at, 1.0, 0.0).astype(BF))
        for c in range(3):
            at = pl.ds(c * chunk, chunk)
            mine = (lane_c < HEAD) if head == 0 else (lane_c >= HEAD)
            feats = dot(hot_ref[at, :], map_ref[head])
            left = jnp.where(mine, q_ref[at, :].astype(F32), feats[:, :PAIR]).astype(BF)
            right = feats[:, PAIR:]
            query = jnp.concatenate([left, right.astype(BF)], axis=1)
            scores = dot_nt(query, kx_ref[...])
            top = jnp.max(scores, axis=1, keepdims=True)
            weights = jnp.exp2(scores - top).astype(BF)
            mixed = dot(weights, vx_ref[...])
            total = mixed[:, one_at : one_at + 1]
            lse = top + jnp.log2(total)
            high, middle, low = split3(lse)
            spot = lane_c - (LSE_AT - HEAD)
            right = jnp.where(spot == 0, -high, jnp.where(spot == 1, -middle, jnp.where(spot == 2, -low, right)))
            qx_ref[head, at, :PAIR] = left
            qx_ref[head, at, PAIR:] = right.astype(BF)
            out = mixed / total
            if head == 0:
                outs.append(out)
            else:
                o_ref[at, :] = jnp.where(mine, out, outs[c]).astype(BF)


def attn_forward(hot, maps, project, partner, keys):
    rows, width = project.shape[0], project.shape[1] // 3
    pairs = width // PAIR
    col = lambda off: pl.BlockSpec((rows, PAIR), lambda g: (0, off + g))
    whole = lambda shape: pl.BlockSpec(shape, lambda g: (0,) * len(shape))
    return pl.pallas_call(
        attn_fwd_kernel,
        grid=(pairs,),
        in_specs=[
            whole((rows, 128)),
            pl.BlockSpec((2, 128, 256), lambda g: (g, 0, 0)),
            col(0),
            col(pairs),
            col(0),
            col(2 * pairs),
            col(pairs),
            whole((2 * rows, 256)),
        ],
        out_specs=[col(0), pl.BlockSpec((2, rows, 256), lambda g: (g, 0, 0))],
        out_shape=[
            jax.ShapeDtypeStruct((rows, width), BF),
            jax.ShapeDtypeStruct((2 * pairs, rows, 256), BF),
        ],
        scratch_shapes=[pltpu.VMEM((2 * rows, 256), BF), pltpu.VMEM((2 * rows, PAIR), BF)],
        compiler_params=pltpu.CompilerParams(vmem_limit_bytes=48 * 2**20),
        cost_estimate=pl.CostEstimate(flops=int(8e9), bytes_accessed=int(1e7), transcendentals=0),
        name="attn_fwd",
    )(hot, maps, project, project, partner, project, partner, keys)


def attn_bwd_kernel(hot_ref, qx_ref, q_ref, ko_ref, kp_ref, vo_ref, vp_ref, key_ref, do_ref, o_ref,
                    dq_ref, dk_ref, dv_ref, gt_ref, kx_ref, vx_ref, ds_ref):
    rows = q_ref.shape[0]
    chunk = rows // 2
    kx_ref[:, PAIR:] = key_ref[:, PAIR:]
    lane = lanes_of(rows)
    lane_c = lanes_of(chunk)
    product = do_ref[...].astype(F32) * o_ref[...].astype(F32)
    dq_halves = []
    for head in range(2):
        mine = (lane < HEAD) if head == 0 else (lane >= HEAD)
        mine_c = (lane_c < HEAD) if head == 0 else (lane_c >= HEAD)
        one_at = HEAD if head == 0 else 0
        spot = lane - one_at
        for part, (k_ref, v_ref) in enumerate(((ko_ref, vo_ref), (kp_ref, vp_ref))):
            at = pl.ds(part * rows, rows)
            kx_ref[at, :PAIR] = jnp.where(mine, k_ref[...], key_ref[at, :PAIR])
            ones = jnp.where((spot >= 0) & (spot < 3), 1.0, 0.0).astype(BF)
            vx_ref[at, :] = jnp.where(mine, v_ref[...], ones)
        delta = jnp.sum(jnp.where(mine, product, 0.0), axis=1, keepdims=True)
        high, middle, low = split3(delta)
        spread = jnp.where(spot == 0, -high, jnp.where(spot == 1, -middle, jnp.where(spot == 2, -low, 0.0)))
        d_out = jnp.where(mine, do_ref[...].astype(F32), spread).astype(BF)
        for c in range(4):
            at = pl.ds(c * chunk, chunk)
            part = c // 2
            inner = pl.ds((c % 2) * chunk, chunk)
            probs = jnp.exp2(dot_nt(kx_ref[at, :], qx_ref[head]))
            d_probs = dot_nt(vx_ref[at, :], d_out)
            d_scores = (probs * d_probs).astype(BF)
            ds_ref[at, :] = d_scores
            d_value = dot(probs.astype(BF), do_ref[...])
            d_key = dot(d_scores, q_ref[...]) * LN2
            if head == 0:
                dv_ref[part, inner, :] = d_value.astype(BF)
                dk_ref[part, inner, :] = d_key.astype(BF)
            else:
                dv_ref[part, inner, :] = jnp.where(mine_c, d_value, dv_ref[part, inner, :].astype(F32)).astype(BF)
                dk_ref[part, inner, :] = jnp.where(mine_c, d_key, dk_ref[part, inner, :].astype(F32)).astype(BF)
        d_query = dot_tn(ds_ref[...], kx_ref[...])
        high_q = d_query.astype(BF)
        low_q = (d_query - high_q.astype(F32)).astype(BF)
        gt_ref[head] = dot_tn(hot_ref[...], high_q) + dot_tn(hot_ref[...], low_q)
        dq_halves.append(d_query[:, :PAIR])
    dq_ref[...] = (jnp.where(lane < HEAD, dq_halves[0], dq_halves[1]) * HEAD**-0.5).astype(BF)


def attn_backward(hot, queries, project, partner, keys, d_context, context):
    rows, width = project.shape[0], project.shape[1] // 3
    pairs = width // PAIR
    col = lambda off: pl.BlockSpec((rows, PAIR), lambda g: (0, off + g))
    both = pl.BlockSpec((2, rows, PAIR), lambda g: (0, 0, g))
    whole = lambda shape: pl.BlockSpec(shape, lambda g: (0,) * len(shape))
    return pl.pallas_call(
        attn_bwd_kernel,
        grid=(pairs,),
        in_specs=[
            whole((rows, 128)),
            pl.BlockSpec((2, rows, 256), lambda g: (g, 0, 0)),
            col(0),
            col(pairs),
            col(0),
            col(2 * pairs),
            col(pairs),
            whole((2 * rows, 256)),
            col(0),
            col(0),
        ],
        out_specs=[col(0), both, both, pl.BlockSpec((2, 128, 256), lambda g: (g, 0, 0))],
        out_shape=[
            jax.ShapeDtypeStruct((rows, width), BF),
            jax.ShapeDtypeStruct((2, rows, width), BF),
            jax.ShapeDtypeStruct((2, rows, width), BF),
            jax.ShapeDtypeStruct((2 * pairs, 128, 256), F32),
        ],
        scratch_shapes=[
            pltpu.VMEM((2 * rows, 256), BF),
            pltpu.VMEM((2 * rows, PAIR), BF),
            pltpu.VMEM((2 * rows, rows), BF),
        ],
        compiler_params=pltpu.CompilerParams(vmem_limit_bytes=48 * 2**20),
        cost_estimate=pl.CostEstimate(flops=int(20e9), bytes_accessed=int(2e7), transcendentals=0),
        name="attn_bwd",
    )(hot, queries, project, project, partner, project, partner, keys, d_context, context)


def layer_norm(row_vals, gain_vec, shift_vec):
    row_mean = jnp.mean(row_vals, axis=-1, keepdims=True)
    centered = row_vals - row_mean
    variance = jnp.mean(centered * centered, axis=-1, keepdims=True)
    return centered * lax.rsqrt(variance + EPSILON) * gain_vec + shift_vec


def layer_norm_back(row_vals, gain_vec, d_normed, grad_out):
    row_mean = jnp.mean(row_vals, axis=-1, keepdims=True)
    centered = row_vals - row_mean
    variance = jnp.mean(centered * centered, axis=-1, keepdims=True)
    scale = lax.rsqrt(variance + EPSILON)
    nhat = centered * scale
    inner = d_normed * gain_vec
    d_in = scale * (
        inner
        - jnp.mean(inner, axis=-1, keepdims=True)
        - nhat * jnp.mean(inner * nhat, axis=-1, keepdims=True)
    )
    return grad_out + d_in, jnp.sum(nhat * d_normed, axis=0), jnp.sum(d_normed, axis=0)


def local(
    inputs, out_grad, page_side, norm_gain, norm_shift, layer_scale, w_first, w_half, rel_table
):
    place = lax.axis_index("pipe")
    sections = lax.axis_size("pipe")
    micro_count, slot_rows, width = inputs.shape
    halves = sections // micro_count
    assert halves == 2
    rows = slot_rows // halves
    micro, half = place // halves, place % halves
    swap = [(i, i ^ 1) for i in range(sections)]
    layers, heads = rel_table.shape[:2]

    first_all = lax.all_gather(w_first[0], "pipe")
    half_all = lax.all_gather(w_half[0], "pipe")
    params = lax.all_gather(jnp.stack([norm_gain[0], norm_shift[0], layer_scale[0]]), "pipe")

    side = lax.dynamic_index_in_dim(page_side, micro, 0, keepdims=False)[0]
    own_rows = lambda x: lax.dynamic_slice(x, (micro, half * rows, 0), (1, rows, width))[0]
    key_ids = (jnp.arange(slot_rows, dtype=jnp.int32) + half * rows) % slot_rows
    layout = geometry(side, key_ids, slot_rows)
    hot = row_features(*(c[:rows] for c in layout))
    keys = key_features(*layout)
    maps = table_maps(rel_table)

    current = own_rows(inputs)
    kept, outs = [], []
    for s in range(sections):
        gain, shift, scale = params[s, 0], params[s, 1], params[s, 2]
        in_float = current.astype(F32)
        normed = layer_norm(in_float, gain, shift).astype(BF)
        if s % 2 == 0:
            q_scale = np.ones((3 * width,), np.float32)
            q_scale[:width] = HEAD**-0.5 * LOG2E
            project = (dot(normed, first_all[s][:, : 3 * width]) * q_scale).astype(BF)
            partner = lax.ppermute(project[:, width:], "pipe", swap)
            context, queries = attn_forward(hot, maps[s // 2], project, partner, keys)
            branch = dot(context, first_all[s][:, 3 * width :])
            kept.append((current, normed, project, partner, context, queries, branch.astype(BF)))
        else:
            down = half_all[s - 1 : s + 1].reshape(-1, width)
            pre = dot(normed, first_all[s])
            hidden = jax.nn.gelu(pre, approximate=True).astype(BF)
            branch = dot(hidden, down)
            kept.append((current, normed, pre.astype(BF), hidden, branch.astype(BF)))
        current = (in_float + scale * branch).astype(BF)
        outs.append(current)

    grad = own_rows(out_grad)
    grads, first_grads, half_grads, vecs, tables = {}, {}, {}, {}, {}
    for s in reversed(range(sections)):
        gain, shift, scale = params[s, 0], params[s, 1], params[s, 2]
        gy = grad.astype(F32)
        d_branch = (gy * scale).astype(BF)
        if s % 2 == 0:
            section_in, normed, project, partner, context, queries, branch = kept[s]
            d_context = dot_nt(d_branch, first_all[s][:, 3 * width :]).astype(BF)
            dq, dk, dv, table = attn_backward(hot, queries, project, partner, keys, d_context, context)
            got_k, got_v = lax.ppermute((dk[1], dv[1]), "pipe", swap)
            d_project = jnp.concatenate([dq, dk[0] + got_k, dv[0] + got_v], axis=1)
            d_normed = dot_nt(d_project, first_all[s][:, : 3 * width])
            first_grads[s] = jnp.concatenate(
                [dot_tn(normed, d_project), dot_tn(context, d_branch)], axis=1
            ).astype(BF)
            tables[s // 2] = table
        else:
            section_in, normed, pre, hidden, branch = kept[s]
            down = half_all[s - 1 : s + 1].reshape(-1, width)
            d_hidden = dot_nt(d_branch, down)
            d_pre = jax.vjp(partial(jax.nn.gelu, approximate=True), pre.astype(F32))[1](d_hidden)[0].astype(BF)
            d_normed = dot_nt(d_pre, first_all[s])
            first_grads[s] = dot_tn(normed, d_pre).astype(BF)
            d_down = dot_tn(hidden, d_branch).astype(BF)
            half_grads[s - 1], half_grads[s] = jnp.split(d_down, 2, axis=0)
        d_in, g_gain, g_shift = layer_norm_back(section_in.astype(F32), gain, d_normed, gy)
        g_scale = jnp.sum(branch.astype(F32) * gy, axis=0)
        vecs[s] = jnp.stack([g_gain, g_shift, g_scale])
        grad = d_in.astype(BF)
        grads[s] = grad

    def spread(parts):
        return lax.all_to_all(jnp.stack([parts[s] for s in range(sections)]), "pipe", 0, 0)

    both = ("pipe", "dp")
    section_out = spread(outs).reshape(1, micro_count, slot_rows, width)
    in_grads = spread(grads).astype(F32).reshape(1, micro_count, slot_rows, width)
    stack = lambda parts: jnp.stack([parts[s] for s in range(sections)])
    g_first = lax.psum_scatter(stack(first_grads), "pipe", scatter_dimension=0, tiled=True)
    g_half = lax.psum_scatter(stack(half_grads), "pipe", scatter_dimension=0, tiled=True)
    g_first = lax.psum_scatter(g_first, "dp", scatter_dimension=1, tiled=True).astype(F32)
    g_half = lax.psum_scatter(g_half, "dp", scatter_dimension=1, tiled=True).astype(F32)
    pairs = np.zeros((CELLS, CELLS, 2 * SIDE_L + 1), np.float32)
    for a in range(CELLS):
        for b in range(CELLS):
            pairs[a, b, a + b] = 1.0
    table_all = []
    for layer in range(layers):
        raw = tables[layer]
        even = jnp.concatenate([raw[0::2, :, HEAD:PAIR], raw[0::2, :, PAIR:]], axis=2)
        odd = jnp.concatenate([raw[1::2, :, :HEAD], raw[1::2, :, PAIR:]], axis=2)
        cols = jnp.stack([even, odd], axis=1).reshape(heads, 128, STATIC)
        grids = jnp.stack([cols[:, :CELLS, :CELLS], cols[:, CELLS : 2 * CELLS, CELLS : 2 * CELLS]], axis=1)
        table_all.append(jnp.einsum("hcab,abt->hct", grids, pairs, precision=lax.Precision.HIGHEST))
    small = jnp.concatenate([stack(vecs).reshape(-1), jnp.stack(table_all).reshape(-1)])
    small = lax.psum(small, ("dp", "pipe"))
    vec_size = sections * 3 * width
    vec_all = small[:vec_size].reshape(sections, 3, width)
    g_table = small[vec_size:].reshape(rel_table.shape)
    share = width // lax.axis_size("dp")
    mine = lax.dynamic_slice(vec_all, (place, 0, lax.axis_index("dp") * share), (1, 3, share))
    return (section_out, in_grads, g_first, g_half, mine[:, 0], mine[:, 1], mine[:, 2], g_table)


def solution(mesh):
    in_specs = (
        P(None, "dp", None),
        P(None, "dp", None),
        P(None, "dp"),
        P("pipe", None),
        P("pipe", None),
        P("pipe", None),
        P("pipe", None, None),
        P("pipe", None, None),
        P(),
    )
    out_specs = (
        P("pipe", None, "dp", None),
        P("pipe", None, "dp", None),
        P("pipe", "dp", None),
        P("pipe", "dp", None),
        P("pipe", "dp"),
        P("pipe", "dp"),
        P("pipe", "dp"),
        P(),
    )
    return jax.shard_map(local, mesh=mesh, in_specs=in_specs, out_specs=out_specs, check_vma=False)
```

```python
from functools import partial

import jax
import jax.numpy as jnp
import numpy as np
from jax import lax
from jax.experimental import pallas as pl
from jax.experimental.pallas import tpu as pltpu
from jax.sharding import PartitionSpec as P

SIDE_L = 32
CELLS = SIDE_L + 1
HEAD = 64
PAIR = 2 * HEAD
PAGES = 8
BLOCK = 40
PAGE_AT = 3 * CELLS
MASKED = 1e30
EPSILON = 1e-06
LOG2E = 1.4426950408889634
LN2 = 0.6931471805599453
BF = jnp.bfloat16
F32 = jnp.float32
NT = (((1,), (1,)), ((), ()))
TN = (((0,), (0,)), ((), ()))


def dot(a, b):
    return jnp.dot(a, b, preferred_element_type=F32)


def dot_nt(a, b):
    return lax.dot_general(a, b, NT, preferred_element_type=F32)


def dot_tn(a, b):
    return lax.dot_general(a, b, TN, preferred_element_type=F32)


def geometry(grid_side, row_ids, slot_rows):
    page_len = grid_side * grid_side + 1
    page_count = slot_rows // page_len
    page_of = jnp.minimum(row_ids // page_len, page_count)
    offset = row_ids - page_of * page_len
    patch_id = jnp.maximum(offset - 1, 0)
    inside = page_of < page_count
    class_row = offset == 0
    coord_y = jnp.where(inside, jnp.where(class_row, SIDE_L, patch_id // grid_side), 0)
    coord_x = jnp.where(inside, jnp.where(class_row, SIDE_L, patch_id % grid_side), 0)
    return page_of, coord_y, coord_x


def row_features(page_of, coord_y, coord_x, flip):
    lane = jnp.arange(128, dtype=jnp.int32)[None, :]
    at = (lambda c: SIDE_L - c) if flip else (lambda c: c)
    hot = (lane == at(coord_y)[:, None]) | (lane == BLOCK + at(coord_x)[:, None])
    hot = hot | (lane == 2 * BLOCK + page_of[:, None])
    return hot.astype(BF)


def key_features(page_of, coord_y, coord_x):
    lane = jnp.arange(256, dtype=jnp.int32)[None, :]
    at_y = SIDE_L - coord_y[:, None]
    at_x = SIDE_L - coord_x[:, None]
    hot = (lane == at_y) | (lane == HEAD + at_y) | (lane == 128 + at_x)
    hot = hot | (lane == 128 + CELLS + at_y) | (lane == 128 + 2 * CELLS + at_x)
    hot = hot | (lane == 128 + PAGE_AT + page_of[:, None])
    return hot.astype(BF)


def table_rows(rel_table):
    layers, heads = rel_table.shape[:2]
    scaled = rel_table * LOG2E
    gap = jnp.zeros((*scaled.shape[:3], 128 - 2 * SIDE_L - 1), F32)
    scaled = jnp.concatenate([scaled[..., SIDE_L:], gap, scaled[..., :SIDE_L]], axis=-1)
    high = scaled.astype(BF).astype(F32)
    return jnp.concatenate([high, scaled - high], axis=2).reshape(layers, heads // 2, 8, 128)


def table_map(table_ref, head):
    row = lax.broadcasted_iota(jnp.int32, (BLOCK, 128), 0)
    lane = lax.broadcasted_iota(jnp.int32, (BLOCK, 128), 1)

    def grid(i, to):
        values = jnp.broadcast_to(table_ref[0, 4 * head + i : 4 * head + i + 1, :], (BLOCK, 128))
        values = pltpu.roll(values, 0, 1, stride=1, stride_axis=0)
        values = jnp.where((row < CELLS) & (lane < CELLS), values, 0.0)
        return pltpu.roll(values, to, 1) if to else values

    none = jnp.zeros((BLOCK, 128), F32)
    far = jnp.where((lane >= PAGE_AT) & (lane < PAGE_AT + PAGES) & (lane - PAGE_AT != row) & (row < PAGES), -MASKED, 0.0)
    left = [grid(0, HEAD if head == 0 else 0), none, none, none[:8]]
    right = [grid(2, CELLS), grid(1, 0) + grid(3, 2 * CELLS), far, none[:8]]
    return jnp.concatenate([jnp.concatenate(left, axis=0), jnp.concatenate(right, axis=0)], axis=1).astype(BF)


def split3(value):
    high = value.astype(BF).astype(F32)
    middle = (value - high).astype(BF).astype(F32)
    return high, middle, value - high - middle


def lanes_of(rows):
    return lax.broadcasted_iota(jnp.int32, (rows, PAIR), 1)


def attn_fwd_kernel(hot_ref, map_ref, q_ref, ko_ref, kp_ref, vo_ref, vp_ref, key_ref,
                    o_ref, rest_ref, inv_ref, w_ref, kx_ref, vx_ref):
    rows = q_ref.shape[0]
    lane = lanes_of(rows)
    for head in range(2):
        mine = (lane < HEAD) if head == 0 else (lane >= HEAD)
        one_at = HEAD if head == 0 else 0
        table = table_map(map_ref, head)
        kx, vx = kx_ref.at[head], vx_ref.at[head]
        kx[:, PAIR:] = key_ref[:, PAIR:]
        for part, (k_ref, v_ref) in enumerate(((ko_ref, vo_ref), (kp_ref, vp_ref))):
            at = pl.ds(part * rows, rows)
            kx[at, :PAIR] = jnp.where(mine, k_ref[...], key_ref[at, :PAIR])
            vx[at, :] = jnp.where(mine, v_ref[...], jnp.where(lane == one_at, 1.0, 0.0).astype(BF))
        feats = dot(hot_ref[...], table).astype(BF)
        query = jnp.concatenate([jnp.where(mine, q_ref[...], feats[:, :PAIR]), feats[:, PAIR:]], axis=1)
        scores = dot_nt(kx[...], query)
        weights = jnp.exp2(scores - jnp.max(scores, axis=0, keepdims=True)).astype(BF)
        w_ref[head] = weights
        mixed = dot_tn(vx[...], weights).T
        inv = 1.0 / mixed[:, one_at : one_at + 1]
        out = mixed * inv
        high = out.astype(BF)
        rest = (out - high.astype(F32)).astype(BF)
        inv = jnp.broadcast_to(inv, out.shape)
        if head == 0:
            o_ref[...], rest_ref[...], inv_ref[...] = high, rest, inv
        else:
            o_ref[...] = jnp.where(mine, high, o_ref[...])
            rest_ref[...] = jnp.where(mine, rest, rest_ref[...])
            inv_ref[...] = jnp.where(mine, inv, inv_ref[...])


def attn_forward(hot, maps, project, partner, keys):
    rows, width = project.shape[0], project.shape[1] // 3
    pairs = width // PAIR
    col = lambda off: pl.BlockSpec((rows, PAIR), lambda g: (0, off + g))
    return pl.pallas_call(
        attn_fwd_kernel,
        grid=(pairs,),
        in_specs=[
            whole((rows, 128)),
            pl.BlockSpec((1, 8, 128), lambda g: (g, 0, 0)),
            col(0),
            col(pairs),
            col(0),
            col(2 * pairs),
            col(pairs),
            whole((2 * rows, 256)),
        ],
        out_specs=[col(0), col(0), col(0), pl.BlockSpec((2, 2 * rows, rows), lambda g: (g, 0, 0))],
        out_shape=[
            jax.ShapeDtypeStruct((rows, width), BF),
            jax.ShapeDtypeStruct((rows, width), BF),
            jax.ShapeDtypeStruct((rows, width), F32),
            jax.ShapeDtypeStruct((2 * pairs, 2 * rows, rows), BF),
        ],
        scratch_shapes=[pltpu.VMEM((2, 2 * rows, 256), BF), pltpu.VMEM((2, 2 * rows, PAIR), BF)],
        compiler_params=params_for(56),
        cost_estimate=cost(26),
        name="attn_fwd",
    )(hot, maps, project, project, partner, project, partner, keys)


def attn_bwd_kernel(hot_ref, w_ref, q_ref, ko_ref, kp_ref, vo_ref, vp_ref, key_ref, do_ref, o_ref, rest_ref, inv_ref,
                    dq_ref, mine_ref, other_ref, gt_ref, kx_ref, vx_ref, ds_ref):
    rows = q_ref.shape[0]
    lane = lanes_of(rows)
    scaled = (do_ref[...].astype(F32) * inv_ref[...]).astype(BF)
    product = scaled.astype(F32) * (o_ref[...].astype(F32) + rest_ref[...].astype(F32))
    for head in range(2):
        mine = (lane < HEAD) if head == 0 else (lane >= HEAD)
        spot = lane - (HEAD if head == 0 else 0)
        kx, vx, ds = kx_ref.at[head], vx_ref.at[head], ds_ref.at[head]
        kx[:, PAIR:] = key_ref[:, PAIR:]
        ones = jnp.where((spot >= 0) & (spot < 3), 1.0, 0.0).astype(BF)
        for part, (k_ref, v_ref) in enumerate(((ko_ref, vo_ref), (kp_ref, vp_ref))):
            at = pl.ds(part * rows, rows)
            kx[at, :PAIR] = jnp.where(mine, k_ref[...], key_ref[at, :PAIR])
            vx[at, :] = jnp.where(mine, v_ref[...], ones)
        delta = jnp.sum(jnp.where(mine, product, 0.0), axis=1, keepdims=True)
        high, middle, low = split3(delta)
        spread = jnp.where(spot == 0, -high, jnp.where(spot == 1, -middle, jnp.where(spot == 2, -low, 0.0)))
        d_out = jnp.where(mine, scaled, spread.astype(BF))
        for part, out_ref in enumerate((mine_ref, other_ref)):
            at = pl.ds(part * rows, rows)
            weights = w_ref[head, at, :]
            d_scores = (weights.astype(F32) * dot_nt(vx[at, :], d_out)).astype(BF)
            ds[at, :] = d_scores
            d_value = dot(weights, scaled).astype(BF)
            d_key = (dot(d_scores, q_ref[...]) * LN2).astype(BF)
            if head == 0:
                out_ref[1], out_ref[0] = d_value, d_key
            else:
                out_ref[1] = jnp.where(mine, d_value, out_ref[1])
                out_ref[0] = jnp.where(mine, d_key, out_ref[0])
        d_query = dot_tn(ds[...], kx[...])
        high_q = d_query.astype(BF)
        low_q = (d_query - high_q.astype(F32)).astype(BF)
        grid = dot_tn(hot_ref[...], high_q) + dot_tn(hot_ref[...], low_q)
        row = lax.broadcasted_iota(jnp.int32, (BLOCK, 128), 0)
        column = lax.broadcasted_iota(jnp.int32, (BLOCK, 128), 1)
        for axis in range(2):
            part = grid[axis * BLOCK : (axis + 1) * BLOCK, axis * 128 : (axis + 1) * 128]
            part = pltpu.roll(part, HEAD, 1) if axis == 0 and head == 0 else part
            part = jnp.where((row < CELLS) & (column < CELLS), part, 0.0)
            along = pltpu.roll(part, 0, 1, stride=1, stride_axis=0)
            gt_ref[0, 2 * head + axis : 2 * head + axis + 1, :] = jnp.sum(along, axis=0, keepdims=True)
        d_query = (d_query[:, :PAIR] * HEAD**-0.5).astype(BF)
        dq_ref[...] = d_query if head == 0 else jnp.where(mine, d_query, dq_ref[...])
    gt_ref[0, 4:8, :] = jnp.zeros((4, 128), F32)


def attn_backward(hot, weights, project, partner, keys, d_context, outcome, first, count):
    rows, width = project.shape[0], project.shape[1] // 3
    pairs = width // PAIR
    col = lambda off: pl.BlockSpec((rows, PAIR), lambda g: (0, off + first + g))
    out = pl.BlockSpec((rows, PAIR), lambda g: (0, g))
    both = pl.BlockSpec((2, rows, PAIR), lambda g: (0, 0, g))
    return pl.pallas_call(
        attn_bwd_kernel,
        grid=(count,),
        in_specs=[
            whole((rows, 128)),
            pl.BlockSpec((2, 2 * rows, rows), lambda g: (first + g, 0, 0)),
            col(0),
            col(pairs),
            col(0),
            col(2 * pairs),
            col(pairs),
            whole((2 * rows, 256)),
            col(0),
            col(0),
            col(0),
            col(0),
        ],
        out_specs=[out, both, both, pl.BlockSpec((1, 8, 128), lambda g: (g, 0, 0))],
        out_shape=[
            jax.ShapeDtypeStruct((rows, count * PAIR), BF),
            jax.ShapeDtypeStruct((2, rows, count * PAIR), BF),
            jax.ShapeDtypeStruct((2, rows, count * PAIR), BF),
            jax.ShapeDtypeStruct((count, 8, 128), F32),
        ],
        scratch_shapes=[
            pltpu.VMEM((2, 2 * rows, 256), BF),
            pltpu.VMEM((2, 2 * rows, PAIR), BF),
            pltpu.VMEM((2, 2 * rows, rows), BF),
        ],
        compiler_params=params_for(56),
        cost_estimate=cost(6 * count),
        name="attn_bwd",
    )(hot, weights, project, project, partner, project, partner, keys, d_context, *outcome)


def centred(values):
    values = values - jnp.mean(values, axis=-1, keepdims=True)
    inv = lax.rsqrt(jnp.mean(values * values, axis=-1, keepdims=True) + EPSILON)
    return values * inv, inv


def start_first(info_ref, kind, cols, refs, dst, sem):
    own, near, far_own, far_other = refs
    local, core = info_ref[0] == 1, info_ref[1]
    part = far_own.shape[0]

    @pl.when(local & (core == kind))
    def _():
        pltpu.make_async_copy(own.at[:, cols], dst, sem).start()

    @pl.when(local & (core != kind))
    def _():
        pltpu.make_async_copy(near.at[:, cols], dst, sem).start()

    @pl.when(jnp.logical_not(local))
    def _():
        pltpu.make_async_copy(far_own.at[:, cols], dst.at[pl.ds(core * part, part)], sem).start()
        pltpu.make_async_copy(far_other.at[:, cols], dst.at[pl.ds((1 - core) * part, part)], sem).start()


def start_down(info_ref, refs, dst, sem):
    own, near, *far = refs
    local, core = info_ref[0] == 1, info_ref[1]
    part, cut = own.shape[0], far[0].shape[0]
    cuts = part // cut

    @pl.when(local)
    def _():
        pltpu.make_async_copy(own, dst.at[pl.ds(core * part, part)], sem).start()
        pltpu.make_async_copy(near, dst.at[pl.ds((1 - core) * part, part)], sem).start()

    @pl.when(jnp.logical_not(local))
    def _():
        for i in range(2 * cuts):
            at = (core if i < cuts else 1 - core) * part + (i % cuts) * cut
            pltpu.make_async_copy(far[i], dst.at[pl.ds(at, cut)], sem).start()


def wait_for(dst, sem):
    pltpu.make_async_copy(dst, dst, sem).wait()


EARLY = True
SMEM = pl.BlockSpec(memory_space=pltpu.SMEM)
ANY = pl.BlockSpec(memory_space=pl.ANY)


def whole(shape):
    return pl.BlockSpec(shape, lambda *g: (0,) * len(shape))


def params_for(mib):
    return pltpu.CompilerParams(vmem_limit_bytes=mib * 2**20)


def cost(us):
    return pl.CostEstimate(flops=int(us * 2e7), bytes_accessed=1000, transcendentals=0)


def project_kernel(info_ref, x_ref, p_ref, own, near, far_own, far_other, normed_ref, out_ref, w_ref, sem):
    width = x_ref.shape[1]
    start_first(info_ref, 0, pl.ds(0, 3 * width), (own, near, far_own, far_other), w_ref, sem)
    nhat, _ = centred(x_ref[...].astype(F32))
    normed = (nhat * p_ref[0:1, :] + p_ref[1:2, :]).astype(BF)
    normed_ref[...] = normed
    wait_for(w_ref, sem)
    for j in range(3):
        at = pl.ds(j * width, width)
        value = dot(normed, w_ref[:, at])
        if j == 0:
            value = value * (HEAD**-0.5 * LOG2E)
        out_ref[:, at] = value.astype(BF)


def project(info, x, p, first_refs):
    rows, width = x.shape
    return pl.pallas_call(
        project_kernel,
        in_specs=[SMEM, whole(x.shape), whole(p.shape)] + [ANY] * 4,
        out_specs=[whole((rows, width)), whole((rows, 3 * width))],
        out_shape=[jax.ShapeDtypeStruct((rows, width), BF), jax.ShapeDtypeStruct((rows, 3 * width), BF)],
        scratch_shapes=[pltpu.VMEM((width, 3 * width), BF), pltpu.SemaphoreType.DMA],
        compiler_params=params_for(40),
        cost_estimate=cost(5),
        name="project",
    )(info, x, p, *first_refs)


def block_out_kernel(info_ref, x_ref, ctx_ref, p0_ref, p1_ref, *refs):
    att, up, refs = refs[:4], refs[:2] + refs[4:6], refs[6:]
    down, refs = refs[:8], refs[8:]
    b0_ref, x1_ref, n1_ref, slope_ref, hid_ref, b1_ref, x2_ref, wo_ref, wu_ref, wd_ref, slopes, hiddens, sems, out_sems = refs
    width = x_ref.shape[1]
    start_first(info_ref, 0, pl.ds(3 * width, width), att, wo_ref, sems.at[0])
    for j in range(4):
        start_first(info_ref, 1, pl.ds(j * width, width), up, wu_ref.at[j], sems.at[1 + j])
    start_down(info_ref, down, wd_ref, sems.at[5])
    wait_for(wo_ref, sems.at[0])
    branch = dot(ctx_ref[...], wo_ref[...])
    b0_ref[...] = branch.astype(BF)
    x1 = (x_ref[...].astype(F32) + p0_ref[2:3, :] * branch).astype(BF)
    x1_ref[...] = x1
    x1 = x1.astype(F32)
    nhat, _ = centred(x1)
    normed = (nhat * p1_ref[0:1, :] + p1_ref[1:2, :]).astype(BF)
    n1_ref[...] = normed
    for j in range(4):
        wait_for(wu_ref.at[j], sems.at[1 + j])
    wait_for(wd_ref, sems.at[5])
    total = jnp.zeros(x1.shape, F32)
    for j in range(4):
        at = pl.ds(j * width, width)
        v = dot(normed, wu_ref[j])
        square = v * v
        bend = jnp.tanh(v * (0.7978845608028654 + (0.7978845608028654 * 0.044715) * square))
        up_half = 0.5 + 0.5 * bend
        along = v * (2 * 0.7978845608028654 + (6 * 0.7978845608028654 * 0.044715) * square)
        slopes[j] = (up_half + along * (up_half * (1.0 - up_half))).astype(BF)
        hiddens[j] = (v * up_half).astype(BF)
        if EARLY:
            pltpu.make_async_copy(slopes.at[j], slope_ref.at[:, at], out_sems.at[0, j]).start()
            pltpu.make_async_copy(hiddens.at[j], hid_ref.at[:, at], out_sems.at[1, j]).start()
        total = total + dot(hiddens[j], wd_ref[at, :])
    b1_ref[...] = total.astype(BF)
    x2_ref[...] = (x1 + p1_ref[2:3, :] * total).astype(BF)
    if not EARLY:
        for j in range(4):
            at = pl.ds(j * width, width)
            pltpu.make_async_copy(slopes.at[j], slope_ref.at[:, at], out_sems.at[0, j]).start()
            pltpu.make_async_copy(hiddens.at[j], hid_ref.at[:, at], out_sems.at[1, j]).start()
    for j in range(4):
        wait_for(slopes.at[j], out_sems.at[0, j])
        wait_for(hiddens.at[j], out_sems.at[1, j])


def block_out(info, x, context, p0, p1, att_refs, up_refs, down_refs):
    rows, width = x.shape
    one = whole((rows, width))
    shape = lambda n: jax.ShapeDtypeStruct((rows, n), BF)
    widths = [width, width, width, 4 * width, 4 * width, width, width]
    refs = (*att_refs, *up_refs[2:], *down_refs)
    return pl.pallas_call(
        block_out_kernel,
        grid=(1,),
        in_specs=[SMEM, one, one, whole(p0.shape), whole(p1.shape)] + [ANY] * len(refs),
        out_specs=[one if n == width else ANY for n in widths],
        out_shape=[shape(n) for n in widths],
        scratch_shapes=[
            pltpu.VMEM((width, width), BF),
            pltpu.VMEM((4, width, width), BF),
            pltpu.VMEM((4 * width, width), BF),
            pltpu.VMEM((4, rows, width), BF),
            pltpu.VMEM((4, rows, width), BF),
            pltpu.SemaphoreType.DMA((6,)),
            pltpu.SemaphoreType.DMA((2, 4)),
        ],
        compiler_params=params_for(58),
        cost_estimate=cost(12),
        name="block_out",
    )(info, x, context, p0, p1, *refs)


def norm_back(x, gain, d_normed, gy):
    nhat, inv = centred(x)
    inner = d_normed * gain
    shift = jnp.mean(inner, axis=-1, keepdims=True)
    along = jnp.mean(inner * nhat, axis=-1, keepdims=True)
    total = lambda v: jnp.sum(v, axis=0, keepdims=True)
    return gy + inv * (inner - shift - nhat * along), total(nhat * d_normed), total(d_normed)


def block_back_kernel(info_ref, gy_ref, x1_ref, slope_ref, b1_ref, b0_ref, p0_ref, p1_ref, *refs):
    att, up, refs = refs[:4], refs[:2] + refs[4:6], refs[6:]
    down, refs = refs[:8], refs[8:]
    db1_ref, dpre_ref, gx_ref, db0_ref, dctx_ref, vec_ref, wo_ref, wu_ref, wd_ref, slopes, given, sems, more_sems = refs
    width = gy_ref.shape[1]
    start_down(info_ref, down, wd_ref, sems.at[5])
    for j in range(4):
        at = pl.ds(j * width, width)
        start_first(info_ref, 1, at, up, wu_ref.at[j], sems.at[1 + j])
        pltpu.make_async_copy(slope_ref.at[:, at], slopes.at[j], more_sems.at[0, j]).start()
    start_first(info_ref, 0, pl.ds(3 * width, width), att, wo_ref, sems.at[0])
    total = lambda v: jnp.sum(v, axis=0, keepdims=True)
    gy = gy_ref[...].astype(F32)
    d_branch = (gy * p1_ref[2:3, :]).astype(BF)
    db1_ref[...] = d_branch
    vec_ref[2:3, :] = total(b1_ref[...].astype(F32) * gy)
    vec_ref[4:, :] = jnp.zeros((4, width), F32)
    d_normed = jnp.zeros(gy.shape, F32)
    wait_for(wd_ref, sems.at[5])
    for j in range(4):
        wait_for(slopes.at[j], more_sems.at[0, j])
        wait_for(wu_ref.at[j], sems.at[1 + j])
    for j in range(4):
        at = pl.ds(j * width, width)
        d_hidden = dot_nt(d_branch, wd_ref[at, :])
        given[j] = (d_hidden * slopes[j].astype(F32)).astype(BF)
        if EARLY:
            pltpu.make_async_copy(given.at[j], dpre_ref.at[:, at], more_sems.at[1, j]).start()
        d_normed = d_normed + dot_nt(given[j], wu_ref[j])
    if not EARLY:
        for j in range(4):
            pltpu.make_async_copy(given.at[j], dpre_ref.at[:, pl.ds(j * width, width)], more_sems.at[1, j]).start()
    gx, g_gain, g_shift = norm_back(x1_ref[...].astype(F32), p1_ref[0:1, :], d_normed, gy)
    vec_ref[0:1, :] = g_gain
    vec_ref[1:2, :] = g_shift
    gx = gx.astype(BF)
    gx_ref[...] = gx
    gx = gx.astype(F32)
    d_att = (gx * p0_ref[2:3, :]).astype(BF)
    db0_ref[...] = d_att
    vec_ref[3:4, :] = total(b0_ref[...].astype(F32) * gx)
    wait_for(wo_ref, sems.at[0])
    dctx_ref[...] = dot_nt(d_att, wo_ref[...]).astype(BF)
    for j in range(4):
        wait_for(given.at[j], more_sems.at[1, j])


def block_back(info, gy, x1, slope, b1, b0, p0, p1, att_refs, up_refs, down_refs):
    rows, width = gy.shape
    one = whole((rows, width))
    shape = lambda n: jax.ShapeDtypeStruct((rows, n), BF)
    widths = [width, 4 * width, width, width, width]
    refs = (*att_refs, *up_refs[2:], *down_refs)
    return pl.pallas_call(
        block_back_kernel,
        grid=(1,),
        in_specs=[SMEM, one, one, ANY, one, one, whole(p0.shape), whole(p1.shape)] + [ANY] * len(refs),
        out_specs=[one if n == width else ANY for n in widths] + [whole((8, width))],
        out_shape=[shape(n) for n in widths] + [jax.ShapeDtypeStruct((8, width), F32)],
        scratch_shapes=[
            pltpu.VMEM((width, width), BF),
            pltpu.VMEM((4, width, width), BF),
            pltpu.VMEM((4 * width, width), BF),
            pltpu.VMEM((4, rows, width), BF),
            pltpu.VMEM((4, rows, width), BF),
            pltpu.SemaphoreType.DMA((6,)),
            pltpu.SemaphoreType.DMA((2, 4)),
        ],
        compiler_params=params_for(58),
        cost_estimate=cost(14),
        name="block_back",
    )(info, gy, x1, slope, b1, b0, p0, p1, *refs)


def project_back_kernel(info_ref, gy_ref, x_ref, p_ref, dqa, dqb, mya, myb, gota, gotb, own, near, far_own, far_other,
                        dproj_ref, gx_ref, vec_ref, w_ref, sem):
    width = x_ref.shape[1]
    start_first(info_ref, 0, pl.ds(0, 3 * width), (own, near, far_own, far_other), w_ref, sem)
    half = width // 2
    for i, (dq, my, got) in enumerate(((dqa, mya, gota), (dqb, myb, gotb))):
        dproj_ref[:, i * half : (i + 1) * half] = dq[...]
        for j in range(2):
            at = pl.ds((1 + j) * width + i * half, half)
            dproj_ref[:, at] = (my[j].astype(F32) + got[j].astype(F32)).astype(BF)
    wait_for(w_ref, sem)
    d_normed = dot_nt(dproj_ref[:, :width], w_ref[:, :width])
    for j in (1, 2):
        at = pl.ds(j * width, width)
        d_normed = d_normed + dot_nt(dproj_ref[:, at], w_ref[:, at])
    gx, g_gain, g_shift = norm_back(x_ref[...].astype(F32), p_ref[0:1, :], d_normed, gy_ref[...].astype(F32))
    gx_ref[...] = gx.astype(BF)
    vec_ref[0:1, :] = g_gain
    vec_ref[1:2, :] = g_shift
    vec_ref[2:, :] = jnp.zeros((6, width), F32)


def project_back(info, gy, x, p, parts, first_refs):
    rows, width = x.shape
    one = whole((rows, width))
    return pl.pallas_call(
        project_back_kernel,
        in_specs=[SMEM, one, one, whole(p.shape)] + [whole(v.shape) for v in parts] + [ANY] * 4,
        out_specs=[whole((rows, 3 * width)), one, whole((8, width))],
        out_shape=[
            jax.ShapeDtypeStruct((rows, 3 * width), BF),
            jax.ShapeDtypeStruct((rows, width), BF),
            jax.ShapeDtypeStruct((8, width), F32),
        ],
        grid=(1,),
        scratch_shapes=[pltpu.VMEM((width, 3 * width), BF), pltpu.SemaphoreType.DMA],
        compiler_params=params_for(48),
        cost_estimate=cost(7),
        name="project_back",
    )(info, gy, x, p, *parts, *first_refs)


def gather_kernel(info_ref, mine, by_x, by_z, diag_x, diag_z, out_ref, sem):
    quarter = mine.shape[0]
    part = quarter // 2
    q = info_ref[0]
    at = lambda i: pl.multiple_of(i * quarter, part)
    pltpu.make_async_copy(mine, out_ref.at[pl.ds(at(q), quarter)], sem).start()
    pltpu.make_async_copy(by_x, out_ref.at[pl.ds(at(info_ref[1]), quarter)], sem).start()
    pltpu.make_async_copy(by_z, out_ref.at[pl.ds(at(info_ref[2]), quarter)], sem).start()
    pltpu.make_async_copy(diag_x, out_ref.at[pl.ds(at(info_ref[3]), part)], sem).start()
    pltpu.make_async_copy(diag_z, out_ref.at[pl.ds(at(info_ref[3]) + part, part)], sem).start()
    wait_for(out_ref, sem)


def dp_swap(value, bit):
    return lax.ppermute(value, "dp", [(i, i ^ bit) for i in range(lax.axis_size("dp"))])


def tie(value, *deps):
    return lax.optimization_barrier((value, deps))[0]


def hold(values, count):
    state = values[-1]
    if not isinstance(state, list):
        return lax.optimization_barrier(values)
    arrays = [part[:2] for part in state]
    *values, arrays = lax.optimization_barrier((*values[:count], arrays))
    return (*values, [(*part, names) for part, (_, _, names) in zip(arrays, state)])


def together(values):
    return lax.optimization_barrier(values)


def quad_start(mine):
    return (mine, *together((dp_swap(mine, 1), dp_swap(mine, 2))))


def quad_end(mine, by_x, by_z):
    part = mine.shape[0] // 2
    return (mine, by_x, by_z, *together((dp_swap(by_z[:part], 1), dp_swap(by_x[part:], 2))))


def quad_place(mine, *others):
    quarter = mine.shape[0]
    q = lax.axis_index("dp") % 4
    spots = jnp.stack([q, q ^ 1, q ^ 2, q ^ 3]).astype(jnp.int32)
    return pl.pallas_call(
        gather_kernel,
        in_specs=[SMEM] + [ANY] * 5,
        out_specs=whole((4 * quarter, *mine.shape[1:])),
        out_shape=jax.ShapeDtypeStruct((4 * quarter, *mine.shape[1:]), mine.dtype),
        scratch_shapes=[pltpu.SemaphoreType.DMA],
        compiler_params=params_for(16),
        cost_estimate=cost(3),
        name="assemble",
    )(spots, mine, *others)


def put_rows(values, slot, tmp_ref, keep_ref, send_ref, core, for_d, at, sems):
    tmp = tmp_ref.at[slot].reshape(values.shape)
    tmp[...] = values
    pltpu.make_async_copy(tmp.at[:, core], keep_ref.at[for_d, at], sems.at[slot, 0]).start()
    pltpu.make_async_copy(tmp.at[:, 1 - core], send_ref.at[for_d, at], sems.at[slot, 1]).start()


def mlp_grads_kernel(core_ref, n_ref, pre_ref, hid_ref, db_ref, keep_ref, send_ref, tmp_ref, sems):
    core, j = core_ref[0], pl.program_id(0)
    width = n_ref.shape[1]
    size = keep_ref.shape[0]
    short, long = width // (2 * size), 2 * width // (2 * size)

    def finish(slot, long_rows):
        for i, ref in enumerate((keep_ref, send_ref)):
            to = ref.at[pl.ds(0, size // 2), pl.ds(0, long)] if long_rows else ref.at[:, pl.ds(0, short)]
            pltpu.make_async_copy(to, to, sems.at[slot, i]).wait()

    @pl.when(j > 0)
    def _():
        finish(0, False)
    up = dot_tn(n_ref[...], pre_ref[...]).astype(BF).reshape(size, 2, short, width)
    put_rows(up, 0, tmp_ref, keep_ref, send_ref, core, pl.ds(0, size), pl.ds(j * short, short), sems)

    @pl.when(j > 0)
    def _():
        finish(1, True)
    down = dot_tn(hid_ref[...], db_ref[...]).astype(BF).reshape(size // 2, 2, long, width)
    at = pl.ds(4 * short + (j // 2) * long, long)
    put_rows(down, 1, tmp_ref, keep_ref, send_ref, core, pl.ds((j % 2) * (size // 2), size // 2), at, sems)

    @pl.when(j == pl.num_programs(0) - 1)
    def _():
        finish(0, False)
        finish(1, True)


def att_grads_kernel(core_ref, n_ref, dproj_ref, ctx_ref, db_ref, keep_ref, send_ref, tmp_ref, sems):
    core, j = core_ref[0], pl.program_id(0)
    width = n_ref.shape[1]
    size = keep_ref.shape[0]
    short = width // (2 * size)
    slot = lax.rem(j, 2)
    tmp = tmp_ref.at[slot].reshape(size, 2, short, width)

    def finish(at):
        for i, ref in enumerate((keep_ref, send_ref)):
            to = ref.at[:, pl.ds(0, short)]
            pltpu.make_async_copy(to, to, sems.at[at, i]).wait()

    @pl.when(j > 1)
    def _():
        finish(slot)

    @pl.when(j < 3)
    def _():
        tmp[...] = dot_tn(n_ref[...], dproj_ref[...]).astype(BF).reshape(tmp.shape)

    @pl.when(j == 3)
    def _():
        tmp[...] = dot_tn(ctx_ref[...], db_ref[...]).astype(BF).reshape(tmp.shape)

    at = pl.ds(j * short, short)
    pltpu.make_async_copy(tmp.at[:, core], keep_ref.at[:, at], sems.at[slot, 0]).start()
    pltpu.make_async_copy(tmp.at[:, 1 - core], send_ref.at[:, at], sems.at[slot, 1]).start()

    @pl.when(j == 3)
    def _():
        finish(0)
        finish(1)


def plain_grads(att, core, shape, a, b, c, d):
    size, _, width = shape
    cut = lambda grad: [grad[:, j * width : (j + 1) * width].reshape(size, 2, -1, width) for j in range(grad.shape[1] // width)]
    parts = cut(dot_tn(a, b).astype(BF))
    if att:
        parts += cut(dot_tn(c, d).astype(BF))
    else:
        parts += [half.reshape(size, 2, -1, width) for half in jnp.split(dot_tn(c, d).astype(BF), 2, axis=0)]
    both = jnp.concatenate(parts, axis=2)
    at = lambda i: lax.dynamic_index_in_dim(both, i, 1, keepdims=False)
    return at(core), at(1 - core)


def weight_grads(kernel, core, size, us, a, b, c, d):
    rows, width = a.shape
    att = kernel is att_grads_kernel
    shape = (size, (2 * width if att else 4 * width) // size, width)
    if width // (2 * size) % 16:
        return plain_grads(att, core, shape, a, b, c, d)
    col = pl.BlockSpec((rows, width), lambda j: (0, jnp.minimum(j, 2 if att else 3)))
    return pl.pallas_call(
        kernel,
        grid=(4,),
        in_specs=[SMEM, whole(a.shape), col, whole(c.shape) if att else col, whole(d.shape)],
        out_specs=[ANY] * 2,
        out_shape=[jax.ShapeDtypeStruct(shape, BF)] * 2,
        scratch_shapes=[pltpu.VMEM((2, width, width), BF), pltpu.SemaphoreType.DMA((2, 2))],
        compiler_params=params_for(48),
        cost_estimate=cost(us),
        name=kernel.__name__[:-7],
    )(core.astype(jnp.int32).reshape(1), a, b, c, d)


def send(value, pairs):
    return lax.ppermute(value, "pipe", pairs)


def swap(value, bit):
    return send(value, [(i, i ^ bit) for i in range(lax.axis_size("pipe"))])


def to_target(value, target, bit):
    return send(value, [(target ^ bit, target)])


def pick(core, mine_first, mine_second):
    return jnp.where(core == 0, mine_first, mine_second)


ORDERS = (("x", "y", "z2", "z4"), ("y", "z2", "x", "z4"), ("z2", "x", "y", "z4"))
AT = {"x": ("dp", 1), "z2": ("dp", 2), "z4": ("dp", 4), "y": ("pipe", 2)}


def cube_start(parts):
    size, rows, width = parts.shape
    if size != 8:
        return parts
    parts = parts.reshape(2, 2, 2, 2, rows // 2, width)
    share = width // len(ORDERS)
    return [(parts[..., i * share : (i + 1) * share], None, ["z4", "z2", "x", "y"]) for i in range(len(ORDERS))]


def settled(part, got):
    return part if got is None else part + got


def halve(part, names, axis):
    name, bit = AT[axis]
    i = names.index(axis)
    me = (lax.axis_index(name) // bit) % 2
    at = lambda j: lax.dynamic_index_in_dim(part, j, i, keepdims=False)
    give = at(1 - me)
    got = lax.ppermute(give, name, [(k, k ^ bit) for k in range(lax.axis_size(name))])
    return at(me), got, [n for n in names if n != axis], give


def cube_step(state, step):
    if not isinstance(state, list):
        return state, state
    done = [halve(settled(part, got), names, order[step]) for (part, got, names), order in zip(state, ORDERS)]
    gots = together([d[1] for d in done])
    return [(d[0], got, d[2]) for d, got in zip(done, gots)], [d[3] for d in done]


def cube_end(state):
    if not isinstance(state, list):
        plane = lax.axis_index("pipe") // 2
        parts = state.reshape(state.shape[0], 2, -1, state.shape[2])
        at = lambda i: lax.dynamic_index_in_dim(parts, i, 1, keepdims=False)
        return (lax.psum_scatter(at(plane) + swap(at(1 - plane), 2), "dp", scatter_dimension=0), None), state
    whole_part = jnp.concatenate([settled(part, got) for part, got, _ in state], axis=-1)
    mine, got, _, give = halve(whole_part, ["z4"], "z4")
    return (mine, got), give


def line_start(parts):
    return lax.psum_scatter(parts, "dp", scatter_dimension=0)


def line_end(mine):
    plane = lax.axis_index("pipe") // 2
    mine = mine.reshape(2, -1, mine.shape[1])
    at = lambda i: lax.dynamic_index_in_dim(mine, i, 0, keepdims=False)
    return at(plane) + swap(at(1 - plane), 2)


def from_pipe(value, target, sources):
    return [value if i == target else send(value, [(i, target)]) for i in sources]


def att_result(piece, s):
    rows = piece.shape[0] // 2
    got = together(from_pipe(piece, s, range(4)))
    cols = []
    for j in range(4):
        cols.append(jnp.concatenate([got[(j // 2) * 2 + c][(j % 2) * rows : (j % 2 + 1) * rows] for c in range(2)], axis=0))
    return jnp.concatenate(cols, axis=1)


def mlp_result(piece, s):
    rows = piece.shape[0] // 4
    up, low, high = together((from_pipe(piece, s, (0, 1)), from_pipe(piece[: 2 * rows], s - 1, (2, 3)), from_pipe(piece[2 * rows :], s, (2, 3))))
    first = jnp.concatenate(
        [jnp.concatenate([up[c][j * rows : (j + 1) * rows] for c in range(2)], axis=0) for j in range(4)], axis=1
    )
    low, high = jnp.concatenate(low, axis=0), jnp.concatenate(high, axis=0)
    return first, low, high


def choose(place, options):
    result = options[-1]
    for s in range(len(options) - 2, -1, -1):
        result = jnp.where(place == s, options[s], result)
    return result


def small_sum(value, step):
    if lax.axis_size("dp") != 8:
        return lax.psum(value, ("dp", "pipe")) if step == 0 else value
    if step < 2:
        return value + swap(value, step + 1)
    return value + dp_swap(value, 1 << (step - 2))


def local(
    inputs, out_grad, page_side, norm_gain, norm_shift, layer_scale, w_first, w_half, rel_table
):
    place = lax.axis_index("pipe")
    sections = lax.axis_size("pipe")
    dp_size, dp_place = lax.axis_size("dp"), lax.axis_index("dp")
    micro_count, slot_rows, width = inputs.shape
    halves = sections // micro_count
    assert halves == 2 and sections == 4
    rows = slot_rows // halves
    plane, core = place // 2, place % 2
    layers, heads = rel_table.shape[:2]

    own_params = jnp.stack([norm_gain[0], norm_shift[0], layer_scale[0]])
    seen = [own_params] + [swap(own_params, bit) for bit in (1, 2, 3)]
    params = [choose(place, [seen[s ^ p] for p in range(sections)]) for s in range(sections)]

    own_first, own_half = w_first[0], w_half[0]
    count = own_first.shape[0] // 2
    quarter = count // 4
    q = dp_place % 4
    share = [lax.dynamic_slice_in_dim(own_first, c * count + q * quarter, quarter, 0) for c in range(2)]
    mine_att = pick(core, send(share[0], [(0, 2), (2, 0)]), send(share[1], [(0, 3), (2, 1)]))
    some_att = quad_start(mine_att)
    share, own_half_y = tie((share, own_half), mine_att, seen)
    mine_up = pick(core, send(share[0], [(1, 2), (3, 0)]), send(share[1], [(1, 3), (3, 1)]))
    near_first = swap(tie(own_first, mine_att, seen), 1)
    all_att = quad_end(*tie(some_att, mine_up))
    some_up = quad_start(tie(mine_up, some_att))
    cut_half = own_half.shape[0] // 3
    own_half_y = tie(own_half_y, mine_up)
    far_half = [swap(own_half_y[i * cut_half : (i + 1) * cut_half], 2) for i in range(3)]
    far_att = quad_place(*tie(all_att, some_up, far_half[0]))
    far_att_other = swap(far_att, 1)
    near_half = swap(tie(own_half, far_att), 1)
    att_refs = (own_first, near_first, far_att, far_att_other)
    infos = [jnp.stack([(plane == layer).astype(jnp.int32), core.astype(jnp.int32)]) for layer in range(layers)]

    micro, half = plane, core
    side = lax.dynamic_index_in_dim(page_side, micro, 0, keepdims=False)[0]
    own_rows = lambda x: lax.dynamic_slice(x, (micro, half * rows, 0), (1, rows, width))[0]
    key_ids = (jnp.arange(slot_rows, dtype=jnp.int32) + half * rows) % slot_rows
    layout = geometry(side, key_ids, slot_rows)
    own_layout = [c[:rows] for c in layout]
    hot, hot_back = row_features(*own_layout, True), row_features(*own_layout, False)
    keys = key_features(*layout)
    maps = table_rows(rel_table)

    def shared(even, odd, layer):
        mine, other = pick(core, even, odd), pick(core, odd, even)
        inside = [(2 * layer, 2 * layer + 1), (2 * layer + 1, 2 * layer)]
        straight = [(p ^ 2, p) for p in (2 * layer, 2 * layer + 1)]
        across = [(p ^ 3, p) for p in (2 * layer, 2 * layer + 1)]
        return [mine, send(other, inside), send(mine, straight), send(other, across)]

    def to_one(value, s):
        return [value] + [to_target(value, s, bit) for bit in (1, 2, 3)]

    def collected(parts):
        return choose(place, [jnp.stack([parts[s][i ^ s] for i in range(sections)]) for s in range(sections)])

    current = own_rows(inputs)
    kept, outs = [], {}
    for layer in range(layers):
        p0, p1, info = params[2 * layer], params[2 * layer + 1], infos[layer]
        normed, proj = project(info, current, p0, att_refs)
        if layer == 0:
            normed, proj = tie((normed, proj), far_half[1])
        partner = swap(proj[:, width:], 1)
        if layer == 0:
            far_up = quad_place(*quad_end(*tie(some_up, normed)))
            partner = tie(partner, far_up)
        context, rest, inv, queries = attn_forward(hot, maps[layer], proj, partner, keys)
        if layer == 0:
            far_up_other = swap(far_up, 1)
            far_half_other = [swap(part, 1) for part in far_half[:2]]
            context, last_half = tie((context, far_half[2]), far_up_other, near_half, far_half_other)
            up_refs = (own_first, near_first, far_up, far_up_other)
            down_refs = (own_half, near_half, far_half[0], far_half[1], last_half, *far_half_other, swap(last_half, 1))
        else:
            context, rest, inv, queries = tie((context, rest, inv, queries), outs[0][2])
        b0, x1, n1, slope, hidden, b1, x2 = block_out(info, current, context, p0, p1, att_refs, up_refs, down_refs)
        if layer == 1:
            b0, x1, n1, slope, hidden, b1, x2 = tie((b0, x1, n1, slope, hidden, b1, x2), outs[0])
        kept.append((current, normed, proj, partner, (context, rest, inv), queries, b0, x1, n1, slope, hidden, b1))
        outs[2 * layer] = outs[2 * layer + 1] = shared(x1, x2, layer)
        current = x2

    cut = heads // 4
    tables, vecs, grads = {}, {}, {}
    core_id = core.astype(jnp.int32)

    x, normed, proj, partner, outcome, queries, b0, x1, n1, slope, hidden, b1 = kept[1]
    p0, p1, info = params[2], params[3], infos[1]
    grad = tie(own_rows(out_grad), current)
    db1, d_pre, gx1, db0, d_context, vec1 = block_back(info, grad, x1, slope, b1, b0, p0, p1, att_refs, up_refs, down_refs)
    db1, d_pre, gx1, db0, d_context, vec1 = tie((db1, d_pre, gx1, db0, d_context, vec1), outs[2][2])
    keep, other = weight_grads(mlp_grads_kernel, core, dp_size, 15, n1, d_pre, hidden, db1)
    keep, other = tie((keep, other), outs[2])
    got = swap(other, 1)
    back = lambda d_ctx, i: attn_backward(hot_back, queries, proj, partner, keys, d_ctx, outcome, i * cut, cut)
    dqa, mya, oa, ta = back(tie(d_context, keep), 0)
    dqa, mya, oa, ta, got = together((dqa, mya, oa, ta, got))
    mlp_b = keep + got
    gota = swap(oa, 1)
    dqb, myb, ob, tb = back(tie(d_context, mlp_b, oa), 1)
    dqb, myb, ob, tb, gota = together((dqb, myb, ob, tb, gota))
    gotb = swap(ob, 1)
    mlp_b = line_start(mlp_b)
    d_proj, gx0, vec0 = project_back(info, gx1, x, p0, (dqa, dqb, mya, myb, gota, gotb), att_refs)
    keep, other = weight_grads(att_grads_kernel, core, dp_size, 9, normed, d_proj, outcome[0], db0)
    got = swap(other, 1)
    grads[2] = grads[3] = shared(gx0, gx1, 1)
    tables[1] = (ta, tb)
    vecs[3], vecs[2] = vec1[:3], jnp.concatenate([vec0[:2], vec1[3:4]])

    x, normed, proj, partner, outcome, queries, b0, x1, n1, slope, hidden, b1 = kept[0]
    p0, p1, info = params[0], params[1], infos[0]
    db1, d_pre, gx1, db0, d_context, vec1 = block_back(info, tie(gx0, keep), x1, slope, b1, b0, p0, p1, att_refs, up_refs, down_refs)
    db1, d_pre, gx1, db0, d_context, vec1, got = tie((db1, d_pre, gx1, db0, d_context, vec1, got), grads[2][2])
    att_b = keep + got
    d_pre = tie(d_pre, att_b)
    att_b = line_start(att_b)
    keep, other = weight_grads(mlp_grads_kernel, core, dp_size, 15, n1, d_pre, hidden, db1)
    keep, other = tie((keep, other), grads[2])
    got = swap(other, 1)
    grads[1] = to_one(gx1, 1)
    dqa, mya, oa, ta = back(tie(d_context, keep), 0)
    dqa, mya, oa, ta, got, mlp_b = tie((dqa, mya, oa, ta, got, mlp_b), grads[1])
    mlp_a = cube_start(keep + got)
    gota = swap(oa, 1)
    mlp_a, given = cube_step(mlp_a, 0)
    dqb, myb, ob, tb = back(tie(d_context, given, oa), 1)
    dqb, myb, ob, tb, gota, mlp_a = hold((dqb, myb, ob, tb, gota, mlp_a), 5)
    gotb = swap(ob, 1)
    mlp_a, given = cube_step(mlp_a, 1)
    gotb = tie(gotb, given)
    d_proj, gx0, vec0 = project_back(info, gx1, x, p0, (dqa, dqb, mya, myb, gota, gotb), att_refs)
    d_proj, gx0, vec0, mlp_a = hold((d_proj, gx0, vec0, mlp_a), 3)
    mlp_a, given = cube_step(mlp_a, 2)
    keep, other = weight_grads(att_grads_kernel, core, dp_size, 9, tie(normed, given), d_proj, outcome[0], db0)
    keep, other, att_b, mlp_a = hold((keep, other, att_b, mlp_a), 3)
    got = swap(other, 1)
    tables = [(ta, tb), tables[1]]
    vecs[1], vecs[0] = vec1[:3], jnp.concatenate([vec0[:2], vec1[3:4]])
    stack = lambda parts: jnp.stack([parts[s] for s in range(sections)])
    table_all = [jnp.concatenate(tables[layer])[:, :4].reshape(heads, 2, 128)[..., : 2 * SIDE_L + 1] for layer in range(layers)]
    small = jnp.concatenate([stack(vecs).reshape(-1), jnp.stack(table_all).reshape(-1)])
    small = small_sum(small, 0)
    mlp_a, _ = cube_end(mlp_a)
    got, keep, small = together((got, keep, small))
    att_a = cube_start(keep + got)
    att_a, given = cube_step(att_a, 0)
    small = small_sum(small, 1)
    section_out = collected(tie(outs, given)).reshape(1, micro_count, slot_rows, width)
    small, section_out, mlp_a, att_a = hold((small, section_out, mlp_a, att_a), 3)
    att_a, given = cube_step(att_a, 1)
    small = small_sum(small, 2)
    mlp_a, gx0 = tie((settled(*mlp_a), gx0), given)
    grads[0] = to_one(gx0, 0)
    mlp_result_a = mlp_result(mlp_a, 1)
    small, att_a = hold((small, att_a), 1)
    att_a, given = cube_step(att_a, 2)
    small = small_sum(small, 3)
    mlp_b, att_b = tie((mlp_b, att_b), given)
    mlp_b, att_b = line_end(mlp_b), line_end(att_b)
    small, mlp_b, att_b, grads[0], mlp_result_a, att_a = hold((small, mlp_b, att_b, grads[0], mlp_result_a, att_a), 5)
    att_a, given = cube_end(att_a)
    small = small_sum(small, 4)
    mlp_b, att_b, grads = tie((mlp_b, att_b, grads), given)
    mlp_result_b, att_b = mlp_result(mlp_b, 3), att_result(att_b, 2)
    in_grads = collected({s: [part.astype(F32) for part in grads[s]] for s in range(sections)}).reshape(1, micro_count, slot_rows, width)
    small, mlp_result_b, att_b, in_grads, att_a = together((small, mlp_result_b, att_b, in_grads, att_a))
    att_a = settled(*att_a)

    first_grads, half_grads = {}, {}
    first_grads[3], half_grads[2], half_grads[3] = mlp_result_b
    first_grads[2] = att_b
    first_grads[1], half_grads[0], half_grads[1] = mlp_result_a
    first_grads[0] = att_result(att_a, 0)

    g_first = choose(place, [first_grads[s].astype(F32) for s in range(sections)])[None]
    g_half = choose(place, [half_grads[s].astype(F32) for s in range(sections)])[None]
    vec_size = sections * 3 * width
    vec_all = small[:vec_size].reshape(sections, 3, width)
    g_table = small[vec_size:].reshape(rel_table.shape)
    cols = width // dp_size
    mine = lax.dynamic_slice(vec_all, (place, 0, dp_place * cols), (1, 3, cols))
    return (section_out, in_grads, g_first, g_half, mine[:, 0], mine[:, 1], mine[:, 2], g_table)


def solution(mesh):
    in_specs = (
        P(None, "dp", None),
        P(None, "dp", None),
        P(None, "dp"),
        P("pipe", None),
        P("pipe", None),
        P("pipe", None),
        P("pipe", None, None),
        P("pipe", None, None),
        P(),
    )
    out_specs = (
        P("pipe", None, "dp", None),
        P("pipe", None, "dp", None),
        P("pipe", "dp", None),
        P("pipe", "dp", None),
        P("pipe", "dp"),
        P("pipe", "dp"),
        P("pipe", "dp"),
        P(),
    )
    return jax.shard_map(local, mesh=mesh, in_specs=in_specs, out_specs=out_specs, check_vma=False)
```

```python
from functools import partial

import jax
import jax.numpy as jnp
import numpy as np
from jax import lax
from jax.experimental import pallas as pl
from jax.experimental.pallas import tpu as pltpu
from jax.sharding import PartitionSpec as P

SIDE_L = 32
CELLS = SIDE_L + 1
HEAD = 64
PAIR = 2 * HEAD
PAGES = 8
BLOCK = 40
PAGE_AT = 3 * CELLS
MASKED = 1e30
EPSILON = 1e-06
LOG2E = 1.4426950408889634
LN2 = 0.6931471805599453
BF = jnp.bfloat16
F32 = jnp.float32
NT = (((1,), (1,)), ((), ()))
TN = (((0,), (0,)), ((), ()))


def dot(a, b):
    return jnp.dot(a, b, preferred_element_type=F32)


def dot_nt(a, b):
    return lax.dot_general(a, b, NT, preferred_element_type=F32)


def dot_tn(a, b):
    return lax.dot_general(a, b, TN, preferred_element_type=F32)


def geometry(grid_side, row_ids, slot_rows):
    page_len = grid_side * grid_side + 1
    page_count = slot_rows // page_len
    page_of = jnp.minimum(row_ids // page_len, page_count)
    offset = row_ids - page_of * page_len
    patch_id = jnp.maximum(offset - 1, 0)
    inside = page_of < page_count
    class_row = offset == 0
    coord_y = jnp.where(inside, jnp.where(class_row, SIDE_L, patch_id // grid_side), 0)
    coord_x = jnp.where(inside, jnp.where(class_row, SIDE_L, patch_id % grid_side), 0)
    return page_of, coord_y, coord_x


def row_features(page_of, coord_y, coord_x, flip):
    lane = jnp.arange(128, dtype=jnp.int32)[None, :]
    at = (lambda c: SIDE_L - c) if flip else (lambda c: c)
    hot = (lane == at(coord_y)[:, None]) | (lane == BLOCK + at(coord_x)[:, None])
    hot = hot | (lane == 2 * BLOCK + page_of[:, None])
    return hot.astype(BF)


def key_features(page_of, coord_y, coord_x):
    lane = jnp.arange(256, dtype=jnp.int32)[None, :]
    at_y = SIDE_L - coord_y[:, None]
    at_x = SIDE_L - coord_x[:, None]
    hot = (lane == at_y) | (lane == HEAD + at_y) | (lane == 128 + at_x)
    hot = hot | (lane == 128 + CELLS + at_y) | (lane == 128 + 2 * CELLS + at_x)
    hot = hot | (lane == 128 + PAGE_AT + page_of[:, None])
    return hot.astype(BF)


def table_rows(rel_table):
    layers, heads = rel_table.shape[:2]
    scaled = rel_table * LOG2E
    gap = jnp.zeros((*scaled.shape[:3], 128 - 2 * SIDE_L - 1), F32)
    scaled = jnp.concatenate([scaled[..., SIDE_L:], gap, scaled[..., :SIDE_L]], axis=-1)
    high = scaled.astype(BF).astype(F32)
    return jnp.concatenate([high, scaled - high], axis=2).reshape(layers, heads // 2, 8, 128)


def table_map(table_ref, head):
    row = lax.broadcasted_iota(jnp.int32, (BLOCK, 128), 0)
    lane = lax.broadcasted_iota(jnp.int32, (BLOCK, 128), 1)

    def grid(i, to):
        values = jnp.broadcast_to(table_ref[0, 4 * head + i : 4 * head + i + 1, :], (BLOCK, 128))
        values = pltpu.roll(values, 0, 1, stride=1, stride_axis=0)
        values = jnp.where((row < CELLS) & (lane < CELLS), values, 0.0)
        return pltpu.roll(values, to, 1) if to else values

    none = jnp.zeros((BLOCK, 128), F32)
    far = jnp.where((lane >= PAGE_AT) & (lane < PAGE_AT + PAGES) & (lane - PAGE_AT != row) & (row < PAGES), -MASKED, 0.0)
    left = [grid(0, HEAD if head == 0 else 0), none, none, none[:8]]
    right = [grid(2, CELLS), grid(1, 0) + grid(3, 2 * CELLS), far, none[:8]]
    return jnp.concatenate([jnp.concatenate(left, axis=0), jnp.concatenate(right, axis=0)], axis=1).astype(BF)


def split3(value):
    high = value.astype(BF).astype(F32)
    middle = (value - high).astype(BF).astype(F32)
    return high, middle, value - high - middle


def lanes_of(rows):
    return lax.broadcasted_iota(jnp.int32, (rows, PAIR), 1)


def attn_fwd_kernel(hot_ref, map_ref, q_ref, ko_ref, kp_ref, vo_ref, vp_ref, key_ref,
                    o_ref, rest_ref, inv_ref, w_ref, kx_ref, vx_ref):
    rows = q_ref.shape[0]
    lane = lanes_of(rows)
    for head in range(2):
        mine = (lane < HEAD) if head == 0 else (lane >= HEAD)
        one_at = HEAD if head == 0 else 0
        table = table_map(map_ref, head)
        kx, vx = kx_ref.at[head], vx_ref.at[head]
        kx[:, PAIR:] = key_ref[:, PAIR:]
        for part, (k_ref, v_ref) in enumerate(((ko_ref, vo_ref), (kp_ref, vp_ref))):
            at = pl.ds(part * rows, rows)
            kx[at, :PAIR] = jnp.where(mine, k_ref[...], key_ref[at, :PAIR])
            vx[at, :] = jnp.where(mine, v_ref[...], jnp.where(lane == one_at, 1.0, 0.0).astype(BF))
        feats = dot(hot_ref[...], table).astype(BF)
        query = jnp.concatenate([jnp.where(mine, q_ref[...], feats[:, :PAIR]), feats[:, PAIR:]], axis=1)
        scores = dot_nt(kx[...], query)
        weights = jnp.exp2(scores - jnp.max(scores, axis=0, keepdims=True)).astype(BF)
        w_ref[head] = weights
        mixed = dot_tn(vx[...], weights).T
        inv = 1.0 / mixed[:, one_at : one_at + 1]
        out = mixed * inv
        high = out.astype(BF)
        rest = (out - high.astype(F32)).astype(BF)
        inv = jnp.broadcast_to(inv, out.shape)
        if head == 0:
            o_ref[...], rest_ref[...], inv_ref[...] = high, rest, inv
        else:
            o_ref[...] = jnp.where(mine, high, o_ref[...])
            rest_ref[...] = jnp.where(mine, rest, rest_ref[...])
            inv_ref[...] = jnp.where(mine, inv, inv_ref[...])


def attn_forward(hot, maps, project, partner, keys, first, count):
    rows, width = project.shape[0], project.shape[1] // 3
    pairs = width // PAIR
    col = lambda off: pl.BlockSpec((rows, PAIR), lambda g: (0, off + first + g))
    out = pl.BlockSpec((rows, PAIR), lambda g: (0, g))
    return pl.pallas_call(
        attn_fwd_kernel,
        grid=(count,),
        in_specs=[
            whole((rows, 128)),
            pl.BlockSpec((1, 8, 128), lambda g: (first + g, 0, 0)),
            col(0),
            col(pairs),
            col(0),
            col(2 * pairs),
            col(pairs),
            whole((2 * rows, 256)),
        ],
        out_specs=[out, out, out, pl.BlockSpec((2, 2 * rows, rows), lambda g: (g, 0, 0))],
        out_shape=[
            jax.ShapeDtypeStruct((rows, count * PAIR), BF),
            jax.ShapeDtypeStruct((rows, count * PAIR), BF),
            jax.ShapeDtypeStruct((rows, count * PAIR), F32),
            jax.ShapeDtypeStruct((2 * count, 2 * rows, rows), BF),
        ],
        scratch_shapes=[pltpu.VMEM((2, 2 * rows, 256), BF), pltpu.VMEM((2, 2 * rows, PAIR), BF)],
        compiler_params=params_for(56),
        cost_estimate=cost(26),
        name="attn_fwd",
    )(hot, maps, project, project, partner, project, partner, keys)


def attn_bwd_kernel(hot_ref, w_ref, q_ref, ko_ref, kp_ref, vo_ref, vp_ref, key_ref, do_ref, o_ref, rest_ref, inv_ref,
                    dq_ref, mine_ref, other_ref, gt_ref, kx_ref, vx_ref, ds_ref):
    rows = q_ref.shape[0]
    lane = lanes_of(rows)
    scaled = (do_ref[...].astype(F32) * inv_ref[...]).astype(BF)
    product = scaled.astype(F32) * (o_ref[...].astype(F32) + rest_ref[...].astype(F32))
    for head in range(2):
        mine = (lane < HEAD) if head == 0 else (lane >= HEAD)
        spot = lane - (HEAD if head == 0 else 0)
        kx, vx, ds = kx_ref.at[head], vx_ref.at[head], ds_ref.at[head]
        kx[:, PAIR:] = key_ref[:, PAIR:]
        ones = jnp.where((spot >= 0) & (spot < 3), 1.0, 0.0).astype(BF)
        for part, (k_ref, v_ref) in enumerate(((ko_ref, vo_ref), (kp_ref, vp_ref))):
            at = pl.ds(part * rows, rows)
            kx[at, :PAIR] = jnp.where(mine, k_ref[...], key_ref[at, :PAIR])
            vx[at, :] = jnp.where(mine, v_ref[...], ones)
        delta = jnp.sum(jnp.where(mine, product, 0.0), axis=1, keepdims=True)
        high, middle, low = split3(delta)
        spread = jnp.where(spot == 0, -high, jnp.where(spot == 1, -middle, jnp.where(spot == 2, -low, 0.0)))
        d_out = jnp.where(mine, scaled, spread.astype(BF))
        for part, out_ref in enumerate((mine_ref, other_ref)):
            at = pl.ds(part * rows, rows)
            weights = w_ref[head, at, :]
            d_scores = (weights.astype(F32) * dot_nt(vx[at, :], d_out)).astype(BF)
            ds[at, :] = d_scores
            d_value = dot(weights, scaled).astype(BF)
            d_key = (dot(d_scores, q_ref[...]) * LN2).astype(BF)
            if head == 0:
                out_ref[1], out_ref[0] = d_value, d_key
            else:
                out_ref[1] = jnp.where(mine, d_value, out_ref[1])
                out_ref[0] = jnp.where(mine, d_key, out_ref[0])
        d_query = dot_tn(ds[...], kx[...])
        high_q = d_query.astype(BF)
        low_q = (d_query - high_q.astype(F32)).astype(BF)
        grid = dot_tn(hot_ref[...], high_q) + dot_tn(hot_ref[...], low_q)
        row = lax.broadcasted_iota(jnp.int32, (BLOCK, 128), 0)
        column = lax.broadcasted_iota(jnp.int32, (BLOCK, 128), 1)
        for axis in range(2):
            part = grid[axis * BLOCK : (axis + 1) * BLOCK, axis * 128 : (axis + 1) * 128]
            part = pltpu.roll(part, HEAD, 1) if axis == 0 and head == 0 else part
            part = jnp.where((row < CELLS) & (column < CELLS), part, 0.0)
            along = pltpu.roll(part, 0, 1, stride=1, stride_axis=0)
            gt_ref[0, 2 * head + axis : 2 * head + axis + 1, :] = jnp.sum(along, axis=0, keepdims=True)
        d_query = (d_query[:, :PAIR] * HEAD**-0.5).astype(BF)
        dq_ref[...] = d_query if head == 0 else jnp.where(mine, d_query, dq_ref[...])
    gt_ref[0, 4:8, :] = jnp.zeros((4, 128), F32)


def attn_backward(hot, weights, project, partner, keys, d_context, outcome, first, count):
    rows, width = project.shape[0], project.shape[1] // 3
    pairs = width // PAIR
    col = lambda off: pl.BlockSpec((rows, PAIR), lambda g: (0, off + first + g))
    out = pl.BlockSpec((rows, PAIR), lambda g: (0, g))
    both = pl.BlockSpec((2, rows, PAIR), lambda g: (0, 0, g))
    return pl.pallas_call(
        attn_bwd_kernel,
        grid=(count,),
        in_specs=[
            whole((rows, 128)),
            pl.BlockSpec((2, 2 * rows, rows), lambda g: (g, 0, 0)),
            col(0),
            col(pairs),
            col(0),
            col(2 * pairs),
            col(pairs),
            whole((2 * rows, 256)),
            col(0),
            out,
            out,
            out,
        ],
        out_specs=[out, both, both, pl.BlockSpec((1, 8, 128), lambda g: (g, 0, 0))],
        out_shape=[
            jax.ShapeDtypeStruct((rows, count * PAIR), BF),
            jax.ShapeDtypeStruct((2, rows, count * PAIR), BF),
            jax.ShapeDtypeStruct((2, rows, count * PAIR), BF),
            jax.ShapeDtypeStruct((count, 8, 128), F32),
        ],
        scratch_shapes=[
            pltpu.VMEM((2, 2 * rows, 256), BF),
            pltpu.VMEM((2, 2 * rows, PAIR), BF),
            pltpu.VMEM((2, 2 * rows, rows), BF),
        ],
        compiler_params=params_for(56),
        cost_estimate=cost(6 * count),
        name="attn_bwd",
    )(hot, weights, project, project, partner, project, partner, keys, d_context, *outcome)


def centred(values):
    values = values - jnp.mean(values, axis=-1, keepdims=True)
    inv = lax.rsqrt(jnp.mean(values * values, axis=-1, keepdims=True) + EPSILON)
    return values * inv, inv


def start_first(info_ref, kind, cols, far_cols, refs, dst, sem):
    own, near, far_own, far_other = refs
    local, core = info_ref[0] == 1, info_ref[1]
    part = far_own.shape[0]

    @pl.when(local & (core == kind))
    def _():
        pltpu.make_async_copy(own.at[:, cols], dst, sem).start()

    @pl.when(local & (core != kind))
    def _():
        pltpu.make_async_copy(near.at[:, cols], dst, sem).start()

    @pl.when(jnp.logical_not(local))
    def _():
        if part == dst.shape[0]:
            pltpu.make_async_copy(far_own, dst, sem).start()
            return
        pltpu.make_async_copy(far_own.at[:, far_cols], dst.at[pl.ds(core * part, part)], sem).start()
        pltpu.make_async_copy(far_other.at[:, far_cols], dst.at[pl.ds((1 - core) * part, part)], sem).start()


def start_down(info_ref, refs, dst, sem):
    own, near, far_own, far_other = refs
    local, core = info_ref[0] == 1, info_ref[1]
    part = own.shape[0]
    for here, mine, other in ((local, own, near), (jnp.logical_not(local), far_own, far_other)):

        @pl.when(here)
        def _(mine=mine, other=other):
            pltpu.make_async_copy(mine, dst.at[pl.ds(core * part, part)], sem).start()
            pltpu.make_async_copy(other, dst.at[pl.ds((1 - core) * part, part)], sem).start()


def wait_for(dst, sem):
    pltpu.make_async_copy(dst, dst, sem).wait()


EARLY = True
SMEM = pl.BlockSpec(memory_space=pltpu.SMEM)
ANY = pl.BlockSpec(memory_space=pl.ANY)


def whole(shape):
    return pl.BlockSpec(shape, lambda *g: (0,) * len(shape))


def params_for(mib):
    return pltpu.CompilerParams(vmem_limit_bytes=mib * 2**20)


def cost(us):
    return pl.CostEstimate(flops=int(us * 2e7), bytes_accessed=1000, transcendentals=0)


def project_kernel(info_ref, x_ref, p_ref, own, near, far_own, far_other, normed_ref, out_ref, w_ref, sem):
    width = x_ref.shape[1]
    start_first(info_ref, 0, pl.ds(0, 3 * width), pl.ds(0, 3 * width), (own, near, far_own, far_other), w_ref, sem)
    nhat, _ = centred(x_ref[...].astype(F32))
    normed = (nhat * p_ref[0:1, :] + p_ref[1:2, :]).astype(BF)
    normed_ref[...] = normed
    wait_for(w_ref, sem)
    for j in range(3):
        at = pl.ds(j * width, width)
        value = dot(normed, w_ref[:, at])
        if j == 0:
            value = value * (HEAD**-0.5 * LOG2E)
        out_ref[:, at] = value.astype(BF)


def project(info, x, p, first_refs):
    rows, width = x.shape
    return pl.pallas_call(
        project_kernel,
        in_specs=[SMEM, whole(x.shape), whole(p.shape)] + [ANY] * 4,
        out_specs=[whole((rows, width)), whole((rows, 3 * width))],
        out_shape=[jax.ShapeDtypeStruct((rows, width), BF), jax.ShapeDtypeStruct((rows, 3 * width), BF)],
        scratch_shapes=[pltpu.VMEM((width, 3 * width), BF), pltpu.SemaphoreType.DMA],
        compiler_params=params_for(40),
        cost_estimate=cost(5),
        name="project",
    )(info, x, p, *first_refs)


def block_out_kernel(info_ref, x_ref, ctx_a, ctx_b, p0_ref, p1_ref, *refs):
    att, up, refs = refs[:4], refs[:2] + refs[4:6], refs[6:]
    down, refs = refs[:4], refs[4:]
    b0_ref, x1_ref, n1_ref, slope_ref, hid_ref, b1_ref, x2_ref, wo_ref, wu_ref, wd_ref, slopes, hiddens, sems, out_sems = refs
    width = x_ref.shape[1]
    start_first(info_ref, 0, pl.ds(3 * width, width), pl.ds(0, width), att, wo_ref, sems.at[0])
    for j in range(4):
        start_first(info_ref, 1, pl.ds(j * width, width), pl.ds(j * width, width), up, wu_ref.at[j], sems.at[1 + j])
    start_down(info_ref, down, wd_ref, sems.at[5])
    wait_for(wo_ref, sems.at[0])
    half = width // 2
    branch = dot(ctx_a[...], wo_ref[:half]) + dot(ctx_b[...], wo_ref[half:])
    b0_ref[...] = branch.astype(BF)
    x1 = (x_ref[...].astype(F32) + p0_ref[2:3, :] * branch).astype(BF)
    x1_ref[...] = x1
    x1 = x1.astype(F32)
    nhat, _ = centred(x1)
    normed = (nhat * p1_ref[0:1, :] + p1_ref[1:2, :]).astype(BF)
    n1_ref[...] = normed
    for j in range(4):
        wait_for(wu_ref.at[j], sems.at[1 + j])
    wait_for(wd_ref, sems.at[5])
    total = jnp.zeros(x1.shape, F32)
    for j in range(4):
        at = pl.ds(j * width, width)
        v = dot(normed, wu_ref[j])
        square = v * v
        bend = jnp.tanh(v * (0.7978845608028654 + (0.7978845608028654 * 0.044715) * square))
        up_half = 0.5 + 0.5 * bend
        along = v * (2 * 0.7978845608028654 + (6 * 0.7978845608028654 * 0.044715) * square)
        slopes[j] = (up_half + along * (up_half * (1.0 - up_half))).astype(BF)
        hiddens[j] = (v * up_half).astype(BF)
        if EARLY:
            pltpu.make_async_copy(slopes.at[j], slope_ref.at[:, at], out_sems.at[0, j]).start()
            pltpu.make_async_copy(hiddens.at[j], hid_ref.at[:, at], out_sems.at[1, j]).start()
        total = total + dot(hiddens[j], wd_ref[at, :])
    b1_ref[...] = total.astype(BF)
    x2_ref[...] = (x1 + p1_ref[2:3, :] * total).astype(BF)
    if not EARLY:
        for j in range(4):
            at = pl.ds(j * width, width)
            pltpu.make_async_copy(slopes.at[j], slope_ref.at[:, at], out_sems.at[0, j]).start()
            pltpu.make_async_copy(hiddens.at[j], hid_ref.at[:, at], out_sems.at[1, j]).start()
    for j in range(4):
        wait_for(slopes.at[j], out_sems.at[0, j])
        wait_for(hiddens.at[j], out_sems.at[1, j])


def block_out(info, x, context, p0, p1, more_refs, up_refs, down_refs):
    rows, width = x.shape
    one = whole((rows, width))
    shape = lambda n: jax.ShapeDtypeStruct((rows, n), BF)
    widths = [width, width, width, 4 * width, 4 * width, width, width]
    refs = (*more_refs, *up_refs[2:], *down_refs)
    return pl.pallas_call(
        block_out_kernel,
        grid=(1,),
        in_specs=[SMEM, one, *[whole(c.shape) for c in context], whole(p0.shape), whole(p1.shape)] + [ANY] * len(refs),
        out_specs=[one if n == width else ANY for n in widths],
        out_shape=[shape(n) for n in widths],
        scratch_shapes=[
            pltpu.VMEM((width, width), BF),
            pltpu.VMEM((4, width, width), BF),
            pltpu.VMEM((4 * width, width), BF),
            pltpu.VMEM((4, rows, width), BF),
            pltpu.VMEM((4, rows, width), BF),
            pltpu.SemaphoreType.DMA((6,)),
            pltpu.SemaphoreType.DMA((2, 4)),
        ],
        compiler_params=params_for(58),
        cost_estimate=cost(12),
        name="block_out",
    )(info, x, *context, p0, p1, *refs)


def norm_back(x, gain, d_normed, gy):
    nhat, inv = centred(x)
    inner = d_normed * gain
    shift = jnp.mean(inner, axis=-1, keepdims=True)
    along = jnp.mean(inner * nhat, axis=-1, keepdims=True)
    total = lambda v: jnp.sum(v, axis=0, keepdims=True)
    return gy + inv * (inner - shift - nhat * along), total(nhat * d_normed), total(d_normed)


def block_back_kernel(info_ref, gy_ref, x1_ref, slope_ref, b1_ref, b0_ref, p0_ref, p1_ref, *refs):
    att, up, refs = refs[:4], refs[:2] + refs[4:6], refs[6:]
    down, refs = refs[:4], refs[4:]
    db1_ref, dpre_ref, gx_ref, db0_ref, dctx_ref, vec_ref, wo_ref, wu_ref, wd_ref, slopes, given, sems, more_sems = refs
    width = gy_ref.shape[1]
    start_down(info_ref, down, wd_ref, sems.at[5])
    for j in range(4):
        at = pl.ds(j * width, width)
        start_first(info_ref, 1, at, at, up, wu_ref.at[j], sems.at[1 + j])
        pltpu.make_async_copy(slope_ref.at[:, at], slopes.at[j], more_sems.at[0, j]).start()
    start_first(info_ref, 0, pl.ds(3 * width, width), pl.ds(0, width), att, wo_ref, sems.at[0])
    total = lambda v: jnp.sum(v, axis=0, keepdims=True)
    gy = gy_ref[...].astype(F32)
    d_branch = (gy * p1_ref[2:3, :]).astype(BF)
    db1_ref[...] = d_branch
    vec_ref[2:3, :] = total(b1_ref[...].astype(F32) * gy)
    vec_ref[4:, :] = jnp.zeros((4, width), F32)
    d_normed = jnp.zeros(gy.shape, F32)
    wait_for(wd_ref, sems.at[5])
    for j in range(4):
        wait_for(slopes.at[j], more_sems.at[0, j])
        wait_for(wu_ref.at[j], sems.at[1 + j])
    for j in range(4):
        at = pl.ds(j * width, width)
        d_hidden = dot_nt(d_branch, wd_ref[at, :])
        given[j] = (d_hidden * slopes[j].astype(F32)).astype(BF)
        if EARLY:
            pltpu.make_async_copy(given.at[j], dpre_ref.at[:, at], more_sems.at[1, j]).start()
        d_normed = d_normed + dot_nt(given[j], wu_ref[j])
    if not EARLY:
        for j in range(4):
            pltpu.make_async_copy(given.at[j], dpre_ref.at[:, pl.ds(j * width, width)], more_sems.at[1, j]).start()
    gx, g_gain, g_shift = norm_back(x1_ref[...].astype(F32), p1_ref[0:1, :], d_normed, gy)
    vec_ref[0:1, :] = g_gain
    vec_ref[1:2, :] = g_shift
    gx = gx.astype(BF)
    gx_ref[...] = gx
    gx = gx.astype(F32)
    d_att = (gx * p0_ref[2:3, :]).astype(BF)
    db0_ref[...] = d_att
    vec_ref[3:4, :] = total(b0_ref[...].astype(F32) * gx)
    wait_for(wo_ref, sems.at[0])
    dctx_ref[...] = dot_nt(d_att, wo_ref[...]).astype(BF)
    for j in range(4):
        wait_for(given.at[j], more_sems.at[1, j])


def block_back(info, gy, x1, slope, b1, b0, p0, p1, more_refs, up_refs, down_refs):
    rows, width = gy.shape
    one = whole((rows, width))
    shape = lambda n: jax.ShapeDtypeStruct((rows, n), BF)
    widths = [width, 4 * width, width, width, width]
    refs = (*more_refs, *up_refs[2:], *down_refs)
    return pl.pallas_call(
        block_back_kernel,
        grid=(1,),
        in_specs=[SMEM, one, one, ANY, one, one, whole(p0.shape), whole(p1.shape)] + [ANY] * len(refs),
        out_specs=[one if n == width else ANY for n in widths] + [whole((8, width))],
        out_shape=[shape(n) for n in widths] + [jax.ShapeDtypeStruct((8, width), F32)],
        scratch_shapes=[
            pltpu.VMEM((width, width), BF),
            pltpu.VMEM((4, width, width), BF),
            pltpu.VMEM((4 * width, width), BF),
            pltpu.VMEM((4, rows, width), BF),
            pltpu.VMEM((4, rows, width), BF),
            pltpu.SemaphoreType.DMA((6,)),
            pltpu.SemaphoreType.DMA((2, 4)),
        ],
        compiler_params=params_for(58),
        cost_estimate=cost(14),
        name="block_back",
    )(info, gy, x1, slope, b1, b0, p0, p1, *refs)


def project_back_kernel(info_ref, gy_ref, x_ref, p_ref, dqa, dqb, mya, myb, gota, gotb, own, near, far_own, far_other,
                        dproj_ref, gx_ref, vec_ref, w_ref, sem):
    width = x_ref.shape[1]
    start_first(info_ref, 0, pl.ds(0, 3 * width), pl.ds(0, 3 * width), (own, near, far_own, far_other), w_ref, sem)
    half = width // 2
    for i, (dq, my, got) in enumerate(((dqa, mya, gota), (dqb, myb, gotb))):
        dproj_ref[:, i * half : (i + 1) * half] = dq[...]
        for j in range(2):
            at = pl.ds((1 + j) * width + i * half, half)
            dproj_ref[:, at] = (my[j].astype(F32) + got[j].astype(F32)).astype(BF)
    wait_for(w_ref, sem)
    d_normed = dot_nt(dproj_ref[:, :width], w_ref[:, :width])
    for j in (1, 2):
        at = pl.ds(j * width, width)
        d_normed = d_normed + dot_nt(dproj_ref[:, at], w_ref[:, at])
    gx, g_gain, g_shift = norm_back(x_ref[...].astype(F32), p_ref[0:1, :], d_normed, gy_ref[...].astype(F32))
    gx_ref[...] = gx.astype(BF)
    vec_ref[0:1, :] = g_gain
    vec_ref[1:2, :] = g_shift
    vec_ref[2:, :] = jnp.zeros((6, width), F32)


def project_back(info, gy, x, p, parts, first_refs):
    rows, width = x.shape
    one = whole((rows, width))
    return pl.pallas_call(
        project_back_kernel,
        in_specs=[SMEM, one, one, whole(p.shape)] + [whole(v.shape) for v in parts] + [ANY] * 4,
        out_specs=[whole((rows, 3 * width)), one, whole((8, width))],
        out_shape=[
            jax.ShapeDtypeStruct((rows, 3 * width), BF),
            jax.ShapeDtypeStruct((rows, width), BF),
            jax.ShapeDtypeStruct((8, width), F32),
        ],
        grid=(1,),
        scratch_shapes=[pltpu.VMEM((width, 3 * width), BF), pltpu.SemaphoreType.DMA],
        compiler_params=params_for(48),
        cost_estimate=cost(7),
        name="project_back",
    )(info, gy, x, p, *parts, *first_refs)


def gather_kernel(info_ref, mine, by_x, by_z, diag_x, diag_z, out_ref, sem):
    quarter = mine.shape[0]
    part = quarter // 2
    q = info_ref[0]
    at = lambda i: pl.multiple_of(i * quarter, part)
    pltpu.make_async_copy(mine, out_ref.at[pl.ds(at(q), quarter)], sem).start()
    pltpu.make_async_copy(by_x, out_ref.at[pl.ds(at(info_ref[1]), quarter)], sem).start()
    pltpu.make_async_copy(by_z, out_ref.at[pl.ds(at(info_ref[2]), quarter)], sem).start()
    pltpu.make_async_copy(diag_x, out_ref.at[pl.ds(at(info_ref[3]), part)], sem).start()
    pltpu.make_async_copy(diag_z, out_ref.at[pl.ds(at(info_ref[3]) + part, part)], sem).start()
    wait_for(out_ref, sem)


def dp_swap(value, bit):
    return lax.ppermute(value, "dp", [(i, i ^ bit) for i in range(lax.axis_size("dp"))])


def tie(value, *deps):
    return lax.optimization_barrier((value, deps))[0]


def hold(values, count):
    state = values[-1]
    if not isinstance(state, list):
        return lax.optimization_barrier(values)
    arrays = [part[:2] for part in state]
    *values, arrays = lax.optimization_barrier((*values[:count], arrays))
    return (*values, [(*part, names) for part, (_, _, names) in zip(arrays, state)])


def together(values):
    return lax.optimization_barrier(values)


def quad_start(mine):
    return mine, dp_swap(mine, 1), dp_swap(mine, 2)


def quad_end(mine, by_x, by_z):
    part = mine.shape[0] // 2
    return mine, by_x, by_z, dp_swap(by_z[:part], 1), dp_swap(by_x[part:], 2)


def quad_place(mine, *others):
    quarter = mine.shape[0]
    q = lax.axis_index("dp") % 4
    spots = jnp.stack([q, q ^ 1, q ^ 2, q ^ 3]).astype(jnp.int32)
    return pl.pallas_call(
        gather_kernel,
        in_specs=[SMEM] + [ANY] * 5,
        out_specs=whole((4 * quarter, *mine.shape[1:])),
        out_shape=jax.ShapeDtypeStruct((4 * quarter, *mine.shape[1:]), mine.dtype),
        scratch_shapes=[pltpu.SemaphoreType.DMA],
        compiler_params=params_for(16),
        cost_estimate=cost(3),
        name="assemble",
    )(spots, mine, *others)


def put_rows(values, slot, tmp_ref, keep_ref, send_ref, core, for_d, at, sems):
    tmp = tmp_ref.at[slot].reshape(values.shape)
    tmp[...] = values
    pltpu.make_async_copy(tmp.at[:, core], keep_ref.at[for_d, at], sems.at[slot, 0]).start()
    pltpu.make_async_copy(tmp.at[:, 1 - core], send_ref.at[for_d, at], sems.at[slot, 1]).start()


def mlp_grads_kernel(core_ref, n_ref, pre_ref, hid_ref, db_ref, keep_ref, send_ref, tmp_ref, sems):
    core, j = core_ref[0], pl.program_id(0)
    width = n_ref.shape[1]
    size = keep_ref.shape[0]
    short, long = width // (2 * size), 2 * width // (2 * size)

    def finish(slot, long_rows):
        for i, ref in enumerate((keep_ref, send_ref)):
            to = ref.at[pl.ds(0, size // 2), pl.ds(0, long)] if long_rows else ref.at[:, pl.ds(0, short)]
            pltpu.make_async_copy(to, to, sems.at[slot, i]).wait()

    @pl.when(j > 0)
    def _():
        finish(0, False)
    up = dot_tn(n_ref[...], pre_ref[...]).astype(BF).reshape(size, 2, short, width)
    put_rows(up, 0, tmp_ref, keep_ref, send_ref, core, pl.ds(0, size), pl.ds(j * short, short), sems)

    @pl.when(j > 0)
    def _():
        finish(1, True)
    down = dot_tn(hid_ref[...], db_ref[...]).astype(BF).reshape(size // 2, 2, long, width)
    at = pl.ds(4 * short + (j // 2) * long, long)
    put_rows(down, 1, tmp_ref, keep_ref, send_ref, core, pl.ds((j % 2) * (size // 2), size // 2), at, sems)

    @pl.when(j == pl.num_programs(0) - 1)
    def _():
        finish(0, False)
        finish(1, True)


def att_grads_kernel(core_ref, n_ref, dproj_ref, ctx_a, ctx_b, db_ref, keep_ref, send_ref, tmp_ref, sems):
    core, j = core_ref[0], pl.program_id(0)
    width = n_ref.shape[1]
    size = keep_ref.shape[0]
    short = width // (2 * size)
    slot = lax.rem(j, 2)
    tmp = tmp_ref.at[slot].reshape(size, 2, short, width)

    def finish(at):
        for i, ref in enumerate((keep_ref, send_ref)):
            to = ref.at[:, pl.ds(0, short)]
            pltpu.make_async_copy(to, to, sems.at[at, i]).wait()

    @pl.when(j > 1)
    def _():
        finish(slot)

    @pl.when(j < 3)
    def _():
        tmp[...] = dot_tn(n_ref[...], dproj_ref[...]).astype(BF).reshape(tmp.shape)

    @pl.when(j == 3)
    def _():
        for i, ctx_ref in enumerate((ctx_a, ctx_b)):
            grad = dot_tn(ctx_ref[...], db_ref[...]).astype(BF)
            tmp[pl.ds(i * (size // 2), size // 2)] = grad.reshape(size // 2, 2, short, width)

    at = pl.ds(j * short, short)
    pltpu.make_async_copy(tmp.at[:, core], keep_ref.at[:, at], sems.at[slot, 0]).start()
    pltpu.make_async_copy(tmp.at[:, 1 - core], send_ref.at[:, at], sems.at[slot, 1]).start()

    @pl.when(j == 3)
    def _():
        finish(0)
        finish(1)


def plain_grads(att, core, shape, a, b, c, d):
    size, _, width = shape
    cut = lambda grad: [grad[:, j * width : (j + 1) * width].reshape(size, 2, -1, width) for j in range(grad.shape[1] // width)]
    parts = cut(dot_tn(a, b).astype(BF))
    if att:
        parts += cut(dot_tn(c, d).astype(BF))
    else:
        parts += [half.reshape(size, 2, -1, width) for half in jnp.split(dot_tn(c, d).astype(BF), 2, axis=0)]
    both = jnp.concatenate(parts, axis=2)
    at = lambda i: lax.dynamic_index_in_dim(both, i, 1, keepdims=False)
    return at(core), at(1 - core)


def weight_grads(kernel, core, size, us, a, b, c, d):
    rows, width = a.shape
    att = kernel is att_grads_kernel
    shape = (size, (2 * width if att else 4 * width) // size, width)
    if width // (2 * size) % 16:
        return plain_grads(att, core, shape, a, b, jnp.concatenate(c, axis=1), d)
    col = pl.BlockSpec((rows, width), lambda j: (0, jnp.minimum(j, 2 if att else 3)))
    return pl.pallas_call(
        kernel,
        grid=(4,),
        in_specs=[SMEM, whole(a.shape), col, *([whole(v.shape) for v in c] if att else [col]), whole(d.shape)],
        out_specs=[ANY] * 2,
        out_shape=[jax.ShapeDtypeStruct(shape, BF)] * 2,
        scratch_shapes=[pltpu.VMEM((2, width, width), BF), pltpu.SemaphoreType.DMA((2, 2))],
        compiler_params=params_for(48),
        cost_estimate=cost(us),
        name=kernel.__name__[:-7],
    )(core.astype(jnp.int32).reshape(1), a, b, *c, d)


def send(value, pairs):
    return lax.ppermute(value, "pipe", pairs)


def swap(value, bit):
    return send(value, [(i, i ^ bit) for i in range(lax.axis_size("pipe"))])


def to_target(value, target, bit):
    return send(value, [(target ^ bit, target)])


def pick(core, mine_first, mine_second):
    return jnp.where(core == 0, mine_first, mine_second)


ORDERS = (("x", "y", "z2", "z4"), ("y", "z2", "x", "z4"), ("z2", "x", "y", "z4"))
AT = {"x": ("dp", 1), "z2": ("dp", 2), "z4": ("dp", 4), "y": ("pipe", 2)}


def cube_start(parts):
    size, rows, width = parts.shape
    if size != 8:
        return parts
    parts = parts.reshape(2, 2, 2, 2, rows // 2, width)
    share = width // len(ORDERS)
    return [(parts[..., i * share : (i + 1) * share], None, ["z4", "z2", "x", "y"]) for i in range(len(ORDERS))]


def settled(part, got):
    return part if got is None else part + got


def halve(part, names, axis):
    name, bit = AT[axis]
    i = names.index(axis)
    me = (lax.axis_index(name) // bit) % 2
    at = lambda j: lax.dynamic_index_in_dim(part, j, i, keepdims=False)
    give = at(1 - me)
    got = lax.ppermute(give, name, [(k, k ^ bit) for k in range(lax.axis_size(name))])
    return at(me), got, [n for n in names if n != axis], give


def cube_step(state, step):
    if not isinstance(state, list):
        return state, state
    done = [halve(settled(part, got), names, order[step]) for (part, got, names), order in zip(state, ORDERS)]
    return [d[:3] for d in done], [d[3] for d in done]


def cube_end(state):
    if not isinstance(state, list):
        plane = lax.axis_index("pipe") // 2
        parts = state.reshape(state.shape[0], 2, -1, state.shape[2])
        at = lambda i: lax.dynamic_index_in_dim(parts, i, 1, keepdims=False)
        return (lax.psum_scatter(at(plane) + swap(at(1 - plane), 2), "dp", scatter_dimension=0), None), state
    whole_part = jnp.concatenate([settled(part, got) for part, got, _ in state], axis=-1)
    mine, got, _, give = halve(whole_part, ["z4"], "z4")
    return (mine, got), give


def line_start(parts):
    return lax.psum_scatter(parts, "dp", scatter_dimension=0)


def line_end(mlp, att):
    plane = lax.axis_index("pipe") // 2
    cut = lambda v, i: lax.dynamic_index_in_dim(v.reshape(2, -1, v.shape[1]), i, 0, keepdims=False)
    got = swap(jnp.concatenate([cut(mlp, 1 - plane), cut(att, 1 - plane)], axis=0), 2)
    rows = mlp.shape[0] // 2
    return cut(mlp, plane) + got[:rows], cut(att, plane) + got[rows:]


def by_sender(layer, even, odd, core, bits):
    targets = (2 * layer, 2 * layer + 1)
    mine, other = pick(core, even, odd), pick(core, odd, even)
    return [send(mine if bit == 2 else other, [(t ^ bit, t) for t in targets]) for bit in bits]


def from_pipe(value, target, sources):
    return [value if i == target else send(value, [(i, target)]) for i in sources]


def att_result(got):
    rows = got[0].shape[0] // 2
    cols = []
    for j in range(4):
        cols.append(jnp.concatenate([got[(j // 2) * 2 + c][(j % 2) * rows : (j % 2 + 1) * rows] for c in range(2)], axis=0))
    return jnp.concatenate(cols, axis=1)


def up_result(up):
    rows = up[0].shape[0] // 4
    return jnp.concatenate([jnp.concatenate([v[j * rows : (j + 1) * rows] for v in up], axis=0) for j in range(4)], axis=1)


def choose(place, options):
    result = options[-1]
    for s in range(len(options) - 2, -1, -1):
        result = jnp.where(place == s, options[s], result)
    return result


def small_sum(value, step):
    if lax.axis_size("dp") != 8:
        return lax.psum(value, ("dp", "pipe")) if step == 0 else value
    if step < 2:
        return value + swap(value, step + 1)
    return value + dp_swap(value, 1 << (step - 2))


def local(
    inputs, out_grad, page_side, norm_gain, norm_shift, layer_scale, w_first, w_half, rel_table
):
    place = lax.axis_index("pipe")
    sections = lax.axis_size("pipe")
    dp_size, dp_place = lax.axis_size("dp"), lax.axis_index("dp")
    micro_count, slot_rows, width = inputs.shape
    halves = sections // micro_count
    assert halves == 2 and sections == 4
    rows = slot_rows // halves
    plane, core = place // 2, place % 2
    layers, heads = rel_table.shape[:2]

    own_params = jnp.stack([norm_gain[0], norm_shift[0], layer_scale[0]])
    seen = [own_params] + [swap(own_params, bit) for bit in (1, 2, 3)]
    params = [choose(place, [seen[s ^ p] for p in range(sections)]) for s in range(sections)]

    own_first, own_half = w_first[0], w_half[0]
    count = own_first.shape[0] // 2
    quarter = count // 4
    q = dp_place % 4
    infos = [jnp.stack([(plane == layer).astype(jnp.int32), core.astype(jnp.int32)]) for layer in range(layers)]

    micro, half = plane, core
    side = lax.dynamic_index_in_dim(page_side, micro, 0, keepdims=False)[0]
    own_rows = lambda x: lax.dynamic_slice(x, (micro, half * rows, 0), (1, rows, width))[0]
    key_ids = (jnp.arange(slot_rows, dtype=jnp.int32) + half * rows) % slot_rows
    layout = geometry(side, key_ids, slot_rows)
    own_layout = [c[:rows] for c in layout]
    hot, hot_back = row_features(*own_layout, True), row_features(*own_layout, False)
    keys = key_features(*layout)
    maps = table_rows(rel_table)

    current = own_rows(inputs)
    qkv = own_first[:, : 3 * width]
    far_qkv = (send(qkv[:count], [(0, 2), (2, 0)]), send(qkv[count:], [(0, 3), (2, 1)]))
    share = [lax.dynamic_slice_in_dim(own_first, c * count + q * quarter, quarter, 0) for c in range(2)]
    half_rows = own_half.shape[0] // 4
    share_half = lax.dynamic_slice_in_dim(own_half, q * half_rows, half_rows, 0)
    own_out = own_first[:, 3 * width :]
    ready = (far_qkv, params, infos, current, hot, hot_back, keys, maps, share, share_half, own_out)
    far_qkv, params, infos, current, hot, hot_back, keys, maps, share, share_half, own_out = together(ready)
    far_qkv = pick(core, *far_qkv)
    qkv_refs = (own_first, swap(own_first, 1), far_qkv, swap(far_qkv, 1))
    mine_up = (send(share[0], [(1, 2), (3, 0)]), send(share[1], [(1, 3), (3, 1)]))
    mine_half = swap(share_half, 2)

    def shared(even, odd, layer):
        mine, other = pick(core, even, odd), pick(core, odd, even)
        inside = [(2 * layer, 2 * layer + 1), (2 * layer + 1, 2 * layer)]
        straight = [(p ^ 2, p) for p in (2 * layer, 2 * layer + 1)]
        across = [(p ^ 3, p) for p in (2 * layer, 2 * layer + 1)]
        return [mine, send(other, inside), send(mine, straight), send(other, across)]

    def to_one(value, s):
        return [value] + [to_target(value, s, bit) for bit in (1, 2, 3)]

    def collected(parts):
        return choose(place, [jnp.stack([parts[s][i ^ s] for i in range(sections)]) for s in range(sections)])

    kept, outs = [], {}
    cut = heads // 4
    for layer in range(layers):
        p0, p1, info = params[2 * layer], params[2 * layer + 1], infos[layer]
        normed, proj = project(info, current, p0, qkv_refs)
        if layer == 0:
            normed, proj, mine_up, mine_half = together((normed, proj, mine_up, mine_half))
            some_up = quad_start(pick(core, *mine_up))
        partner = swap(proj[:, width:], 1)
        front = lambda keys, i: attn_forward(hot, maps[layer], proj, partner, keys, i * cut, cut)
        if layer == 0:
            partner, own_out = together((partner, own_out))
            some_half = quad_start(mine_half)
            far_out = send(own_out, [(0, 2), (2, 0)])
        part_a = front(keys, 0)
        if layer == 0:
            part_a, some_up, some_half = together((part_a, some_up, some_half))
            all_up, all_half = quad_end(*some_up), quad_end(*some_half)
        part_b = front(tie(keys, part_a[0]), 1)
        if layer == 0:
            part_b, all_up, all_half, far_out = together((part_b, all_up, all_half, far_out))
            far_up, far_half = quad_place(*all_up), quad_place(*all_half)
            far_out = pick(core, far_out, swap(far_out, 1))
            near_half = swap(tie(own_half, far_qkv), 1)
            more_refs = (qkv_refs[0], qkv_refs[1], far_out, far_out)
            up_refs = (qkv_refs[0], qkv_refs[1], far_up, swap(far_up, 1))
            down_refs = (own_half, near_half, far_half, swap(far_half, 1))
        else:
            part_b = tie(part_b, outs[0][2])
        context = (part_a[0], part_b[0])
        b0, x1, n1, slope, hidden, b1, x2 = block_out(info, current, context, p0, p1, more_refs, up_refs, down_refs)
        if layer == 1:
            b0, x1, n1, slope, hidden, b1, x2 = tie((b0, x1, n1, slope, hidden, b1, x2), outs[0])
        kept.append((current, normed, proj, partner, (part_a, part_b), b0, x1, n1, slope, hidden, b1))
        outs[2 * layer] = outs[2 * layer + 1] = shared(x1, x2, layer)
        current = x2

    tables, vecs, grads = {}, {}, {}
    core_id = core.astype(jnp.int32)

    x, normed, proj, partner, outcome, b0, x1, n1, slope, hidden, b1 = kept[1]
    p0, p1, info = params[2], params[3], infos[1]
    grad = tie(own_rows(out_grad), current)
    db1, d_pre, gx1, db0, d_context, vec1 = block_back(info, grad, x1, slope, b1, b0, p0, p1, more_refs, up_refs, down_refs)
    db1, d_pre, gx1, db0, d_context, vec1 = tie((db1, d_pre, gx1, db0, d_context, vec1), outs[2][2])
    keep, other = weight_grads(mlp_grads_kernel, core, dp_size, 15, n1, d_pre, (hidden,), db1)
    keep, other = tie((keep, other), outs[2])
    got = swap(other, 1)
    back = lambda d_ctx, i: attn_backward(hot_back, outcome[i][3], proj, partner, keys, d_ctx, outcome[i][:3], i * cut, cut)
    dqa, mya, oa, ta = back(tie(d_context, keep), 0)
    dqa, mya, oa, ta, got = together((dqa, mya, oa, ta, got))
    mlp_b = keep + got
    gota = swap(oa, 1)
    dqb, myb, ob, tb = back(tie(d_context, mlp_b, oa), 1)
    dqb, myb, ob, tb, gota = together((dqb, myb, ob, tb, gota))
    gotb = swap(ob, 1)
    mlp_b = line_start(mlp_b)
    d_proj, gx0, vec0 = project_back(info, gx1, x, p0, (dqa, dqb, mya, myb, gota, gotb), qkv_refs)
    keep, other = weight_grads(att_grads_kernel, core, dp_size, 9, normed, d_proj, [part[0] for part in outcome], db0)
    got = swap(other, 1)
    grads[2] = grads[3] = shared(gx0, gx1, 1)
    tables[1] = (ta, tb)
    vecs[3], vecs[2] = vec1[:3], jnp.concatenate([vec0[:2], vec1[3:4]])

    x, normed, proj, partner, outcome, b0, x1, n1, slope, hidden, b1 = kept[0]
    p0, p1, info = params[0], params[1], infos[0]
    db1, d_pre, gx1, db0, d_context, vec1 = block_back(info, tie(gx0, keep), x1, slope, b1, b0, p0, p1, more_refs, up_refs, down_refs)
    db1, d_pre, gx1, db0, d_context, vec1, got = tie((db1, d_pre, gx1, db0, d_context, vec1, got), grads[2][2])
    att_b = keep + got
    d_pre = tie(d_pre, att_b)
    att_b = line_start(att_b)
    keep, other = weight_grads(mlp_grads_kernel, core, dp_size, 15, n1, d_pre, (hidden,), db1)
    keep, other = tie((keep, other), grads[2])
    got = swap(other, 1)
    grads[1] = to_one(gx1, 1)
    dqa, mya, oa, ta = back(tie(d_context, keep), 0)
    dqa, mya, oa, ta, got, mlp_b = tie((dqa, mya, oa, ta, got, mlp_b), grads[1])
    mlp_a = cube_start(keep + got)
    gota = swap(oa, 1)
    mlp_a, given = cube_step(mlp_a, 0)
    dqb, myb, ob, tb = back(tie(d_context, given, oa), 1)
    dqb, myb, ob, tb, gota, mlp_a = hold((dqb, myb, ob, tb, gota, mlp_a), 5)
    gotb = swap(ob, 1)
    mlp_a, given = cube_step(mlp_a, 1)
    gotb = tie(gotb, given)
    d_proj, gx0, vec0 = project_back(info, gx1, x, p0, (dqa, dqb, mya, myb, gota, gotb), qkv_refs)
    d_proj, gx0, vec0, mlp_a = hold((d_proj, gx0, vec0, mlp_a), 3)
    mlp_a, given = cube_step(mlp_a, 2)
    grads[0] = to_one(tie(gx0, given), 0)
    keep, other = weight_grads(att_grads_kernel, core, dp_size, 9, tie(normed, given), d_proj, [part[0] for part in outcome], db0)
    keep, other, att_b, grads[0][1], mlp_a = hold((keep, other, att_b, grads[0][1], mlp_a), 4)
    got = swap(other, 1)
    tables = [(ta, tb), tables[1]]
    vecs[1], vecs[0] = vec1[:3], jnp.concatenate([vec0[:2], vec1[3:4]])
    stack = lambda parts: jnp.stack([parts[s] for s in range(sections)])
    table_all = [jnp.concatenate(tables[layer])[:, :4].reshape(heads, 2, 128)[..., : 2 * SIDE_L + 1] for layer in range(layers)]
    small = jnp.concatenate([stack(vecs).reshape(-1), jnp.stack(table_all).reshape(-1)])
    small = small_sum(small, 0)
    mlp_a, _ = cube_end(mlp_a)
    got, keep, small = together((got, keep, small))
    att_sum = keep + got
    att_a = line_start(att_sum)
    mlp_b, att_b, small, outs = tie((mlp_b, att_b, small, outs), att_sum)
    mlp_b, att_b = line_end(mlp_b, att_b)
    small = small_sum(small, 1)
    section_out = collected(outs).reshape(1, micro_count, slot_rows, width)
    small, section_out, mlp_b, att_b, mlp_a, grads[0] = together((small, section_out, mlp_b, att_b, mlp_a, grads[0]))
    mlp_a = settled(*mlp_a)
    low, high = jnp.split(mlp_a, 2, axis=0)
    small = small_sum(small, 2)
    ups = [mlp_a, send(mlp_a, [(0, 1)])]
    downs = by_sender(0, low, high, core, (2, 3))
    small, ups, downs, mlp_b, att_b = together((small, ups, downs, mlp_b, att_b))
    small = small_sum(small, 3)
    even = jnp.concatenate([att_b, mlp_b[: att_b.shape[0]]], axis=0)
    own_b = pick(core, even, mlp_b)
    got_b = by_sender(1, even, mlp_b, core, (1, 2, 3))
    grads = tie(grads, own_b)
    in_grads = collected({s: [part.astype(F32) for part in grads[s]] for s in range(sections)}).reshape(1, micro_count, slot_rows, width)
    small, got_b, in_grads, att_a = together((small, got_b, in_grads, att_a))
    small = small_sum(small, 4)
    got_a = from_pipe(att_a, 0, range(4))

    first_grads, half_grads = {}, {}
    rows_a = [(got_a[c].astype(F32) + got_a[2 + c].astype(F32)).reshape(4, -1, width) for c in range(2)]
    first_grads[0] = jnp.concatenate([jnp.concatenate([v[j] for v in rows_a], axis=0) for j in range(4)], axis=1)
    first_grads[1] = up_result([ups[1], ups[0]])
    half_grads[0] = jnp.concatenate(downs, axis=0)
    half_grads[1] = jnp.concatenate(downs[::-1], axis=0)
    by_bit = [own_b, *got_b]
    on = lambda target: [by_bit[p ^ target] for p in range(sections)]
    piece = att_b.shape[0]
    first_grads[2] = att_result([v[:piece] for v in on(2)])
    half_grads[2] = jnp.concatenate([v[piece:] for v in on(2)[2:]], axis=0)
    first_grads[3] = up_result(on(3)[:2])
    half_grads[3] = jnp.concatenate([v[piece:] for v in on(3)[2:]], axis=0)

    g_first = choose(place, [first_grads[s].astype(F32) for s in range(sections)])[None]
    g_half = choose(place, [half_grads[s].astype(F32) for s in range(sections)])[None]
    vec_size = sections * 3 * width
    vec_all = small[:vec_size].reshape(sections, 3, width)
    g_table = small[vec_size:].reshape(rel_table.shape)
    cols = width // dp_size
    mine = lax.dynamic_slice(vec_all, (place, 0, dp_place * cols), (1, 3, cols))
    return (section_out, in_grads, g_first, g_half, mine[:, 0], mine[:, 1], mine[:, 2], g_table)


def solution(mesh):
    in_specs = (
        P(None, "dp", None),
        P(None, "dp", None),
        P(None, "dp"),
        P("pipe", None),
        P("pipe", None),
        P("pipe", None),
        P("pipe", None, None),
        P("pipe", None, None),
        P(),
    )
    out_specs = (
        P("pipe", None, "dp", None),
        P("pipe", None, "dp", None),
        P("pipe", "dp", None),
        P("pipe", "dp", None),
        P("pipe", "dp"),
        P("pipe", "dp"),
        P("pipe", "dp"),
        P(),
    )
    return jax.shard_map(local, mesh=mesh, in_specs=in_specs, out_specs=out_specs, check_vma=False)
```

```python
from functools import partial

import jax
import jax.numpy as jnp
import numpy as np
from jax import lax
from jax.experimental import pallas as pl
from jax.experimental.pallas import tpu as pltpu
from jax.sharding import PartitionSpec as P

SIDE_L = 32
CELLS = SIDE_L + 1
HEAD = 64
PAIR = 2 * HEAD
PAGES = 8
BLOCK = 40
PAGE_AT = 3 * CELLS
MASKED = 1e30
EPSILON = 1e-06
LOG2E = 1.4426950408889634
LN2 = 0.6931471805599453
BF = jnp.bfloat16
F32 = jnp.float32
NT = (((1,), (1,)), ((), ()))
TN = (((0,), (0,)), ((), ()))


def dot(a, b):
    return jnp.dot(a, b, preferred_element_type=F32)


def dot_nt(a, b):
    return lax.dot_general(a, b, NT, preferred_element_type=F32)


def dot_tn(a, b):
    return lax.dot_general(a, b, TN, preferred_element_type=F32)


def geometry(grid_side, row_ids, slot_rows):
    page_len = grid_side * grid_side + 1
    page_count = slot_rows // page_len
    page_of = jnp.minimum(row_ids // page_len, page_count)
    offset = row_ids - page_of * page_len
    patch_id = jnp.maximum(offset - 1, 0)
    inside = page_of < page_count
    class_row = offset == 0
    coord_y = jnp.where(inside, jnp.where(class_row, SIDE_L, patch_id // grid_side), 0)
    coord_x = jnp.where(inside, jnp.where(class_row, SIDE_L, patch_id % grid_side), 0)
    return page_of, coord_y, coord_x


def row_features(page_of, coord_y, coord_x, flip):
    lane = jnp.arange(128, dtype=jnp.int32)[None, :]
    at = (lambda c: SIDE_L - c) if flip else (lambda c: c)
    hot = (lane == at(coord_y)[:, None]) | (lane == BLOCK + at(coord_x)[:, None])
    hot = hot | (lane == 2 * BLOCK + page_of[:, None])
    return hot.astype(BF)


def key_features(page_of, coord_y, coord_x):
    lane = jnp.arange(256, dtype=jnp.int32)[None, :]
    at_y = SIDE_L - coord_y[:, None]
    at_x = SIDE_L - coord_x[:, None]
    hot = (lane == at_y) | (lane == HEAD + at_y) | (lane == 128 + at_x)
    hot = hot | (lane == 128 + CELLS + at_y) | (lane == 128 + 2 * CELLS + at_x)
    hot = hot | (lane == 128 + PAGE_AT + page_of[:, None])
    return hot.astype(BF)


def table_rows(rel_table):
    layers, heads = rel_table.shape[:2]
    scaled = rel_table * LOG2E
    gap = jnp.zeros((*scaled.shape[:3], 128 - 2 * SIDE_L - 1), F32)
    scaled = jnp.concatenate([scaled[..., SIDE_L:], gap, scaled[..., :SIDE_L]], axis=-1)
    high = scaled.astype(BF).astype(F32)
    return jnp.concatenate([high, scaled - high], axis=2).reshape(layers, heads // 2, 8, 128)


def table_map(table_ref, head):
    row = lax.broadcasted_iota(jnp.int32, (BLOCK, 128), 0)
    lane = lax.broadcasted_iota(jnp.int32, (BLOCK, 128), 1)

    def grid(i, to):
        values = jnp.broadcast_to(table_ref[0, 4 * head + i : 4 * head + i + 1, :], (BLOCK, 128))
        values = pltpu.roll(values, 0, 1, stride=1, stride_axis=0)
        values = jnp.where((row < CELLS) & (lane < CELLS), values, 0.0)
        return pltpu.roll(values, to, 1) if to else values

    none = jnp.zeros((BLOCK, 128), F32)
    far = jnp.where((lane >= PAGE_AT) & (lane < PAGE_AT + PAGES) & (lane - PAGE_AT != row) & (row < PAGES), -MASKED, 0.0)
    left = [grid(0, HEAD if head == 0 else 0), none, none, none[:8]]
    right = [grid(2, CELLS), grid(1, 0) + grid(3, 2 * CELLS), far, none[:8]]
    return jnp.concatenate([jnp.concatenate(left, axis=0), jnp.concatenate(right, axis=0)], axis=1).astype(BF)


def split3(value):
    high = value.astype(BF).astype(F32)
    middle = (value - high).astype(BF).astype(F32)
    return high, middle, value - high - middle


def lanes_of(rows):
    return lax.broadcasted_iota(jnp.int32, (rows, PAIR), 1)


def attn_fwd_kernel(hot_ref, map_ref, q_ref, ko_ref, kp_ref, vo_ref, vp_ref, key_ref,
                    o_ref, rest_ref, inv_ref, w_ref, kx_ref, vx_ref):
    rows = q_ref.shape[0]
    lane = lanes_of(rows)
    for head in range(2):
        mine = (lane < HEAD) if head == 0 else (lane >= HEAD)
        one_at = HEAD if head == 0 else 0
        table = table_map(map_ref, head)
        kx, vx = kx_ref.at[head], vx_ref.at[head]
        kx[:, PAIR:] = key_ref[:, PAIR:]
        for part, (k_ref, v_ref) in enumerate(((ko_ref, vo_ref), (kp_ref, vp_ref))):
            at = pl.ds(part * rows, rows)
            kx[at, :PAIR] = jnp.where(mine, k_ref[...], key_ref[at, :PAIR])
            vx[at, :] = jnp.where(mine, v_ref[...], jnp.where(lane == one_at, 1.0, 0.0).astype(BF))
        feats = dot(hot_ref[...], table).astype(BF)
        query = jnp.concatenate([jnp.where(mine, q_ref[...], feats[:, :PAIR]), feats[:, PAIR:]], axis=1)
        scores = dot_nt(kx[...], query)
        weights = jnp.exp2(scores - jnp.max(scores, axis=0, keepdims=True)).astype(BF)
        w_ref[head] = weights
        mixed = dot_tn(vx[...], weights).T
        inv = 1.0 / mixed[:, one_at : one_at + 1]
        out = mixed * inv
        high = out.astype(BF)
        rest = (out - high.astype(F32)).astype(BF)
        inv = jnp.broadcast_to(inv, out.shape)
        if head == 0:
            o_ref[...], rest_ref[...], inv_ref[...] = high, rest, inv
        else:
            o_ref[...] = jnp.where(mine, high, o_ref[...])
            rest_ref[...] = jnp.where(mine, rest, rest_ref[...])
            inv_ref[...] = jnp.where(mine, inv, inv_ref[...])


def attn_forward(hot, maps, project, partner, keys, first, count):
    rows, width = project.shape[0], project.shape[1] // 3
    pairs = width // PAIR
    col = lambda off: pl.BlockSpec((rows, PAIR), lambda g: (0, off + first + g))
    out = pl.BlockSpec((rows, PAIR), lambda g: (0, g))
    return pl.pallas_call(
        attn_fwd_kernel,
        grid=(count,),
        in_specs=[
            whole((rows, 128)),
            pl.BlockSpec((1, 8, 128), lambda g: (first + g, 0, 0)),
            col(0),
            col(pairs),
            col(0),
            col(2 * pairs),
            col(pairs),
            whole((2 * rows, 256)),
        ],
        out_specs=[out, out, out, pl.BlockSpec((2, 2 * rows, rows), lambda g: (g, 0, 0))],
        out_shape=[
            jax.ShapeDtypeStruct((rows, count * PAIR), BF),
            jax.ShapeDtypeStruct((rows, count * PAIR), BF),
            jax.ShapeDtypeStruct((rows, count * PAIR), F32),
            jax.ShapeDtypeStruct((2 * count, 2 * rows, rows), BF),
        ],
        scratch_shapes=[pltpu.VMEM((2, 2 * rows, 256), BF), pltpu.VMEM((2, 2 * rows, PAIR), BF)],
        compiler_params=params_for(56),
        cost_estimate=cost(26),
        name="attn_fwd",
    )(hot, maps, project, project, partner, project, partner, keys)


def attn_bwd_kernel(hot_ref, w_ref, q_ref, ko_ref, kp_ref, vo_ref, vp_ref, key_ref, do_ref, o_ref, rest_ref, inv_ref,
                    dq_ref, mine_ref, other_ref, gt_ref, kx_ref, vx_ref, ds_ref):
    rows = q_ref.shape[0]
    lane = lanes_of(rows)
    scaled = (do_ref[...].astype(F32) * inv_ref[...]).astype(BF)
    product = scaled.astype(F32) * (o_ref[...].astype(F32) + rest_ref[...].astype(F32))
    for head in range(2):
        mine = (lane < HEAD) if head == 0 else (lane >= HEAD)
        spot = lane - (HEAD if head == 0 else 0)
        kx, vx, ds = kx_ref.at[head], vx_ref.at[head], ds_ref.at[head]
        kx[:, PAIR:] = key_ref[:, PAIR:]
        ones = jnp.where((spot >= 0) & (spot < 3), 1.0, 0.0).astype(BF)
        for part, (k_ref, v_ref) in enumerate(((ko_ref, vo_ref), (kp_ref, vp_ref))):
            at = pl.ds(part * rows, rows)
            kx[at, :PAIR] = jnp.where(mine, k_ref[...], key_ref[at, :PAIR])
            vx[at, :] = jnp.where(mine, v_ref[...], ones)
        delta = jnp.sum(jnp.where(mine, product, 0.0), axis=1, keepdims=True)
        high, middle, low = split3(delta)
        spread = jnp.where(spot == 0, -high, jnp.where(spot == 1, -middle, jnp.where(spot == 2, -low, 0.0)))
        d_out = jnp.where(mine, scaled, spread.astype(BF))
        for part, out_ref in enumerate((mine_ref, other_ref)):
            at = pl.ds(part * rows, rows)
            weights = w_ref[head, at, :]
            d_scores = (weights.astype(F32) * dot_nt(vx[at, :], d_out)).astype(BF)
            ds[at, :] = d_scores
            d_value = dot(weights, scaled).astype(BF)
            d_key = (dot(d_scores, q_ref[...]) * LN2).astype(BF)
            if head == 0:
                out_ref[1], out_ref[0] = d_value, d_key
            else:
                out_ref[1] = jnp.where(mine, d_value, out_ref[1])
                out_ref[0] = jnp.where(mine, d_key, out_ref[0])
        d_query = dot_tn(ds[...], kx[...])
        high_q = d_query.astype(BF)
        low_q = (d_query - high_q.astype(F32)).astype(BF)
        grid = dot_tn(hot_ref[...], high_q) + dot_tn(hot_ref[...], low_q)
        row = lax.broadcasted_iota(jnp.int32, (BLOCK, 128), 0)
        column = lax.broadcasted_iota(jnp.int32, (BLOCK, 128), 1)
        for axis in range(2):
            part = grid[axis * BLOCK : (axis + 1) * BLOCK, axis * 128 : (axis + 1) * 128]
            part = pltpu.roll(part, HEAD, 1) if axis == 0 and head == 0 else part
            part = jnp.where((row < CELLS) & (column < CELLS), part, 0.0)
            along = pltpu.roll(part, 0, 1, stride=1, stride_axis=0)
            gt_ref[0, 2 * head + axis : 2 * head + axis + 1, :] = jnp.sum(along, axis=0, keepdims=True)
        d_query = (d_query[:, :PAIR] * HEAD**-0.5).astype(BF)
        dq_ref[...] = d_query if head == 0 else jnp.where(mine, d_query, dq_ref[...])
    gt_ref[0, 4:8, :] = jnp.zeros((4, 128), F32)


def attn_backward(hot, weights, project, partner, keys, d_context, outcome, first, count):
    rows, width = project.shape[0], project.shape[1] // 3
    pairs = width // PAIR
    col = lambda off: pl.BlockSpec((rows, PAIR), lambda g: (0, off + first + g))
    out = pl.BlockSpec((rows, PAIR), lambda g: (0, g))
    both = pl.BlockSpec((2, rows, PAIR), lambda g: (0, 0, g))
    return pl.pallas_call(
        attn_bwd_kernel,
        grid=(count,),
        in_specs=[
            whole((rows, 128)),
            pl.BlockSpec((2, 2 * rows, rows), lambda g: (g, 0, 0)),
            col(0),
            col(pairs),
            col(0),
            col(2 * pairs),
            col(pairs),
            whole((2 * rows, 256)),
            col(0),
            out,
            out,
            out,
        ],
        out_specs=[out, both, both, pl.BlockSpec((1, 8, 128), lambda g: (g, 0, 0))],
        out_shape=[
            jax.ShapeDtypeStruct((rows, count * PAIR), BF),
            jax.ShapeDtypeStruct((2, rows, count * PAIR), BF),
            jax.ShapeDtypeStruct((2, rows, count * PAIR), BF),
            jax.ShapeDtypeStruct((count, 8, 128), F32),
        ],
        scratch_shapes=[
            pltpu.VMEM((2, 2 * rows, 256), BF),
            pltpu.VMEM((2, 2 * rows, PAIR), BF),
            pltpu.VMEM((2, 2 * rows, rows), BF),
        ],
        compiler_params=params_for(56),
        cost_estimate=cost(6 * count),
        name="attn_bwd",
    )(hot, weights, project, project, partner, project, partner, keys, d_context, *outcome)


def centred(values):
    values = values - jnp.mean(values, axis=-1, keepdims=True)
    inv = lax.rsqrt(jnp.mean(values * values, axis=-1, keepdims=True) + EPSILON)
    return values * inv, inv


def start_first(info_ref, kind, cols, far_cols, refs, dst, sem):
    own, near, far_own, far_other = refs
    local, core = info_ref[0] == 1, info_ref[1]
    part = far_own.shape[0]

    @pl.when(local & (core == kind))
    def _():
        pltpu.make_async_copy(own.at[:, cols], dst, sem).start()

    @pl.when(local & (core != kind))
    def _():
        pltpu.make_async_copy(near.at[:, cols], dst, sem).start()

    @pl.when(jnp.logical_not(local))
    def _():
        if part == dst.shape[0]:
            pltpu.make_async_copy(far_own, dst, sem).start()
            return
        pltpu.make_async_copy(far_own.at[:, far_cols], dst.at[pl.ds(core * part, part)], sem).start()
        pltpu.make_async_copy(far_other.at[:, far_cols], dst.at[pl.ds((1 - core) * part, part)], sem).start()


def start_down(info_ref, refs, dst, sem):
    own, near, far_own, far_other = refs
    local, core = info_ref[0] == 1, info_ref[1]
    part = own.shape[0]
    for here, mine, other in ((local, own, near), (jnp.logical_not(local), far_own, far_other)):

        @pl.when(here)
        def _(mine=mine, other=other):
            pltpu.make_async_copy(mine, dst.at[pl.ds(core * part, part)], sem).start()
            pltpu.make_async_copy(other, dst.at[pl.ds((1 - core) * part, part)], sem).start()


def wait_for(dst, sem):
    pltpu.make_async_copy(dst, dst, sem).wait()


EARLY = True
SMEM = pl.BlockSpec(memory_space=pltpu.SMEM)
ANY = pl.BlockSpec(memory_space=pl.ANY)


def whole(shape):
    return pl.BlockSpec(shape, lambda *g: (0,) * len(shape))


def params_for(mib):
    return pltpu.CompilerParams(vmem_limit_bytes=mib * 2**20)


def cost(us):
    return pl.CostEstimate(flops=int(us * 2e7), bytes_accessed=1000, transcendentals=0)


def project_kernel(info_ref, x_ref, p_ref, own, near, far_own, far_other, normed_ref, out_ref, w_ref, sem):
    width = x_ref.shape[1]
    start_first(info_ref, 0, pl.ds(0, 3 * width), pl.ds(0, 3 * width), (own, near, far_own, far_other), w_ref, sem)
    nhat, _ = centred(x_ref[...].astype(F32))
    normed = (nhat * p_ref[0:1, :] + p_ref[1:2, :]).astype(BF)
    normed_ref[...] = normed
    wait_for(w_ref, sem)
    for j in range(3):
        at = pl.ds(j * width, width)
        value = dot(normed, w_ref[:, at])
        if j == 0:
            value = value * (HEAD**-0.5 * LOG2E)
        out_ref[:, at] = value.astype(BF)


def project(info, x, p, first_refs):
    rows, width = x.shape
    return pl.pallas_call(
        project_kernel,
        in_specs=[SMEM, whole(x.shape), whole(p.shape)] + [ANY] * 4,
        out_specs=[whole((rows, width)), whole((rows, 3 * width))],
        out_shape=[jax.ShapeDtypeStruct((rows, width), BF), jax.ShapeDtypeStruct((rows, 3 * width), BF)],
        scratch_shapes=[pltpu.VMEM((width, 3 * width), BF), pltpu.SemaphoreType.DMA],
        compiler_params=params_for(40),
        cost_estimate=cost(5),
        name="project",
    )(info, x, p, *first_refs)


def block_out_kernel(info_ref, x_ref, ctx_a, ctx_b, p0_ref, p1_ref, *refs):
    att, up, refs = refs[:4], refs[:2] + refs[4:6], refs[6:]
    down, refs = refs[:4], refs[4:]
    b0_ref, x1_ref, n1_ref, slope_ref, hid_ref, b1_ref, x2_ref, wo_ref, wu_ref, wd_ref, slopes, hiddens, sems, out_sems = refs
    width = x_ref.shape[1]
    start_first(info_ref, 0, pl.ds(3 * width, width), pl.ds(0, width), att, wo_ref, sems.at[0])
    for j in range(4):
        start_first(info_ref, 1, pl.ds(j * width, width), pl.ds(j * width, width), up, wu_ref.at[j], sems.at[1 + j])
    start_down(info_ref, down, wd_ref, sems.at[5])
    wait_for(wo_ref, sems.at[0])
    half = width // 2
    branch = dot(ctx_a[...], wo_ref[:half]) + dot(ctx_b[...], wo_ref[half:])
    b0_ref[...] = branch.astype(BF)
    x1 = (x_ref[...].astype(F32) + p0_ref[2:3, :] * branch).astype(BF)
    x1_ref[...] = x1
    x1 = x1.astype(F32)
    nhat, _ = centred(x1)
    normed = (nhat * p1_ref[0:1, :] + p1_ref[1:2, :]).astype(BF)
    n1_ref[...] = normed
    for j in range(4):
        wait_for(wu_ref.at[j], sems.at[1 + j])
    wait_for(wd_ref, sems.at[5])
    total = jnp.zeros(x1.shape, F32)
    for j in range(4):
        at = pl.ds(j * width, width)
        v = dot(normed, wu_ref[j])
        square = v * v
        bend = jnp.tanh(v * (0.7978845608028654 + (0.7978845608028654 * 0.044715) * square))
        up_half = 0.5 + 0.5 * bend
        along = v * (2 * 0.7978845608028654 + (6 * 0.7978845608028654 * 0.044715) * square)
        slopes[j] = (up_half + along * (up_half * (1.0 - up_half))).astype(BF)
        hiddens[j] = (v * up_half).astype(BF)
        if EARLY:
            pltpu.make_async_copy(slopes.at[j], slope_ref.at[:, at], out_sems.at[0, j]).start()
            pltpu.make_async_copy(hiddens.at[j], hid_ref.at[:, at], out_sems.at[1, j]).start()
        total = total + dot(hiddens[j], wd_ref[at, :])
    b1_ref[...] = total.astype(BF)
    x2_ref[...] = (x1 + p1_ref[2:3, :] * total).astype(BF)
    if not EARLY:
        for j in range(4):
            at = pl.ds(j * width, width)
            pltpu.make_async_copy(slopes.at[j], slope_ref.at[:, at], out_sems.at[0, j]).start()
            pltpu.make_async_copy(hiddens.at[j], hid_ref.at[:, at], out_sems.at[1, j]).start()
    for j in range(4):
        wait_for(slopes.at[j], out_sems.at[0, j])
        wait_for(hiddens.at[j], out_sems.at[1, j])


def block_out(info, x, context, p0, p1, more_refs, up_refs, down_refs):
    rows, width = x.shape
    one = whole((rows, width))
    shape = lambda n: jax.ShapeDtypeStruct((rows, n), BF)
    widths = [width, width, width, 4 * width, 4 * width, width, width]
    refs = (*more_refs, *up_refs[2:], *down_refs)
    return pl.pallas_call(
        block_out_kernel,
        grid=(1,),
        in_specs=[SMEM, one, *[whole(c.shape) for c in context], whole(p0.shape), whole(p1.shape)] + [ANY] * len(refs),
        out_specs=[one if n == width else ANY for n in widths],
        out_shape=[shape(n) for n in widths],
        scratch_shapes=[
            pltpu.VMEM((width, width), BF),
            pltpu.VMEM((4, width, width), BF),
            pltpu.VMEM((4 * width, width), BF),
            pltpu.VMEM((4, rows, width), BF),
            pltpu.VMEM((4, rows, width), BF),
            pltpu.SemaphoreType.DMA((6,)),
            pltpu.SemaphoreType.DMA((2, 4)),
        ],
        compiler_params=params_for(58),
        cost_estimate=cost(12),
        name="block_out",
    )(info, x, *context, p0, p1, *refs)


def norm_back(x, gain, d_normed, gy):
    nhat, inv = centred(x)
    inner = d_normed * gain
    shift = jnp.mean(inner, axis=-1, keepdims=True)
    along = jnp.mean(inner * nhat, axis=-1, keepdims=True)
    total = lambda v: jnp.sum(v, axis=0, keepdims=True)
    return gy + inv * (inner - shift - nhat * along), total(nhat * d_normed), total(d_normed)


def block_back_kernel(info_ref, gy_ref, x1_ref, slope_ref, b1_ref, b0_ref, p0_ref, p1_ref, *refs):
    att, up, refs = refs[:4], refs[:2] + refs[4:6], refs[6:]
    down, refs = refs[:4], refs[4:]
    db1_ref, dpre_ref, gx_ref, db0_ref, dctx_ref, vec_ref, wo_ref, wu_ref, wd_ref, slopes, given, sems, more_sems = refs
    width = gy_ref.shape[1]
    start_down(info_ref, down, wd_ref, sems.at[5])
    for j in range(4):
        at = pl.ds(j * width, width)
        start_first(info_ref, 1, at, at, up, wu_ref.at[j], sems.at[1 + j])
        pltpu.make_async_copy(slope_ref.at[:, at], slopes.at[j], more_sems.at[0, j]).start()
    start_first(info_ref, 0, pl.ds(3 * width, width), pl.ds(0, width), att, wo_ref, sems.at[0])
    total = lambda v: jnp.sum(v, axis=0, keepdims=True)
    gy = gy_ref[...].astype(F32)
    d_branch = (gy * p1_ref[2:3, :]).astype(BF)
    db1_ref[...] = d_branch
    vec_ref[2:3, :] = total(b1_ref[...].astype(F32) * gy)
    vec_ref[4:, :] = jnp.zeros((4, width), F32)
    d_normed = jnp.zeros(gy.shape, F32)
    wait_for(wd_ref, sems.at[5])
    for j in range(4):
        wait_for(slopes.at[j], more_sems.at[0, j])
        wait_for(wu_ref.at[j], sems.at[1 + j])
    for j in range(4):
        at = pl.ds(j * width, width)
        d_hidden = dot_nt(d_branch, wd_ref[at, :])
        given[j] = (d_hidden * slopes[j].astype(F32)).astype(BF)
        if EARLY:
            pltpu.make_async_copy(given.at[j], dpre_ref.at[:, at], more_sems.at[1, j]).start()
        d_normed = d_normed + dot_nt(given[j], wu_ref[j])
    if not EARLY:
        for j in range(4):
            pltpu.make_async_copy(given.at[j], dpre_ref.at[:, pl.ds(j * width, width)], more_sems.at[1, j]).start()
    gx, g_gain, g_shift = norm_back(x1_ref[...].astype(F32), p1_ref[0:1, :], d_normed, gy)
    vec_ref[0:1, :] = g_gain
    vec_ref[1:2, :] = g_shift
    gx = gx.astype(BF)
    gx_ref[...] = gx
    gx = gx.astype(F32)
    d_att = (gx * p0_ref[2:3, :]).astype(BF)
    db0_ref[...] = d_att
    vec_ref[3:4, :] = total(b0_ref[...].astype(F32) * gx)
    wait_for(wo_ref, sems.at[0])
    dctx_ref[...] = dot_nt(d_att, wo_ref[...]).astype(BF)
    for j in range(4):
        wait_for(given.at[j], more_sems.at[1, j])


def block_back(info, gy, x1, slope, b1, b0, p0, p1, more_refs, up_refs, down_refs):
    rows, width = gy.shape
    one = whole((rows, width))
    shape = lambda n: jax.ShapeDtypeStruct((rows, n), BF)
    widths = [width, 4 * width, width, width, width]
    refs = (*more_refs, *up_refs[2:], *down_refs)
    return pl.pallas_call(
        block_back_kernel,
        grid=(1,),
        in_specs=[SMEM, one, one, ANY, one, one, whole(p0.shape), whole(p1.shape)] + [ANY] * len(refs),
        out_specs=[one if n == width else ANY for n in widths] + [whole((8, width))],
        out_shape=[shape(n) for n in widths] + [jax.ShapeDtypeStruct((8, width), F32)],
        scratch_shapes=[
            pltpu.VMEM((width, width), BF),
            pltpu.VMEM((4, width, width), BF),
            pltpu.VMEM((4 * width, width), BF),
            pltpu.VMEM((4, rows, width), BF),
            pltpu.VMEM((4, rows, width), BF),
            pltpu.SemaphoreType.DMA((6,)),
            pltpu.SemaphoreType.DMA((2, 4)),
        ],
        compiler_params=params_for(58),
        cost_estimate=cost(14),
        name="block_back",
    )(info, gy, x1, slope, b1, b0, p0, p1, *refs)


def project_back_kernel(info_ref, gy_ref, x_ref, p_ref, dqa, dqb, mya, myb, gota, gotb, own, near, far_own, far_other,
                        dproj_ref, gx_ref, vec_ref, w_ref, sem):
    width = x_ref.shape[1]
    start_first(info_ref, 0, pl.ds(0, 3 * width), pl.ds(0, 3 * width), (own, near, far_own, far_other), w_ref, sem)
    half = width // 2
    for i, (dq, my, got) in enumerate(((dqa, mya, gota), (dqb, myb, gotb))):
        dproj_ref[:, i * half : (i + 1) * half] = dq[...]
        for j in range(2):
            at = pl.ds((1 + j) * width + i * half, half)
            dproj_ref[:, at] = (my[j].astype(F32) + got[j].astype(F32)).astype(BF)
    wait_for(w_ref, sem)
    d_normed = dot_nt(dproj_ref[:, :width], w_ref[:, :width])
    for j in (1, 2):
        at = pl.ds(j * width, width)
        d_normed = d_normed + dot_nt(dproj_ref[:, at], w_ref[:, at])
    gx, g_gain, g_shift = norm_back(x_ref[...].astype(F32), p_ref[0:1, :], d_normed, gy_ref[...].astype(F32))
    gx_ref[...] = gx.astype(BF)
    vec_ref[0:1, :] = g_gain
    vec_ref[1:2, :] = g_shift
    vec_ref[2:, :] = jnp.zeros((6, width), F32)


def project_back(info, gy, x, p, parts, first_refs):
    rows, width = x.shape
    one = whole((rows, width))
    return pl.pallas_call(
        project_back_kernel,
        in_specs=[SMEM, one, one, whole(p.shape)] + [whole(v.shape) for v in parts] + [ANY] * 4,
        out_specs=[whole((rows, 3 * width)), one, whole((8, width))],
        out_shape=[
            jax.ShapeDtypeStruct((rows, 3 * width), BF),
            jax.ShapeDtypeStruct((rows, width), BF),
            jax.ShapeDtypeStruct((8, width), F32),
        ],
        grid=(1,),
        scratch_shapes=[pltpu.VMEM((width, 3 * width), BF), pltpu.SemaphoreType.DMA],
        compiler_params=params_for(48),
        cost_estimate=cost(7),
        name="project_back",
    )(info, gy, x, p, *parts, *first_refs)


def gather_kernel(info_ref, mine, by_x, by_z, diag_x, diag_z, out_ref, sem):
    quarter = mine.shape[0]
    part = quarter // 2
    q = info_ref[0]
    at = lambda i: pl.multiple_of(i * quarter, part)
    pltpu.make_async_copy(mine, out_ref.at[pl.ds(at(q), quarter)], sem).start()
    pltpu.make_async_copy(by_x, out_ref.at[pl.ds(at(info_ref[1]), quarter)], sem).start()
    pltpu.make_async_copy(by_z, out_ref.at[pl.ds(at(info_ref[2]), quarter)], sem).start()
    pltpu.make_async_copy(diag_x, out_ref.at[pl.ds(at(info_ref[3]), part)], sem).start()
    pltpu.make_async_copy(diag_z, out_ref.at[pl.ds(at(info_ref[3]) + part, part)], sem).start()
    wait_for(out_ref, sem)


def dp_swap(value, bit):
    return lax.ppermute(value, "dp", [(i, i ^ bit) for i in range(lax.axis_size("dp"))])


def tie(value, *deps):
    return lax.optimization_barrier((value, deps))[0]


def hold(values, count):
    state = values[-1]
    if not isinstance(state, list):
        return lax.optimization_barrier(values)
    arrays = [part[:2] for part in state]
    *values, arrays = lax.optimization_barrier((*values[:count], arrays))
    return (*values, [(*part, names) for part, (_, _, names) in zip(arrays, state)])


def together(values):
    return lax.optimization_barrier(values)


def quad_start(mine):
    return mine, dp_swap(mine, 1), dp_swap(mine, 2)


def quad_end(mine, by_x, by_z):
    part = mine.shape[0] // 2
    return mine, by_x, by_z, dp_swap(by_z[:part], 1), dp_swap(by_x[part:], 2)


def quad_place(mine, *others):
    quarter = mine.shape[0]
    q = lax.axis_index("dp") % 4
    spots = jnp.stack([q, q ^ 1, q ^ 2, q ^ 3]).astype(jnp.int32)
    return pl.pallas_call(
        gather_kernel,
        in_specs=[SMEM] + [ANY] * 5,
        out_specs=whole((4 * quarter, *mine.shape[1:])),
        out_shape=jax.ShapeDtypeStruct((4 * quarter, *mine.shape[1:]), mine.dtype),
        scratch_shapes=[pltpu.SemaphoreType.DMA],
        compiler_params=params_for(16),
        cost_estimate=cost(3),
        name="assemble",
    )(spots, mine, *others)


def put_rows(values, slot, tmp_ref, keep_ref, send_ref, core, for_d, at, sems):
    tmp = tmp_ref.at[slot].reshape(values.shape)
    tmp[...] = values
    pltpu.make_async_copy(tmp.at[:, core], keep_ref.at[for_d, at], sems.at[slot, 0]).start()
    pltpu.make_async_copy(tmp.at[:, 1 - core], send_ref.at[for_d, at], sems.at[slot, 1]).start()


def mlp_grads_kernel(core_ref, n_ref, pre_ref, hid_ref, db_ref, keep_ref, send_ref, tmp_ref, sems):
    core, j = core_ref[0], pl.program_id(0)
    width = n_ref.shape[1]
    size = keep_ref.shape[0]
    short, long = width // (2 * size), 2 * width // (2 * size)

    def finish(slot, long_rows):
        for i, ref in enumerate((keep_ref, send_ref)):
            to = ref.at[pl.ds(0, size // 2), pl.ds(0, long)] if long_rows else ref.at[:, pl.ds(0, short)]
            pltpu.make_async_copy(to, to, sems.at[slot, i]).wait()

    @pl.when(j > 0)
    def _():
        finish(0, False)
    up = dot_tn(n_ref[...], pre_ref[...]).astype(BF).reshape(size, 2, short, width)
    put_rows(up, 0, tmp_ref, keep_ref, send_ref, core, pl.ds(0, size), pl.ds(j * short, short), sems)

    @pl.when(j > 0)
    def _():
        finish(1, True)
    down = dot_tn(hid_ref[...], db_ref[...]).astype(BF).reshape(size // 2, 2, long, width)
    at = pl.ds(4 * short + (j // 2) * long, long)
    put_rows(down, 1, tmp_ref, keep_ref, send_ref, core, pl.ds((j % 2) * (size // 2), size // 2), at, sems)

    @pl.when(j == pl.num_programs(0) - 1)
    def _():
        finish(0, False)
        finish(1, True)


def att_grads_kernel(core_ref, n_ref, dproj_ref, ctx_a, ctx_b, db_ref, keep_ref, send_ref, tmp_ref, sems):
    core, j = core_ref[0], pl.program_id(0)
    width = n_ref.shape[1]
    size = keep_ref.shape[0]
    short = width // (2 * size)
    slot = lax.rem(j, 2)
    tmp = tmp_ref.at[slot].reshape(size, 2, short, width)

    def finish(at):
        for i, ref in enumerate((keep_ref, send_ref)):
            to = ref.at[:, pl.ds(0, short)]
            pltpu.make_async_copy(to, to, sems.at[at, i]).wait()

    @pl.when(j > 1)
    def _():
        finish(slot)

    @pl.when(j < 3)
    def _():
        tmp[...] = dot_tn(n_ref[...], dproj_ref[...]).astype(BF).reshape(tmp.shape)

    @pl.when(j == 3)
    def _():
        for i, ctx_ref in enumerate((ctx_a, ctx_b)):
            grad = dot_tn(ctx_ref[...], db_ref[...]).astype(BF)
            tmp[pl.ds(i * (size // 2), size // 2)] = grad.reshape(size // 2, 2, short, width)

    at = pl.ds(j * short, short)
    pltpu.make_async_copy(tmp.at[:, core], keep_ref.at[:, at], sems.at[slot, 0]).start()
    pltpu.make_async_copy(tmp.at[:, 1 - core], send_ref.at[:, at], sems.at[slot, 1]).start()

    @pl.when(j == 3)
    def _():
        finish(0)
        finish(1)


def plain_grads(att, core, shape, a, b, c, d):
    size, _, width = shape
    cut = lambda grad: [grad[:, j * width : (j + 1) * width].reshape(size, 2, -1, width) for j in range(grad.shape[1] // width)]
    parts = cut(dot_tn(a, b).astype(BF))
    if att:
        parts += cut(dot_tn(c, d).astype(BF))
    else:
        parts += [half.reshape(size, 2, -1, width) for half in jnp.split(dot_tn(c, d).astype(BF), 2, axis=0)]
    both = jnp.concatenate(parts, axis=2)
    at = lambda i: lax.dynamic_index_in_dim(both, i, 1, keepdims=False)
    return at(core), at(1 - core)


def weight_grads(kernel, core, size, us, a, b, c, d):
    rows, width = a.shape
    att = kernel is att_grads_kernel
    shape = (size, (2 * width if att else 4 * width) // size, width)
    if width // (2 * size) % 16:
        return plain_grads(att, core, shape, a, b, jnp.concatenate(c, axis=1), d)
    col = pl.BlockSpec((rows, width), lambda j: (0, jnp.minimum(j, 2 if att else 3)))
    return pl.pallas_call(
        kernel,
        grid=(4,),
        in_specs=[SMEM, whole(a.shape), col, *([whole(v.shape) for v in c] if att else [col]), whole(d.shape)],
        out_specs=[ANY] * 2,
        out_shape=[jax.ShapeDtypeStruct(shape, BF)] * 2,
        scratch_shapes=[pltpu.VMEM((2, width, width), BF), pltpu.SemaphoreType.DMA((2, 2))],
        compiler_params=params_for(48),
        cost_estimate=cost(us),
        name=kernel.__name__[:-7],
    )(core.astype(jnp.int32).reshape(1), a, b, *c, d)


def send(value, pairs):
    return lax.ppermute(value, "pipe", pairs)


def swap(value, bit):
    return send(value, [(i, i ^ bit) for i in range(lax.axis_size("pipe"))])


def to_target(value, target, bit):
    return send(value, [(target ^ bit, target)])


def pick(core, mine_first, mine_second):
    return jnp.where(core == 0, mine_first, mine_second)


ORDERS = (("x", "y", "z2", "z4"), ("y", "z2", "x", "z4"), ("z2", "x", "y", "z4"))
AT = {"x": ("dp", 1), "z2": ("dp", 2), "z4": ("dp", 4), "y": ("pipe", 2)}


def cube_start(parts):
    size, rows, width = parts.shape
    if size != 8:
        return parts
    parts = parts.reshape(2, 2, 2, 2, rows // 2, width)
    share = width // len(ORDERS)
    return [(parts[..., i * share : (i + 1) * share], None, ["z4", "z2", "x", "y"]) for i in range(len(ORDERS))]


def settled(part, got):
    return part if got is None else part + got


def halve(part, names, axis):
    name, bit = AT[axis]
    i = names.index(axis)
    me = (lax.axis_index(name) // bit) % 2
    at = lambda j: lax.dynamic_index_in_dim(part, j, i, keepdims=False)
    give = at(1 - me)
    got = lax.ppermute(give, name, [(k, k ^ bit) for k in range(lax.axis_size(name))])
    return at(me), got, [n for n in names if n != axis], give


def cube_step(state, step):
    if not isinstance(state, list):
        return state, state
    done = [halve(settled(part, got), names, order[step]) for (part, got, names), order in zip(state, ORDERS)]
    return [d[:3] for d in done], [d[3] for d in done]


def cube_end(state):
    if not isinstance(state, list):
        plane = lax.axis_index("pipe") // 2
        parts = state.reshape(state.shape[0], 2, -1, state.shape[2])
        at = lambda i: lax.dynamic_index_in_dim(parts, i, 1, keepdims=False)
        return (lax.psum_scatter(at(plane) + swap(at(1 - plane), 2), "dp", scatter_dimension=0), None), state
    whole_part = jnp.concatenate([settled(part, got) for part, got, _ in state], axis=-1)
    mine, got, _, give = halve(whole_part, ["z4"], "z4")
    return (mine, got), give


def line_start(parts):
    return lax.psum_scatter(parts, "dp", scatter_dimension=0)


def line_end(mlp, att):
    plane = lax.axis_index("pipe") // 2
    cut = lambda v, i: lax.dynamic_index_in_dim(v.reshape(2, -1, v.shape[1]), i, 0, keepdims=False)
    got = swap(jnp.concatenate([cut(mlp, 1 - plane), cut(att, 1 - plane)], axis=0), 2)
    rows = mlp.shape[0] // 2
    return cut(mlp, plane) + got[:rows], cut(att, plane) + got[rows:]


def by_sender(layer, even, odd, core, bits):
    targets = (2 * layer, 2 * layer + 1)
    mine, other = pick(core, even, odd), pick(core, odd, even)
    return [send(mine if bit == 2 else other, [(t ^ bit, t) for t in targets]) for bit in bits]


def from_pipe(value, target, sources):
    return [value if i == target else send(value, [(i, target)]) for i in sources]


def att_result(got):
    rows = got[0].shape[0] // 2
    cols = []
    for j in range(4):
        cols.append(jnp.concatenate([got[(j // 2) * 2 + c][(j % 2) * rows : (j % 2 + 1) * rows] for c in range(2)], axis=0))
    return jnp.concatenate(cols, axis=1)


def up_result(up):
    rows = up[0].shape[0] // 4
    return jnp.concatenate([jnp.concatenate([v[j * rows : (j + 1) * rows] for v in up], axis=0) for j in range(4)], axis=1)


def choose(place, options):
    result = options[-1]
    for s in range(len(options) - 2, -1, -1):
        result = jnp.where(place == s, options[s], result)
    return result


def small_sum(value, step):
    if lax.axis_size("dp") != 8:
        return lax.psum(value, ("dp", "pipe")) if step == 0 else value
    if step == 2:
        return value + dp_swap(value, 4)
    move = swap if step == 0 else dp_swap
    return (value + move(value, 1)) + (move(value, 2) + move(value, 3))


def local(
    inputs, out_grad, page_side, norm_gain, norm_shift, layer_scale, w_first, w_half, rel_table
):
    place = lax.axis_index("pipe")
    sections = lax.axis_size("pipe")
    dp_size, dp_place = lax.axis_size("dp"), lax.axis_index("dp")
    micro_count, slot_rows, width = inputs.shape
    halves = sections // micro_count
    assert halves == 2 and sections == 4
    rows = slot_rows // halves
    plane, core = place // 2, place % 2
    layers, heads = rel_table.shape[:2]

    own_params = jnp.stack([norm_gain[0], norm_shift[0], layer_scale[0]])
    seen = [own_params] + [swap(own_params, bit) for bit in (1, 2, 3)]
    params = [choose(place, [seen[s ^ p] for p in range(sections)]) for s in range(sections)]

    own_first, own_half = w_first[0], w_half[0]
    count = own_first.shape[0] // 2
    quarter = count // 4
    q = dp_place % 4
    infos = [jnp.stack([(plane == layer).astype(jnp.int32), core.astype(jnp.int32)]) for layer in range(layers)]

    micro, half = plane, core
    side = lax.dynamic_index_in_dim(page_side, micro, 0, keepdims=False)[0]
    own_rows = lambda x: lax.dynamic_slice(x, (micro, half * rows, 0), (1, rows, width))[0]
    key_ids = (jnp.arange(slot_rows, dtype=jnp.int32) + half * rows) % slot_rows
    layout = geometry(side, key_ids, slot_rows)
    own_layout = [c[:rows] for c in layout]
    hot, hot_back = row_features(*own_layout, True), row_features(*own_layout, False)
    keys = key_features(*layout)
    maps = table_rows(rel_table)

    current = own_rows(inputs)
    qkv = own_first[:, : 3 * width]
    far_qkv = (send(qkv[:count], [(0, 2), (2, 0)]), send(qkv[count:], [(0, 3), (2, 1)]))
    share = [lax.dynamic_slice_in_dim(own_first, c * count + q * quarter, quarter, 0) for c in range(2)]
    half_rows = own_half.shape[0] // 4
    share_half = lax.dynamic_slice_in_dim(own_half, q * half_rows, half_rows, 0)
    own_out = own_first[:, 3 * width :]
    last_grad = own_rows(out_grad)
    ready = (far_qkv, params, infos, current, last_grad, hot, hot_back, keys, maps, share, share_half, own_out)
    far_qkv, params, infos, current, last_grad, hot, hot_back, keys, maps, share, share_half, own_out = together(ready)
    far_qkv = pick(core, *far_qkv)
    qkv_refs = (own_first, swap(own_first, 1), far_qkv, swap(far_qkv, 1))
    mine_up = (send(share[0], [(1, 2), (3, 0)]), send(share[1], [(1, 3), (3, 1)]))
    mine_half = swap(share_half, 2)

    def shared(even, odd, layer):
        mine, other = pick(core, even, odd), pick(core, odd, even)
        inside = [(2 * layer, 2 * layer + 1), (2 * layer + 1, 2 * layer)]
        straight = [(p ^ 2, p) for p in (2 * layer, 2 * layer + 1)]
        across = [(p ^ 3, p) for p in (2 * layer, 2 * layer + 1)]
        return [mine, send(other, inside), send(mine, straight), send(other, across)]

    def to_one(value, s):
        return [value] + [to_target(value, s, bit) for bit in (1, 2, 3)]

    def collected(parts):
        return choose(place, [jnp.stack([parts[s][i ^ s] for i in range(sections)]) for s in range(sections)])

    kept, outs = [], {}
    cut = heads // 4
    for layer in range(layers):
        p0, p1, info = params[2 * layer], params[2 * layer + 1], infos[layer]
        normed, proj = project(info, current, p0, qkv_refs)
        if layer == 0:
            own_out = tie(own_out, normed)
        partner = swap(proj[:, width:], 1)
        front = lambda keys, i: attn_forward(hot, maps[layer], proj, partner, keys, i * cut, cut)
        if layer == 0:
            partner, own_out, mine_up = together((partner, own_out, mine_up))
            some_up = quad_start(pick(core, *mine_up))
            far_out = send(own_out, [(0, 2), (2, 0)])
        part_a = front(keys, 0)
        if layer == 0:
            part_a, some_up, mine_half = together((part_a, some_up, mine_half))
            some_half = quad_start(mine_half)
            all_up = quad_end(*some_up)
        part_b = front(tie(keys, part_a[0]), 1)
        if layer == 0:
            part_b, all_up, some_half, far_out = together((part_b, all_up, some_half, far_out))
            near_out, all_half = swap(far_out, 1), quad_end(*some_half)
            far_up, far_half = quad_place(*all_up), quad_place(*all_half)
            far_out = pick(core, far_out, near_out)
            near_half = swap(tie(own_half, far_qkv), 1)
            more_refs = (qkv_refs[0], qkv_refs[1], far_out, far_out)
            up_refs = (qkv_refs[0], qkv_refs[1], far_up, swap(far_up, 1))
            down_refs = (own_half, near_half, far_half, swap(far_half, 1))
        else:
            part_b = tie(part_b, outs[0][2])
        context = (part_a[0], part_b[0])
        b0, x1, n1, slope, hidden, b1, x2 = block_out(info, current, context, p0, p1, more_refs, up_refs, down_refs)
        if layer == 1:
            b0, x1, n1, slope, hidden, b1, x2 = tie((b0, x1, n1, slope, hidden, b1, x2), outs[0])
        kept.append((current, normed, proj, partner, (part_a, part_b), b0, x1, n1, slope, hidden, b1))
        outs[2 * layer] = outs[2 * layer + 1] = shared(x1, x2, layer)
        current = x2

    tables, vecs, grads = {}, {}, {}
    core_id = core.astype(jnp.int32)

    x, normed, proj, partner, outcome, b0, x1, n1, slope, hidden, b1 = kept[1]
    p0, p1, info = params[2], params[3], infos[1]
    grad = tie(last_grad, current)
    db1, d_pre, gx1, db0, d_context, vec1 = block_back(info, grad, x1, slope, b1, b0, p0, p1, more_refs, up_refs, down_refs)
    db1, d_pre, gx1, db0, d_context, vec1 = tie((db1, d_pre, gx1, db0, d_context, vec1), outs[2][2])
    keep, other = weight_grads(mlp_grads_kernel, core, dp_size, 15, n1, d_pre, (hidden,), db1)
    keep, other = tie((keep, other), outs[2])
    got = swap(other, 1)
    back = lambda d_ctx, i: attn_backward(hot_back, outcome[i][3], proj, partner, keys, d_ctx, outcome[i][:3], i * cut, cut)
    dqa, mya, oa, ta = back(tie(d_context, keep), 0)
    dqa, mya, oa, ta, got = together((dqa, mya, oa, ta, got))
    mlp_b = keep + got
    gota = swap(oa, 1)
    dqb, myb, ob, tb = back(tie(d_context, mlp_b, oa), 1)
    dqb, myb, ob, tb, gota = together((dqb, myb, ob, tb, gota))
    gotb = swap(ob, 1)
    mlp_b = line_start(mlp_b)
    d_proj, gx0, vec0 = project_back(info, gx1, x, p0, (dqa, dqb, mya, myb, gota, gotb), qkv_refs)
    keep, other = weight_grads(att_grads_kernel, core, dp_size, 9, normed, d_proj, [part[0] for part in outcome], db0)
    got = swap(other, 1)
    grads[2] = grads[3] = shared(gx0, gx1, 1)
    tables[1] = (ta, tb)
    vecs[3], vecs[2] = vec1[:3], jnp.concatenate([vec0[:2], vec1[3:4]])

    x, normed, proj, partner, outcome, b0, x1, n1, slope, hidden, b1 = kept[0]
    p0, p1, info = params[0], params[1], infos[0]
    db1, d_pre, gx1, db0, d_context, vec1 = block_back(info, tie(gx0, keep), x1, slope, b1, b0, p0, p1, more_refs, up_refs, down_refs)
    db1, d_pre, gx1, db0, d_context, vec1, got = tie((db1, d_pre, gx1, db0, d_context, vec1, got), grads[2][2])
    att_b = keep + got
    d_pre = tie(d_pre, att_b)
    att_b = line_start(att_b)
    keep, other = weight_grads(mlp_grads_kernel, core, dp_size, 15, n1, d_pre, (hidden,), db1)
    keep, other = tie((keep, other), grads[2])
    got = swap(other, 1)
    grads[1] = to_one(gx1, 1)
    dqa, mya, oa, ta = back(tie(d_context, keep), 0)
    dqa, mya, oa, ta, got, mlp_b = tie((dqa, mya, oa, ta, got, mlp_b), grads[1])
    mlp_a = cube_start(keep + got)
    gota = swap(oa, 1)
    mlp_a, given = cube_step(mlp_a, 0)
    dqb, myb, ob, tb = back(tie(d_context, given, oa), 1)
    dqb, myb, ob, tb, gota, mlp_a = hold((dqb, myb, ob, tb, gota, mlp_a), 5)
    gotb = swap(ob, 1)
    mlp_a, given = cube_step(mlp_a, 1)
    gotb = tie(gotb, given)
    d_proj, gx0, vec0 = project_back(info, gx1, x, p0, (dqa, dqb, mya, myb, gota, gotb), qkv_refs)
    d_proj, gx0, vec0, mlp_a = hold((d_proj, gx0, vec0, mlp_a), 3)
    mlp_a, given = cube_step(mlp_a, 2)
    grads[0] = to_one(tie(gx0, given), 0)
    keep, other = weight_grads(att_grads_kernel, core, dp_size, 9, tie(normed, given), d_proj, [part[0] for part in outcome], db0)
    keep, other, att_b, grads[0][1], mlp_a = hold((keep, other, att_b, grads[0][1], mlp_a), 4)
    got = swap(other, 1)
    att_sum = keep + got
    att_a = line_start(att_sum)
    tables = [(ta, tb), tables[1]]
    att_sum, tables, vec0, mlp_b, att_b, outs, mlp_a = hold((att_sum, tables, vec0, mlp_b, att_b, outs, mlp_a), 6)
    vecs[1], vecs[0] = vec1[:3], jnp.concatenate([vec0[:2], vec1[3:4]])
    stack = lambda parts: jnp.stack([parts[s] for s in range(sections)])
    table_all = [jnp.concatenate(tables[layer])[:, :4].reshape(heads, 2, 128)[..., : 2 * SIDE_L + 1] for layer in range(layers)]
    small = jnp.concatenate([stack(vecs).reshape(-1), jnp.stack(table_all).reshape(-1)])
    mlp_a, _ = cube_end(mlp_a)
    mlp_b, att_b = line_end(mlp_b, att_b)
    small = small_sum(small, 0)
    section_out = collected(outs).reshape(1, micro_count, slot_rows, width)
    small, section_out, mlp_b, att_b, mlp_a, grads[0] = together((small, section_out, mlp_b, att_b, mlp_a, grads[0]))
    mlp_a = settled(*mlp_a)
    low, high = jnp.split(mlp_a, 2, axis=0)
    small = small_sum(small, 1)
    ups = [mlp_a, send(mlp_a, [(0, 1)])]
    downs = by_sender(0, low, high, core, (2, 3))
    small, ups, downs, mlp_b, att_b = together((small, ups, downs, mlp_b, att_b))
    small = small_sum(small, 2)
    even = jnp.concatenate([att_b, mlp_b[: att_b.shape[0]]], axis=0)
    own_b = pick(core, even, mlp_b)
    got_b = by_sender(1, even, mlp_b, core, (1, 2, 3))
    grads = tie(grads, own_b)
    in_grads = collected({s: [part.astype(F32) for part in grads[s]] for s in range(sections)}).reshape(1, micro_count, slot_rows, width)
    small, got_b, in_grads, att_a = together((small, got_b, in_grads, att_a))
    got_a = from_pipe(att_a, 0, range(4))

    first_grads, half_grads = {}, {}
    rows_a = [(got_a[c].astype(F32) + got_a[2 + c].astype(F32)).reshape(4, -1, width) for c in range(2)]
    first_grads[0] = jnp.concatenate([jnp.concatenate([v[j] for v in rows_a], axis=0) for j in range(4)], axis=1)
    first_grads[1] = up_result([ups[1], ups[0]])
    half_grads[0] = jnp.concatenate(downs, axis=0)
    half_grads[1] = jnp.concatenate(downs[::-1], axis=0)
    by_bit = [own_b, *got_b]
    on = lambda target: [by_bit[p ^ target] for p in range(sections)]
    piece = att_b.shape[0]
    first_grads[2] = att_result([v[:piece] for v in on(2)])
    half_grads[2] = jnp.concatenate([v[piece:] for v in on(2)[2:]], axis=0)
    first_grads[3] = up_result(on(3)[:2])
    half_grads[3] = jnp.concatenate([v[piece:] for v in on(3)[2:]], axis=0)

    g_first = choose(place, [first_grads[s].astype(F32) for s in range(sections)])[None]
    g_half = choose(place, [half_grads[s].astype(F32) for s in range(sections)])[None]
    vec_size = sections * 3 * width
    vec_all = small[:vec_size].reshape(sections, 3, width)
    g_table = small[vec_size:].reshape(rel_table.shape)
    cols = width // dp_size
    mine = lax.dynamic_slice(vec_all, (place, 0, dp_place * cols), (1, 3, cols))
    return (section_out, in_grads, g_first, g_half, mine[:, 0], mine[:, 1], mine[:, 2], g_table)


def solution(mesh):
    in_specs = (
        P(None, "dp", None),
        P(None, "dp", None),
        P(None, "dp"),
        P("pipe", None),
        P("pipe", None),
        P("pipe", None),
        P("pipe", None, None),
        P("pipe", None, None),
        P(),
    )
    out_specs = (
        P("pipe", None, "dp", None),
        P("pipe", None, "dp", None),
        P("pipe", "dp", None),
        P("pipe", "dp", None),
        P("pipe", "dp"),
        P("pipe", "dp"),
        P("pipe", "dp"),
        P(),
    )
    return jax.shard_map(local, mesh=mesh, in_specs=in_specs, out_specs=out_specs, check_vma=False)
```

```python
from functools import partial

import jax
import jax.numpy as jnp
import numpy as np
from jax import lax
from jax.experimental import pallas as pl
from jax.experimental.pallas import tpu as pltpu
from jax.sharding import PartitionSpec as P

SIDE_L = 32
CELLS = SIDE_L + 1
HEAD = 64
PAIR = 2 * HEAD
PAGES = 8
BLOCK = 40
PAGE_AT = 3 * CELLS
MASKED = 1e30
EPSILON = 1e-06
LOG2E = 1.4426950408889634
LN2 = 0.6931471805599453
BF = jnp.bfloat16
F32 = jnp.float32
NT = (((1,), (1,)), ((), ()))
TN = (((0,), (0,)), ((), ()))


def dot(a, b):
    return jnp.dot(a, b, preferred_element_type=F32)


def dot_nt(a, b):
    return lax.dot_general(a, b, NT, preferred_element_type=F32)


def dot_tn(a, b):
    return lax.dot_general(a, b, TN, preferred_element_type=F32)


def geometry(grid_side, row_ids, slot_rows):
    page_len = grid_side * grid_side + 1
    page_count = slot_rows // page_len
    page_of = jnp.minimum(row_ids // page_len, page_count)
    offset = row_ids - page_of * page_len
    patch_id = jnp.maximum(offset - 1, 0)
    inside = page_of < page_count
    class_row = offset == 0
    coord_y = jnp.where(inside, jnp.where(class_row, SIDE_L, patch_id // grid_side), 0)
    coord_x = jnp.where(inside, jnp.where(class_row, SIDE_L, patch_id % grid_side), 0)
    return page_of, coord_y, coord_x


def row_features(page_of, coord_y, coord_x, flip):
    lane = jnp.arange(128, dtype=jnp.int32)[None, :]
    at = (lambda c: SIDE_L - c) if flip else (lambda c: c)
    hot = (lane == at(coord_y)[:, None]) | (lane == BLOCK + at(coord_x)[:, None])
    hot = hot | (lane == 2 * BLOCK + page_of[:, None])
    return hot.astype(BF)


def key_features(page_of, coord_y, coord_x):
    lane = jnp.arange(256, dtype=jnp.int32)[None, :]
    at_y = SIDE_L - coord_y[:, None]
    at_x = SIDE_L - coord_x[:, None]
    hot = (lane == at_y) | (lane == HEAD + at_y) | (lane == 128 + at_x)
    hot = hot | (lane == 128 + CELLS + at_y) | (lane == 128 + 2 * CELLS + at_x)
    hot = hot | (lane == 128 + PAGE_AT + page_of[:, None])
    return hot.astype(BF)


def table_rows(rel_table):
    layers, heads = rel_table.shape[:2]
    scaled = rel_table * LOG2E
    gap = jnp.zeros((*scaled.shape[:3], 128 - 2 * SIDE_L - 1), F32)
    scaled = jnp.concatenate([scaled[..., SIDE_L:], gap, scaled[..., :SIDE_L]], axis=-1)
    high = scaled.astype(BF).astype(F32)
    return jnp.concatenate([high, scaled - high], axis=2).reshape(layers, heads // 2, 8, 128)


def table_map(table_ref, head):
    row = lax.broadcasted_iota(jnp.int32, (BLOCK, 128), 0)
    lane = lax.broadcasted_iota(jnp.int32, (BLOCK, 128), 1)

    def grid(i, to):
        values = jnp.broadcast_to(table_ref[0, 4 * head + i : 4 * head + i + 1, :], (BLOCK, 128))
        values = pltpu.roll(values, 0, 1, stride=1, stride_axis=0)
        values = jnp.where((row < CELLS) & (lane < CELLS), values, 0.0)
        return pltpu.roll(values, to, 1) if to else values

    none = jnp.zeros((BLOCK, 128), F32)
    far = jnp.where((lane >= PAGE_AT) & (lane < PAGE_AT + PAGES) & (lane - PAGE_AT != row) & (row < PAGES), -MASKED, 0.0)
    left = [grid(0, HEAD if head == 0 else 0), none, none, none[:8]]
    right = [grid(2, CELLS), grid(1, 0) + grid(3, 2 * CELLS), far, none[:8]]
    return jnp.concatenate([jnp.concatenate(left, axis=0), jnp.concatenate(right, axis=0)], axis=1).astype(BF)


def split3(value):
    high = value.astype(BF).astype(F32)
    middle = (value - high).astype(BF).astype(F32)
    return high, middle, value - high - middle


def lanes_of(rows):
    return lax.broadcasted_iota(jnp.int32, (rows, PAIR), 1)


def attn_fwd_kernel(hot_ref, map_ref, q_ref, ko_ref, kp_ref, vo_ref, vp_ref, key_ref,
                    o_ref, rest_ref, inv_ref, w_ref, kx_ref, vx_ref):
    rows = q_ref.shape[0]
    lane = lanes_of(rows)
    for head in range(2):
        mine = (lane < HEAD) if head == 0 else (lane >= HEAD)
        one_at = HEAD if head == 0 else 0
        table = table_map(map_ref, head)
        kx, vx = kx_ref.at[head], vx_ref.at[head]
        kx[:, PAIR:] = key_ref[:, PAIR:]
        for part, (k_ref, v_ref) in enumerate(((ko_ref, vo_ref), (kp_ref, vp_ref))):
            at = pl.ds(part * rows, rows)
            kx[at, :PAIR] = jnp.where(mine, k_ref[...], key_ref[at, :PAIR])
            vx[at, :] = jnp.where(mine, v_ref[...], jnp.where(lane == one_at, 1.0, 0.0).astype(BF))
        feats = dot(hot_ref[...], table).astype(BF)
        query = jnp.concatenate([jnp.where(mine, q_ref[...], feats[:, :PAIR]), feats[:, PAIR:]], axis=1)
        scores = dot_nt(kx[...], query)
        weights = jnp.exp2(scores - jnp.max(scores, axis=0, keepdims=True)).astype(BF)
        w_ref[head] = weights
        mixed = dot_tn(vx[...], weights).T
        inv = 1.0 / mixed[:, one_at : one_at + 1]
        out = mixed * inv
        high = out.astype(BF)
        rest = (out - high.astype(F32)).astype(BF)
        inv = jnp.broadcast_to(inv, out.shape)
        if head == 0:
            o_ref[...], rest_ref[...], inv_ref[...] = high, rest, inv
        else:
            o_ref[...] = jnp.where(mine, high, o_ref[...])
            rest_ref[...] = jnp.where(mine, rest, rest_ref[...])
            inv_ref[...] = jnp.where(mine, inv, inv_ref[...])


def attn_forward(hot, maps, project, partner, keys, first, count):
    rows, width = project.shape[0], project.shape[1] // 3
    pairs = width // PAIR
    col = lambda off: pl.BlockSpec((rows, PAIR), lambda g: (0, off + first + g))
    out = pl.BlockSpec((rows, PAIR), lambda g: (0, g))
    return pl.pallas_call(
        attn_fwd_kernel,
        grid=(count,),
        in_specs=[
            whole((rows, 128)),
            pl.BlockSpec((1, 8, 128), lambda g: (first + g, 0, 0)),
            col(0),
            col(pairs),
            col(0),
            col(2 * pairs),
            col(pairs),
            whole((2 * rows, 256)),
        ],
        out_specs=[out, out, out, pl.BlockSpec((2, 2 * rows, rows), lambda g: (g, 0, 0))],
        out_shape=[
            jax.ShapeDtypeStruct((rows, count * PAIR), BF),
            jax.ShapeDtypeStruct((rows, count * PAIR), BF),
            jax.ShapeDtypeStruct((rows, count * PAIR), F32),
            jax.ShapeDtypeStruct((2 * count, 2 * rows, rows), BF),
        ],
        scratch_shapes=[pltpu.VMEM((2, 2 * rows, 256), BF), pltpu.VMEM((2, 2 * rows, PAIR), BF)],
        compiler_params=params_for(56),
        cost_estimate=cost(26),
        name="attn_fwd",
    )(hot, maps, project, project, partner, project, partner, keys)


def attn_bwd_kernel(hot_ref, w_ref, q_ref, ko_ref, kp_ref, vo_ref, vp_ref, key_ref, do_ref, o_ref, rest_ref, inv_ref,
                    dq_ref, mine_ref, other_ref, gt_ref, kx_ref, vx_ref, ds_ref):
    rows = q_ref.shape[0]
    lane = lanes_of(rows)
    scaled = (do_ref[...].astype(F32) * inv_ref[...]).astype(BF)
    product = scaled.astype(F32) * (o_ref[...].astype(F32) + rest_ref[...].astype(F32))
    for head in range(2):
        mine = (lane < HEAD) if head == 0 else (lane >= HEAD)
        spot = lane - (HEAD if head == 0 else 0)
        kx, vx, ds = kx_ref.at[head], vx_ref.at[head], ds_ref.at[head]
        kx[:, PAIR:] = key_ref[:, PAIR:]
        ones = jnp.where((spot >= 0) & (spot < 3), 1.0, 0.0).astype(BF)
        for part, (k_ref, v_ref) in enumerate(((ko_ref, vo_ref), (kp_ref, vp_ref))):
            at = pl.ds(part * rows, rows)
            kx[at, :PAIR] = jnp.where(mine, k_ref[...], key_ref[at, :PAIR])
            vx[at, :] = jnp.where(mine, v_ref[...], ones)
        delta = jnp.sum(jnp.where(mine, product, 0.0), axis=1, keepdims=True)
        high, middle, low = split3(delta)
        spread = jnp.where(spot == 0, -high, jnp.where(spot == 1, -middle, jnp.where(spot == 2, -low, 0.0)))
        d_out = jnp.where(mine, scaled, spread.astype(BF))
        for part, out_ref in enumerate((mine_ref, other_ref)):
            at = pl.ds(part * rows, rows)
            weights = w_ref[head, at, :]
            d_scores = (weights.astype(F32) * dot_nt(vx[at, :], d_out)).astype(BF)
            ds[at, :] = d_scores
            d_value = dot(weights, scaled).astype(BF)
            d_key = (dot(d_scores, q_ref[...]) * LN2).astype(BF)
            if head == 0:
                out_ref[1], out_ref[0] = d_value, d_key
            else:
                out_ref[1] = jnp.where(mine, d_value, out_ref[1])
                out_ref[0] = jnp.where(mine, d_key, out_ref[0])
        d_query = dot_tn(ds[...], kx[...])
        high_q = d_query.astype(BF)
        low_q = (d_query - high_q.astype(F32)).astype(BF)
        grid = dot_tn(hot_ref[...], high_q) + dot_tn(hot_ref[...], low_q)
        row = lax.broadcasted_iota(jnp.int32, (BLOCK, 128), 0)
        column = lax.broadcasted_iota(jnp.int32, (BLOCK, 128), 1)
        for axis in range(2):
            part = grid[axis * BLOCK : (axis + 1) * BLOCK, axis * 128 : (axis + 1) * 128]
            part = pltpu.roll(part, HEAD, 1) if axis == 0 and head == 0 else part
            part = jnp.where((row < CELLS) & (column < CELLS), part, 0.0)
            along = pltpu.roll(part, 0, 1, stride=1, stride_axis=0)
            gt_ref[0, 2 * head + axis : 2 * head + axis + 1, :] = jnp.sum(along, axis=0, keepdims=True)
        d_query = (d_query[:, :PAIR] * HEAD**-0.5).astype(BF)
        dq_ref[...] = d_query if head == 0 else jnp.where(mine, d_query, dq_ref[...])
    gt_ref[0, 4:8, :] = jnp.zeros((4, 128), F32)


def attn_backward(hot, weights, project, partner, keys, d_context, outcome, first, count):
    rows, width = project.shape[0], project.shape[1] // 3
    pairs = width // PAIR
    col = lambda off: pl.BlockSpec((rows, PAIR), lambda g: (0, off + first + g))
    out = pl.BlockSpec((rows, PAIR), lambda g: (0, g))
    both = pl.BlockSpec((2, rows, PAIR), lambda g: (0, 0, g))
    return pl.pallas_call(
        attn_bwd_kernel,
        grid=(count,),
        in_specs=[
            whole((rows, 128)),
            pl.BlockSpec((2, 2 * rows, rows), lambda g: (g, 0, 0)),
            col(0),
            col(pairs),
            col(0),
            col(2 * pairs),
            col(pairs),
            whole((2 * rows, 256)),
            col(0),
            out,
            out,
            out,
        ],
        out_specs=[out, both, both, pl.BlockSpec((1, 8, 128), lambda g: (g, 0, 0))],
        out_shape=[
            jax.ShapeDtypeStruct((rows, count * PAIR), BF),
            jax.ShapeDtypeStruct((2, rows, count * PAIR), BF),
            jax.ShapeDtypeStruct((2, rows, count * PAIR), BF),
            jax.ShapeDtypeStruct((count, 8, 128), F32),
        ],
        scratch_shapes=[
            pltpu.VMEM((2, 2 * rows, 256), BF),
            pltpu.VMEM((2, 2 * rows, PAIR), BF),
            pltpu.VMEM((2, 2 * rows, rows), BF),
        ],
        compiler_params=params_for(56),
        cost_estimate=cost(6 * count),
        name="attn_bwd",
    )(hot, weights, project, project, partner, project, partner, keys, d_context, *outcome)


def centred(values):
    values = values - jnp.mean(values, axis=-1, keepdims=True)
    inv = lax.rsqrt(jnp.mean(values * values, axis=-1, keepdims=True) + EPSILON)
    return values * inv, inv


def start_first(info_ref, kind, cols, far_cols, refs, dst, sem):
    own, near, far_own, far_other = refs
    local, core = info_ref[0] == 1, info_ref[1]
    part = far_own.shape[0]

    @pl.when(local & (core == kind))
    def _():
        pltpu.make_async_copy(own.at[:, cols], dst, sem).start()

    @pl.when(local & (core != kind))
    def _():
        pltpu.make_async_copy(near.at[:, cols], dst, sem).start()

    @pl.when(jnp.logical_not(local))
    def _():
        if part == dst.shape[0]:
            pltpu.make_async_copy(far_own, dst, sem).start()
            return
        pltpu.make_async_copy(far_own.at[:, far_cols], dst.at[pl.ds(core * part, part)], sem).start()
        pltpu.make_async_copy(far_other.at[:, far_cols], dst.at[pl.ds((1 - core) * part, part)], sem).start()


def start_down(info_ref, refs, dst, sem):
    own, near, far_own, far_other = refs
    local, core = info_ref[0] == 1, info_ref[1]
    part = own.shape[0]
    for here, mine, other in ((local, own, near), (jnp.logical_not(local), far_own, far_other)):

        @pl.when(here)
        def _(mine=mine, other=other):
            pltpu.make_async_copy(mine, dst.at[pl.ds(core * part, part)], sem).start()
            pltpu.make_async_copy(other, dst.at[pl.ds((1 - core) * part, part)], sem).start()


def wait_for(dst, sem):
    pltpu.make_async_copy(dst, dst, sem).wait()


EARLY = True
SMEM = pl.BlockSpec(memory_space=pltpu.SMEM)
ANY = pl.BlockSpec(memory_space=pl.ANY)


def whole(shape):
    return pl.BlockSpec(shape, lambda *g: (0,) * len(shape))


def params_for(mib):
    return pltpu.CompilerParams(vmem_limit_bytes=mib * 2**20)


def cost(us):
    return pl.CostEstimate(flops=int(us * 2e7), bytes_accessed=1000, transcendentals=0)


def project_kernel(info_ref, x_ref, p_ref, own, near, far_own, far_other, normed_ref, out_ref, w_ref, sem):
    width = x_ref.shape[1]
    start_first(info_ref, 0, pl.ds(0, 3 * width), pl.ds(0, 3 * width), (own, near, far_own, far_other), w_ref, sem)
    nhat, _ = centred(x_ref[...].astype(F32))
    normed = (nhat * p_ref[0:1, :] + p_ref[1:2, :]).astype(BF)
    normed_ref[...] = normed
    wait_for(w_ref, sem)
    for j in range(3):
        at = pl.ds(j * width, width)
        value = dot(normed, w_ref[:, at])
        if j == 0:
            value = value * (HEAD**-0.5 * LOG2E)
        out_ref[:, at] = value.astype(BF)


def project(info, x, p, first_refs):
    rows, width = x.shape
    return pl.pallas_call(
        project_kernel,
        in_specs=[SMEM, whole(x.shape), whole(p.shape)] + [ANY] * 4,
        out_specs=[whole((rows, width)), whole((rows, 3 * width))],
        out_shape=[jax.ShapeDtypeStruct((rows, width), BF), jax.ShapeDtypeStruct((rows, 3 * width), BF)],
        scratch_shapes=[pltpu.VMEM((width, 3 * width), BF), pltpu.SemaphoreType.DMA],
        compiler_params=params_for(40),
        cost_estimate=cost(5),
        name="project",
    )(info, x, p, *first_refs)


def block_out_kernel(info_ref, x_ref, ctx_a, ctx_b, p0_ref, p1_ref, *refs):
    att, up, refs = refs[:4], refs[:2] + refs[4:6], refs[6:]
    down, refs = refs[:4], refs[4:]
    b0_ref, x1_ref, n1_ref, slope_ref, hid_ref, b1_ref, x2_ref, mine_ref, other_ref, wo_ref, wu_ref, wd_ref, slopes, hiddens, sems, out_sems = refs
    width = x_ref.shape[1]
    start_first(info_ref, 0, pl.ds(3 * width, width), pl.ds(0, width), att, wo_ref, sems.at[0])
    for j in range(4):
        start_first(info_ref, 1, pl.ds(j * width, width), pl.ds(j * width, width), up, wu_ref.at[j], sems.at[1 + j])
    start_down(info_ref, down, wd_ref, sems.at[5])
    wait_for(wo_ref, sems.at[0])
    half = width // 2
    branch = dot(ctx_a[...], wo_ref[:half]) + dot(ctx_b[...], wo_ref[half:])
    b0_ref[...] = branch.astype(BF)
    x1 = (x_ref[...].astype(F32) + p0_ref[2:3, :] * branch).astype(BF)
    x1_ref[...] = x1
    x1 = x1.astype(F32)
    nhat, _ = centred(x1)
    normed = (nhat * p1_ref[0:1, :] + p1_ref[1:2, :]).astype(BF)
    n1_ref[...] = normed
    for j in range(4):
        wait_for(wu_ref.at[j], sems.at[1 + j])
    wait_for(wd_ref, sems.at[5])
    total = jnp.zeros(x1.shape, F32)
    for j in range(4):
        at = pl.ds(j * width, width)
        v = dot(normed, wu_ref[j])
        square = v * v
        bend = jnp.tanh(v * (0.7978845608028654 + (0.7978845608028654 * 0.044715) * square))
        up_half = 0.5 + 0.5 * bend
        along = v * (2 * 0.7978845608028654 + (6 * 0.7978845608028654 * 0.044715) * square)
        slopes[j] = (up_half + along * (up_half * (1.0 - up_half))).astype(BF)
        hiddens[j] = (v * up_half).astype(BF)
        if EARLY:
            pltpu.make_async_copy(slopes.at[j], slope_ref.at[:, at], out_sems.at[0, j]).start()
            pltpu.make_async_copy(hiddens.at[j], hid_ref.at[:, at], out_sems.at[1, j]).start()
        total = total + dot(hiddens[j], wd_ref[at, :])
    b1_ref[...] = total.astype(BF)
    x2 = (x1 + p1_ref[2:3, :] * total).astype(BF)
    x2_ref[...] = x2
    first = info_ref[1] == 0
    mine_ref[...] = jnp.where(first, x1_ref[...], x2)
    other_ref[...] = jnp.where(first, x2, x1_ref[...])
    if not EARLY:
        for j in range(4):
            at = pl.ds(j * width, width)
            pltpu.make_async_copy(slopes.at[j], slope_ref.at[:, at], out_sems.at[0, j]).start()
            pltpu.make_async_copy(hiddens.at[j], hid_ref.at[:, at], out_sems.at[1, j]).start()
    for j in range(4):
        wait_for(slopes.at[j], out_sems.at[0, j])
        wait_for(hiddens.at[j], out_sems.at[1, j])


def block_out(info, x, context, p0, p1, more_refs, up_refs, down_refs):
    rows, width = x.shape
    one = whole((rows, width))
    shape = lambda n: jax.ShapeDtypeStruct((rows, n), BF)
    widths = [width, width, width, 4 * width, 4 * width, width, width, width, width]
    refs = (*more_refs, *up_refs[2:], *down_refs)
    return pl.pallas_call(
        block_out_kernel,
        grid=(1,),
        in_specs=[SMEM, one, *[whole(c.shape) for c in context], whole(p0.shape), whole(p1.shape)] + [ANY] * len(refs),
        out_specs=[one if n == width else ANY for n in widths],
        out_shape=[shape(n) for n in widths],
        scratch_shapes=[
            pltpu.VMEM((width, width), BF),
            pltpu.VMEM((4, width, width), BF),
            pltpu.VMEM((4 * width, width), BF),
            pltpu.VMEM((4, rows, width), BF),
            pltpu.VMEM((4, rows, width), BF),
            pltpu.SemaphoreType.DMA((6,)),
            pltpu.SemaphoreType.DMA((2, 4)),
        ],
        compiler_params=params_for(58),
        cost_estimate=cost(12),
        name="block_out",
    )(info, x, *context, p0, p1, *refs)


def norm_back(x, gain, d_normed, gy):
    nhat, inv = centred(x)
    inner = d_normed * gain
    shift = jnp.mean(inner, axis=-1, keepdims=True)
    along = jnp.mean(inner * nhat, axis=-1, keepdims=True)
    total = lambda v: jnp.sum(v, axis=0, keepdims=True)
    return gy + inv * (inner - shift - nhat * along), total(nhat * d_normed), total(d_normed)


def block_back_kernel(info_ref, gy_ref, x1_ref, slope_ref, b1_ref, b0_ref, p0_ref, p1_ref, *refs):
    att, up, refs = refs[:4], refs[:2] + refs[4:6], refs[6:]
    down, refs = refs[:4], refs[4:]
    db1_ref, dpre_ref, gx_ref, db0_ref, dctx_ref, vec_ref, wo_ref, wu_ref, wd_ref, slopes, given, sems, more_sems = refs
    width = gy_ref.shape[1]
    start_down(info_ref, down, wd_ref, sems.at[5])
    for j in range(4):
        at = pl.ds(j * width, width)
        start_first(info_ref, 1, at, at, up, wu_ref.at[j], sems.at[1 + j])
        pltpu.make_async_copy(slope_ref.at[:, at], slopes.at[j], more_sems.at[0, j]).start()
    start_first(info_ref, 0, pl.ds(3 * width, width), pl.ds(0, width), att, wo_ref, sems.at[0])
    total = lambda v: jnp.sum(v, axis=0, keepdims=True)
    gy = gy_ref[...].astype(F32)
    d_branch = (gy * p1_ref[2:3, :]).astype(BF)
    db1_ref[...] = d_branch
    vec_ref[2:3, :] = total(b1_ref[...].astype(F32) * gy)
    vec_ref[4:, :] = jnp.zeros((4, width), F32)
    d_normed = jnp.zeros(gy.shape, F32)
    wait_for(wd_ref, sems.at[5])
    for j in range(4):
        wait_for(slopes.at[j], more_sems.at[0, j])
        wait_for(wu_ref.at[j], sems.at[1 + j])
    for j in range(4):
        at = pl.ds(j * width, width)
        d_hidden = dot_nt(d_branch, wd_ref[at, :])
        given[j] = (d_hidden * slopes[j].astype(F32)).astype(BF)
        if EARLY:
            pltpu.make_async_copy(given.at[j], dpre_ref.at[:, at], more_sems.at[1, j]).start()
        d_normed = d_normed + dot_nt(given[j], wu_ref[j])
    if not EARLY:
        for j in range(4):
            pltpu.make_async_copy(given.at[j], dpre_ref.at[:, pl.ds(j * width, width)], more_sems.at[1, j]).start()
    gx, g_gain, g_shift = norm_back(x1_ref[...].astype(F32), p1_ref[0:1, :], d_normed, gy)
    vec_ref[0:1, :] = g_gain
    vec_ref[1:2, :] = g_shift
    gx = gx.astype(BF)
    gx_ref[...] = gx
    gx = gx.astype(F32)
    d_att = (gx * p0_ref[2:3, :]).astype(BF)
    db0_ref[...] = d_att
    vec_ref[3:4, :] = total(b0_ref[...].astype(F32) * gx)
    wait_for(wo_ref, sems.at[0])
    dctx_ref[...] = dot_nt(d_att, wo_ref[...]).astype(BF)
    for j in range(4):
        wait_for(given.at[j], more_sems.at[1, j])


def block_back(info, gy, x1, slope, b1, b0, p0, p1, more_refs, up_refs, down_refs):
    rows, width = gy.shape
    one = whole((rows, width))
    shape = lambda n: jax.ShapeDtypeStruct((rows, n), BF)
    widths = [width, 4 * width, width, width, width]
    refs = (*more_refs, *up_refs[2:], *down_refs)
    return pl.pallas_call(
        block_back_kernel,
        grid=(1,),
        in_specs=[SMEM, one, one, ANY, one, one, whole(p0.shape), whole(p1.shape)] + [ANY] * len(refs),
        out_specs=[one if n == width else ANY for n in widths] + [whole((8, width))],
        out_shape=[shape(n) for n in widths] + [jax.ShapeDtypeStruct((8, width), F32)],
        scratch_shapes=[
            pltpu.VMEM((width, width), BF),
            pltpu.VMEM((4, width, width), BF),
            pltpu.VMEM((4 * width, width), BF),
            pltpu.VMEM((4, rows, width), BF),
            pltpu.VMEM((4, rows, width), BF),
            pltpu.SemaphoreType.DMA((6,)),
            pltpu.SemaphoreType.DMA((2, 4)),
        ],
        compiler_params=params_for(58),
        cost_estimate=cost(14),
        name="block_back",
    )(info, gy, x1, slope, b1, b0, p0, p1, *refs)


def project_back_kernel(info_ref, gy_ref, x_ref, p_ref, dqa, dqb, mya, myb, gota, gotb, own, near, far_own, far_other,
                        dproj_ref, gx_ref, vec_ref, w_ref, sem):
    width = x_ref.shape[1]
    start_first(info_ref, 0, pl.ds(0, 3 * width), pl.ds(0, 3 * width), (own, near, far_own, far_other), w_ref, sem)
    half = width // 2
    for i, (dq, my, got) in enumerate(((dqa, mya, gota), (dqb, myb, gotb))):
        dproj_ref[:, i * half : (i + 1) * half] = dq[...]
        for j in range(2):
            at = pl.ds((1 + j) * width + i * half, half)
            dproj_ref[:, at] = (my[j].astype(F32) + got[j].astype(F32)).astype(BF)
    wait_for(w_ref, sem)
    d_normed = dot_nt(dproj_ref[:, :width], w_ref[:, :width])
    for j in (1, 2):
        at = pl.ds(j * width, width)
        d_normed = d_normed + dot_nt(dproj_ref[:, at], w_ref[:, at])
    gx, g_gain, g_shift = norm_back(x_ref[...].astype(F32), p_ref[0:1, :], d_normed, gy_ref[...].astype(F32))
    gx_ref[...] = gx.astype(BF)
    vec_ref[0:1, :] = g_gain
    vec_ref[1:2, :] = g_shift
    vec_ref[2:, :] = jnp.zeros((6, width), F32)


def project_back(info, gy, x, p, parts, first_refs):
    rows, width = x.shape
    one = whole((rows, width))
    return pl.pallas_call(
        project_back_kernel,
        in_specs=[SMEM, one, one, whole(p.shape)] + [whole(v.shape) for v in parts] + [ANY] * 4,
        out_specs=[whole((rows, 3 * width)), one, whole((8, width))],
        out_shape=[
            jax.ShapeDtypeStruct((rows, 3 * width), BF),
            jax.ShapeDtypeStruct((rows, width), BF),
            jax.ShapeDtypeStruct((8, width), F32),
        ],
        grid=(1,),
        scratch_shapes=[pltpu.VMEM((width, 3 * width), BF), pltpu.SemaphoreType.DMA],
        compiler_params=params_for(48),
        cost_estimate=cost(7),
        name="project_back",
    )(info, gy, x, p, *parts, *first_refs)


def gather_kernel(info_ref, mine, by_x, by_z, diag_x, diag_z, out_ref, sem):
    quarter = mine.shape[0]
    part = quarter // 2
    q = info_ref[0]
    at = lambda i: pl.multiple_of(i * quarter, part)
    pltpu.make_async_copy(mine, out_ref.at[pl.ds(at(q), quarter)], sem).start()
    pltpu.make_async_copy(by_x, out_ref.at[pl.ds(at(info_ref[1]), quarter)], sem).start()
    pltpu.make_async_copy(by_z, out_ref.at[pl.ds(at(info_ref[2]), quarter)], sem).start()
    pltpu.make_async_copy(diag_x, out_ref.at[pl.ds(at(info_ref[3]), part)], sem).start()
    pltpu.make_async_copy(diag_z, out_ref.at[pl.ds(at(info_ref[3]) + part, part)], sem).start()
    wait_for(out_ref, sem)


def dp_swap(value, bit):
    return lax.ppermute(value, "dp", [(i, i ^ bit) for i in range(lax.axis_size("dp"))])


def tie(value, *deps):
    return lax.optimization_barrier((value, deps))[0]


def hold(values, count):
    state = values[-1]
    if not isinstance(state, list):
        return lax.optimization_barrier(values)
    arrays = [part[:2] for part in state]
    *values, arrays = lax.optimization_barrier((*values[:count], arrays))
    return (*values, [(*part, names) for part, (_, _, names) in zip(arrays, state)])


def together(values):
    return lax.optimization_barrier(values)


def quad_start(mine):
    return mine, dp_swap(mine, 1), dp_swap(mine, 2)


def quad_end(mine, by_x, by_z):
    part = mine.shape[0] // 2
    return mine, by_x, by_z, dp_swap(by_z[:part], 1), dp_swap(by_x[part:], 2)


def quad_place(mine, *others):
    quarter = mine.shape[0]
    q = lax.axis_index("dp") % 4
    spots = jnp.stack([q, q ^ 1, q ^ 2, q ^ 3]).astype(jnp.int32)
    return pl.pallas_call(
        gather_kernel,
        in_specs=[SMEM] + [ANY] * 5,
        out_specs=whole((4 * quarter, *mine.shape[1:])),
        out_shape=jax.ShapeDtypeStruct((4 * quarter, *mine.shape[1:]), mine.dtype),
        scratch_shapes=[pltpu.SemaphoreType.DMA],
        compiler_params=params_for(16),
        cost_estimate=cost(3),
        name="assemble",
    )(spots, mine, *others)


def put_rows(values, slot, tmp_ref, keep_ref, send_ref, core, for_d, at, sems):
    tmp = tmp_ref.at[slot].reshape(values.shape)
    tmp[...] = values
    pltpu.make_async_copy(tmp.at[:, core], keep_ref.at[for_d, at], sems.at[slot, 0]).start()
    pltpu.make_async_copy(tmp.at[:, 1 - core], send_ref.at[for_d, at], sems.at[slot, 1]).start()


def mlp_grads_kernel(core_ref, n_ref, pre_ref, hid_ref, db_ref, keep_ref, send_ref, tmp_ref, sems):
    core, j = core_ref[0], pl.program_id(0)
    width = n_ref.shape[1]
    size = keep_ref.shape[0]
    short, long = width // (2 * size), 2 * width // (2 * size)

    def finish(slot, long_rows):
        for i, ref in enumerate((keep_ref, send_ref)):
            to = ref.at[pl.ds(0, size // 2), pl.ds(0, long)] if long_rows else ref.at[:, pl.ds(0, short)]
            pltpu.make_async_copy(to, to, sems.at[slot, i]).wait()

    @pl.when(j > 0)
    def _():
        finish(0, False)
    up = dot_tn(n_ref[...], pre_ref[...]).astype(BF).reshape(size, 2, short, width)
    put_rows(up, 0, tmp_ref, keep_ref, send_ref, core, pl.ds(0, size), pl.ds(j * short, short), sems)

    @pl.when(j > 0)
    def _():
        finish(1, True)
    down = dot_tn(hid_ref[...], db_ref[...]).astype(BF).reshape(size // 2, 2, long, width)
    at = pl.ds(4 * short + (j // 2) * long, long)
    put_rows(down, 1, tmp_ref, keep_ref, send_ref, core, pl.ds((j % 2) * (size // 2), size // 2), at, sems)

    @pl.when(j == pl.num_programs(0) - 1)
    def _():
        finish(0, False)
        finish(1, True)


def att_grads_kernel(core_ref, n_ref, dproj_ref, ctx_a, ctx_b, db_ref, keep_ref, send_ref, tmp_ref, sems):
    core, j = core_ref[0], pl.program_id(0)
    width = n_ref.shape[1]
    size = keep_ref.shape[0]
    short = width // (2 * size)
    slot = lax.rem(j, 2)
    tmp = tmp_ref.at[slot].reshape(size, 2, short, width)

    def finish(at):
        for i, ref in enumerate((keep_ref, send_ref)):
            to = ref.at[:, pl.ds(0, short)]
            pltpu.make_async_copy(to, to, sems.at[at, i]).wait()

    @pl.when(j > 1)
    def _():
        finish(slot)

    @pl.when(j < 3)
    def _():
        tmp[...] = dot_tn(n_ref[...], dproj_ref[...]).astype(BF).reshape(tmp.shape)

    @pl.when(j == 3)
    def _():
        for i, ctx_ref in enumerate((ctx_a, ctx_b)):
            grad = dot_tn(ctx_ref[...], db_ref[...]).astype(BF)
            tmp[pl.ds(i * (size // 2), size // 2)] = grad.reshape(size // 2, 2, short, width)

    at = pl.ds(j * short, short)
    pltpu.make_async_copy(tmp.at[:, core], keep_ref.at[:, at], sems.at[slot, 0]).start()
    pltpu.make_async_copy(tmp.at[:, 1 - core], send_ref.at[:, at], sems.at[slot, 1]).start()

    @pl.when(j == 3)
    def _():
        finish(0)
        finish(1)


def plain_grads(att, core, shape, a, b, c, d):
    size, _, width = shape
    cut = lambda grad: [grad[:, j * width : (j + 1) * width].reshape(size, 2, -1, width) for j in range(grad.shape[1] // width)]
    parts = cut(dot_tn(a, b).astype(BF))
    if att:
        parts += cut(dot_tn(c, d).astype(BF))
    else:
        parts += [half.reshape(size, 2, -1, width) for half in jnp.split(dot_tn(c, d).astype(BF), 2, axis=0)]
    both = jnp.concatenate(parts, axis=2)
    at = lambda i: lax.dynamic_index_in_dim(both, i, 1, keepdims=False)
    return at(core), at(1 - core)


def weight_grads(kernel, core, size, us, a, b, c, d):
    rows, width = a.shape
    att = kernel is att_grads_kernel
    shape = (size, (2 * width if att else 4 * width) // size, width)
    if width // (2 * size) % 16:
        return plain_grads(att, core, shape, a, b, jnp.concatenate(c, axis=1), d)
    col = pl.BlockSpec((rows, width), lambda j: (0, jnp.minimum(j, 2 if att else 3)))
    return pl.pallas_call(
        kernel,
        grid=(4,),
        in_specs=[SMEM, whole(a.shape), col, *([whole(v.shape) for v in c] if att else [col]), whole(d.shape)],
        out_specs=[ANY] * 2,
        out_shape=[jax.ShapeDtypeStruct(shape, BF)] * 2,
        scratch_shapes=[pltpu.VMEM((2, width, width), BF), pltpu.SemaphoreType.DMA((2, 2))],
        compiler_params=params_for(48),
        cost_estimate=cost(us),
        name=kernel.__name__[:-7],
    )(core.astype(jnp.int32).reshape(1), a, b, *c, d)


def send(value, pairs):
    return lax.ppermute(value, "pipe", pairs)


def swap(value, bit):
    return send(value, [(i, i ^ bit) for i in range(lax.axis_size("pipe"))])


def to_target(value, target, bit):
    return send(value, [(target ^ bit, target)])


def pick(core, mine_first, mine_second):
    return jnp.where(core == 0, mine_first, mine_second)


ORDERS = (("x", "y", "z2", "z4"), ("y", "z2", "x", "z4"), ("z2", "x", "y", "z4"))
AT = {"x": ("dp", 1), "z2": ("dp", 2), "z4": ("dp", 4), "y": ("pipe", 2)}


def cube_start(parts):
    size, rows, width = parts.shape
    if size != 8:
        return parts
    parts = parts.reshape(2, 2, 2, 2, rows // 2, width)
    share = width // len(ORDERS)
    return [(parts[..., i * share : (i + 1) * share], None, ["z4", "z2", "x", "y"]) for i in range(len(ORDERS))]


def settled(part, got):
    return part if got is None else part + got


def halve(part, names, axis):
    name, bit = AT[axis]
    i = names.index(axis)
    me = (lax.axis_index(name) // bit) % 2
    at = lambda j: lax.dynamic_index_in_dim(part, j, i, keepdims=False)
    give = at(1 - me)
    got = lax.ppermute(give, name, [(k, k ^ bit) for k in range(lax.axis_size(name))])
    return at(me), got, [n for n in names if n != axis], give


def cube_step(state, step):
    if not isinstance(state, list):
        return state, state
    done = [halve(settled(part, got), names, order[step]) for (part, got, names), order in zip(state, ORDERS)]
    return [d[:3] for d in done], [d[3] for d in done]


def cube_end(state):
    if not isinstance(state, list):
        plane = lax.axis_index("pipe") // 2
        parts = state.reshape(state.shape[0], 2, -1, state.shape[2])
        at = lambda i: lax.dynamic_index_in_dim(parts, i, 1, keepdims=False)
        return (lax.psum_scatter(at(plane) + swap(at(1 - plane), 2), "dp", scatter_dimension=0), None), state
    whole_part = jnp.concatenate([settled(part, got) for part, got, _ in state], axis=-1)
    mine, got, _, give = halve(whole_part, ["z4"], "z4")
    return (mine, got), give


def line_start(parts):
    return lax.psum_scatter(parts, "dp", scatter_dimension=0)


def line_end(mlp, att):
    plane = lax.axis_index("pipe") // 2
    cut = lambda v, i: lax.dynamic_index_in_dim(v.reshape(2, -1, v.shape[1]), i, 0, keepdims=False)
    got = swap(jnp.concatenate([cut(mlp, 1 - plane), cut(att, 1 - plane)], axis=0), 2)
    rows = mlp.shape[0] // 2
    return cut(mlp, plane) + got[:rows], cut(att, plane) + got[rows:]


def by_sender(layer, even, odd, core, bits):
    targets = (2 * layer, 2 * layer + 1)
    mine, other = pick(core, even, odd), pick(core, odd, even)
    return [send(mine if bit == 2 else other, [(t ^ bit, t) for t in targets]) for bit in bits]


def from_pipe(value, target, sources):
    return [value if i == target else send(value, [(i, target)]) for i in sources]


def att_result(got):
    rows = got[0].shape[0] // 2
    cols = []
    for j in range(4):
        cols.append(jnp.concatenate([got[(j // 2) * 2 + c][(j % 2) * rows : (j % 2 + 1) * rows] for c in range(2)], axis=0))
    return jnp.concatenate(cols, axis=1)


def up_result(up):
    rows = up[0].shape[0] // 4
    return jnp.concatenate([jnp.concatenate([v[j * rows : (j + 1) * rows] for v in up], axis=0) for j in range(4)], axis=1)


def choose(place, options):
    result = options[-1]
    for s in range(len(options) - 2, -1, -1):
        result = jnp.where(place == s, options[s], result)
    return result


def small_sum(value, step):
    if lax.axis_size("dp") != 8:
        return lax.psum(value, ("dp", "pipe")) if step == 0 else value
    if step == 2:
        return value + dp_swap(value, 4)
    move = swap if step == 0 else dp_swap
    return (value + move(value, 1)) + (move(value, 2) + move(value, 3))


def local(
    inputs, out_grad, page_side, norm_gain, norm_shift, layer_scale, w_first, w_half, rel_table
):
    place = lax.axis_index("pipe")
    sections = lax.axis_size("pipe")
    dp_size, dp_place = lax.axis_size("dp"), lax.axis_index("dp")
    micro_count, slot_rows, width = inputs.shape
    halves = sections // micro_count
    assert halves == 2 and sections == 4
    rows = slot_rows // halves
    plane, core = place // 2, place % 2
    layers, heads = rel_table.shape[:2]

    own_params = jnp.stack([norm_gain[0], norm_shift[0], layer_scale[0]])
    seen = [own_params] + [swap(own_params, bit) for bit in (1, 2, 3)]
    params = [choose(place, [seen[s ^ p] for p in range(sections)]) for s in range(sections)]

    own_first, own_half = w_first[0], w_half[0]
    count = own_first.shape[0] // 2
    quarter = count // 4
    q = dp_place % 4
    infos = [jnp.stack([(plane == layer).astype(jnp.int32), core.astype(jnp.int32)]) for layer in range(layers)]

    micro, half = plane, core
    side = lax.dynamic_index_in_dim(page_side, micro, 0, keepdims=False)[0]
    own_rows = lambda x: lax.dynamic_slice(x, (micro, half * rows, 0), (1, rows, width))[0]
    key_ids = (jnp.arange(slot_rows, dtype=jnp.int32) + half * rows) % slot_rows
    layout = geometry(side, key_ids, slot_rows)
    own_layout = [c[:rows] for c in layout]
    hot, hot_back = row_features(*own_layout, True), row_features(*own_layout, False)
    keys = key_features(*layout)
    maps = table_rows(rel_table)

    current = own_rows(inputs)
    qkv = own_first[:, : 3 * width]
    far_qkv = (send(qkv[:count], [(0, 2), (2, 0)]), send(qkv[count:], [(0, 3), (2, 1)]))
    share = [lax.dynamic_slice_in_dim(own_first, c * count + q * quarter, quarter, 0) for c in range(2)]
    half_rows = own_half.shape[0] // 4
    share_half = lax.dynamic_slice_in_dim(own_half, q * half_rows, half_rows, 0)
    own_out = own_first[:, 3 * width :]
    last_grad = own_rows(out_grad)
    ready = (far_qkv, params, infos, current, last_grad, hot, hot_back, keys, maps, share, share_half, own_out)
    far_qkv, params, infos, current, last_grad, hot, hot_back, keys, maps, share, share_half, own_out = together(ready)
    far_qkv = pick(core, *far_qkv)
    qkv_refs = (own_first, swap(own_first, 1), far_qkv, swap(far_qkv, 1))
    mine_up = (send(share[0], [(1, 2), (3, 0)]), send(share[1], [(1, 3), (3, 1)]))
    mine_half = swap(share_half, 2)

    def shared(mine, other, layer):
        inside = [(2 * layer, 2 * layer + 1), (2 * layer + 1, 2 * layer)]
        straight = [(p ^ 2, p) for p in (2 * layer, 2 * layer + 1)]
        across = [(p ^ 3, p) for p in (2 * layer, 2 * layer + 1)]
        return [mine, send(other, inside), send(mine, straight), send(other, across)]

    def to_one(value, s):
        return [value] + [to_target(value, s, bit) for bit in (1, 2, 3)]

    def collected(parts):
        return choose(place, [jnp.stack([parts[s][i ^ s] for i in range(sections)]) for s in range(sections)])

    kept, outs = [], {}
    cut = heads // 4
    for layer in range(layers):
        p0, p1, info = params[2 * layer], params[2 * layer + 1], infos[layer]
        normed, proj = project(info, current, p0, qkv_refs)
        if layer == 0:
            own_out = tie(own_out, normed)
        partner = swap(proj[:, width:], 1)
        front = lambda keys, i: attn_forward(hot, maps[layer], proj, partner, keys, i * cut, cut)
        if layer == 0:
            partner, own_out, mine_up = together((partner, own_out, mine_up))
            some_up = quad_start(pick(core, *mine_up))
            far_out = send(own_out, [(0, 2), (2, 0)])
        part_a = front(keys, 0)
        if layer == 0:
            part_a, some_up, mine_half = together((part_a, some_up, mine_half))
            some_half = quad_start(mine_half)
            all_up = quad_end(*some_up)
        part_b = front(tie(keys, part_a[0]), 1)
        if layer == 0:
            part_b, all_up, some_half, far_out = together((part_b, all_up, some_half, far_out))
            near_out, all_half = swap(far_out, 1), quad_end(*some_half)
            far_up, far_half = quad_place(*all_up), quad_place(*all_half)
            far_out = pick(core, far_out, near_out)
            near_half = swap(tie(own_half, far_qkv), 1)
            more_refs = (qkv_refs[0], qkv_refs[1], far_out, far_out)
            up_refs = (qkv_refs[0], qkv_refs[1], far_up, swap(far_up, 1))
            down_refs = (own_half, near_half, far_half, swap(far_half, 1))
        else:
            part_b = tie(part_b, outs[0][2])
        context = (part_a[0], part_b[0])
        b0, x1, n1, slope, hidden, b1, x2, mine, other = block_out(info, current, context, p0, p1, more_refs, up_refs, down_refs)
        if layer == 1:
            b0, x1, n1, slope, hidden, b1, x2, mine, other = tie((b0, x1, n1, slope, hidden, b1, x2, mine, other), outs[0])
        kept.append((current, normed, proj, partner, (part_a, part_b), b0, x1, n1, slope, hidden, b1))
        outs[2 * layer] = outs[2 * layer + 1] = shared(mine, other, layer)
        current = x2

    tables, vecs, grads = {}, {}, {}
    core_id = core.astype(jnp.int32)

    x, normed, proj, partner, outcome, b0, x1, n1, slope, hidden, b1 = kept[1]
    p0, p1, info = params[2], params[3], infos[1]
    grad = tie(last_grad, current)
    db1, d_pre, gx1, db0, d_context, vec1 = block_back(info, grad, x1, slope, b1, b0, p0, p1, more_refs, up_refs, down_refs)
    db1, d_pre, gx1, db0, d_context, vec1 = tie((db1, d_pre, gx1, db0, d_context, vec1), outs[2][2])
    keep, other = weight_grads(mlp_grads_kernel, core, dp_size, 15, n1, d_pre, (hidden,), db1)
    keep, other = tie((keep, other), outs[2])
    got = swap(other, 1)
    back = lambda d_ctx, i: attn_backward(hot_back, outcome[i][3], proj, partner, keys, d_ctx, outcome[i][:3], i * cut, cut)
    dqa, mya, oa, ta = back(tie(d_context, keep), 0)
    dqa, mya, oa, ta, got = together((dqa, mya, oa, ta, got))
    mlp_b = keep + got
    gota = swap(oa, 1)
    dqb, myb, ob, tb = back(tie(d_context, mlp_b, oa), 1)
    dqb, myb, ob, tb, gota = together((dqb, myb, ob, tb, gota))
    gotb = swap(ob, 1)
    mlp_b = line_start(mlp_b)
    d_proj, gx0, vec0 = project_back(info, gx1, x, p0, (dqa, dqb, mya, myb, gota, gotb), qkv_refs)
    keep, other = weight_grads(att_grads_kernel, core, dp_size, 9, normed, d_proj, [part[0] for part in outcome], db0)
    got = swap(other, 1)
    grads[2] = grads[3] = shared(pick(core, gx0, gx1), pick(core, gx1, gx0), 1)
    tables[1] = (ta, tb)
    vecs[3], vecs[2] = vec1[:3], jnp.concatenate([vec0[:2], vec1[3:4]])

    x, normed, proj, partner, outcome, b0, x1, n1, slope, hidden, b1 = kept[0]
    p0, p1, info = params[0], params[1], infos[0]
    db1, d_pre, gx1, db0, d_context, vec1 = block_back(info, tie(gx0, keep), x1, slope, b1, b0, p0, p1, more_refs, up_refs, down_refs)
    db1, d_pre, gx1, db0, d_context, vec1, got = tie((db1, d_pre, gx1, db0, d_context, vec1, got), grads[2][2])
    att_b = keep + got
    d_pre = tie(d_pre, att_b)
    att_b = line_start(att_b)
    keep, other = weight_grads(mlp_grads_kernel, core, dp_size, 15, n1, d_pre, (hidden,), db1)
    keep, other = tie((keep, other), grads[2])
    got = swap(other, 1)
    grads[1] = to_one(gx1, 1)
    dqa, mya, oa, ta = back(tie(d_context, keep), 0)
    dqa, mya, oa, ta, got, mlp_b = tie((dqa, mya, oa, ta, got, mlp_b), grads[1])
    mlp_a = cube_start(keep + got)
    gota = swap(oa, 1)
    mlp_a, given = cube_step(mlp_a, 0)
    dqb, myb, ob, tb = back(tie(d_context, given, oa), 1)
    dqb, myb, ob, tb, gota, mlp_a = hold((dqb, myb, ob, tb, gota, mlp_a), 5)
    gotb = swap(ob, 1)
    mlp_a, given = cube_step(mlp_a, 1)
    gotb = tie(gotb, given)
    d_proj, gx0, vec0 = project_back(info, gx1, x, p0, (dqa, dqb, mya, myb, gota, gotb), qkv_refs)
    d_proj, gx0, vec0, mlp_a = hold((d_proj, gx0, vec0, mlp_a), 3)
    grads[0] = to_one(gx0, 0)
    keep, other = weight_grads(att_grads_kernel, core, dp_size, 9, normed, d_proj, [part[0] for part in outcome], db0)
    keep, other, att_b, grads[0][1] = together((keep, other, att_b, grads[0][1]))
    got = swap(other, 1)
    att_sum = keep + got
    att_a = line_start(att_sum)
    tables = [(ta, tb), tables[1]]
    att_sum, tables, vec0, mlp_b, att_b, outs, mlp_a = hold((att_sum, tables, vec0, mlp_b, att_b, outs, mlp_a), 6)
    vecs[1], vecs[0] = vec1[:3], jnp.concatenate([vec0[:2], vec1[3:4]])
    stack = lambda parts: jnp.stack([parts[s] for s in range(sections)])
    table_all = [jnp.concatenate(tables[layer])[:, :4].reshape(heads, 2, 128)[..., : 2 * SIDE_L + 1] for layer in range(layers)]
    small = jnp.concatenate([stack(vecs).reshape(-1), jnp.stack(table_all).reshape(-1)])
    mlp_a, _ = cube_step(mlp_a, 2)
    mlp_b, att_b = line_end(mlp_b, att_b)
    section_out = collected(outs).reshape(1, micro_count, slot_rows, width)
    small, section_out, mlp_b, att_b, grads[0], mlp_a = hold((small, section_out, mlp_b, att_b, grads[0], mlp_a), 5)
    mlp_a, _ = cube_end(mlp_a)
    small = small_sum(small, 0)
    even = jnp.concatenate([att_b, mlp_b[: att_b.shape[0]]], axis=0)
    own_b = pick(core, even, mlp_b)
    got_b = by_sender(1, even, mlp_b, core, (1, 2, 3))
    small, got_b, own_b, mlp_a = together((small, got_b, own_b, mlp_a))
    mlp_a = settled(*mlp_a)
    low, high = jnp.split(mlp_a, 2, axis=0)
    small = small_sum(small, 1)
    ups = [mlp_a, send(mlp_a, [(0, 1)])]
    downs = by_sender(0, low, high, core, (2, 3))
    grads = tie(grads, own_b)
    in_grads = collected({s: [part.astype(F32) for part in grads[s]] for s in range(sections)}).reshape(1, micro_count, slot_rows, width)
    small, ups, downs, in_grads, att_a = together((small, ups, downs, in_grads, att_a))
    small = small_sum(small, 2)
    got_a = from_pipe(att_a, 0, range(4))

    first_grads, half_grads = {}, {}
    rows_a = [(got_a[c].astype(F32) + got_a[2 + c].astype(F32)).reshape(4, -1, width) for c in range(2)]
    first_grads[0] = jnp.concatenate([jnp.concatenate([v[j] for v in rows_a], axis=0) for j in range(4)], axis=1)
    first_grads[1] = up_result([ups[1], ups[0]])
    half_grads[0] = jnp.concatenate(downs, axis=0)
    half_grads[1] = jnp.concatenate(downs[::-1], axis=0)
    by_bit = [own_b, *got_b]
    on = lambda target: [by_bit[p ^ target] for p in range(sections)]
    piece = att_b.shape[0]
    first_grads[2] = att_result([v[:piece] for v in on(2)])
    half_grads[2] = jnp.concatenate([v[piece:] for v in on(2)[2:]], axis=0)
    first_grads[3] = up_result(on(3)[:2])
    half_grads[3] = jnp.concatenate([v[piece:] for v in on(3)[2:]], axis=0)

    g_first = choose(place, [first_grads[s].astype(F32) for s in range(sections)])[None]
    g_half = choose(place, [half_grads[s].astype(F32) for s in range(sections)])[None]
    vec_size = sections * 3 * width
    vec_all = small[:vec_size].reshape(sections, 3, width)
    g_table = small[vec_size:].reshape(rel_table.shape)
    cols = width // dp_size
    mine = lax.dynamic_slice(vec_all, (place, 0, dp_place * cols), (1, 3, cols))
    return (section_out, in_grads, g_first, g_half, mine[:, 0], mine[:, 1], mine[:, 2], g_table)


def solution(mesh):
    in_specs = (
        P(None, "dp", None),
        P(None, "dp", None),
        P(None, "dp"),
        P("pipe", None),
        P("pipe", None),
        P("pipe", None),
        P("pipe", None, None),
        P("pipe", None, None),
        P(),
    )
    out_specs = (
        P("pipe", None, "dp", None),
        P("pipe", None, "dp", None),
        P("pipe", "dp", None),
        P("pipe", "dp", None),
        P("pipe", "dp"),
        P("pipe", "dp"),
        P("pipe", "dp"),
        P(),
    )
    return jax.shard_map(local, mesh=mesh, in_specs=in_specs, out_specs=out_specs, check_vma=False)
```

```python
from functools import partial

import jax
import jax.numpy as jnp
import numpy as np
from jax import lax
from jax.experimental import pallas as pl
from jax.experimental.pallas import tpu as pltpu
from jax.sharding import PartitionSpec as P

SIDE_L = 32
CELLS = SIDE_L + 1
HEAD = 64
PAIR = 2 * HEAD
PAGES = 8
BLOCK = 40
PAGE_AT = 3 * CELLS
MASKED = 1e30
EPSILON = 1e-06
LOG2E = 1.4426950408889634
LN2 = 0.6931471805599453
BF = jnp.bfloat16
F32 = jnp.float32
NT = (((1,), (1,)), ((), ()))
TN = (((0,), (0,)), ((), ()))


def dot(a, b):
    return jnp.dot(a, b, preferred_element_type=F32)


def dot_nt(a, b):
    return lax.dot_general(a, b, NT, preferred_element_type=F32)


def dot_tn(a, b):
    return lax.dot_general(a, b, TN, preferred_element_type=F32)


def geometry(grid_side, row_ids, slot_rows):
    page_len = grid_side * grid_side + 1
    page_count = slot_rows // page_len
    page_of = jnp.minimum(row_ids // page_len, page_count)
    offset = row_ids - page_of * page_len
    patch_id = jnp.maximum(offset - 1, 0)
    inside = page_of < page_count
    class_row = offset == 0
    coord_y = jnp.where(inside, jnp.where(class_row, SIDE_L, patch_id // grid_side), 0)
    coord_x = jnp.where(inside, jnp.where(class_row, SIDE_L, patch_id % grid_side), 0)
    return page_of, coord_y, coord_x


def row_features(page_of, coord_y, coord_x, flip):
    lane = jnp.arange(128, dtype=jnp.int32)[None, :]
    at = (lambda c: SIDE_L - c) if flip else (lambda c: c)
    hot = (lane == at(coord_y)[:, None]) | (lane == BLOCK + at(coord_x)[:, None])
    hot = hot | (lane == 2 * BLOCK + page_of[:, None])
    return hot.astype(BF)


def key_features(page_of, coord_y, coord_x):
    lane = jnp.arange(256, dtype=jnp.int32)[None, :]
    at_y = SIDE_L - coord_y[:, None]
    at_x = SIDE_L - coord_x[:, None]
    hot = (lane == at_y) | (lane == HEAD + at_y) | (lane == 128 + at_x)
    hot = hot | (lane == 128 + CELLS + at_y) | (lane == 128 + 2 * CELLS + at_x)
    hot = hot | (lane == 128 + PAGE_AT + page_of[:, None])
    return hot.astype(BF)


def table_rows(rel_table):
    layers, heads = rel_table.shape[:2]
    scaled = rel_table * LOG2E
    gap = jnp.zeros((*scaled.shape[:3], 128 - 2 * SIDE_L - 1), F32)
    scaled = jnp.concatenate([scaled[..., SIDE_L:], gap, scaled[..., :SIDE_L]], axis=-1)
    high = scaled.astype(BF).astype(F32)
    return jnp.concatenate([high, scaled - high], axis=2).reshape(layers, heads // 2, 8, 128)


def table_map(table_ref, head):
    row = lax.broadcasted_iota(jnp.int32, (BLOCK, 128), 0)
    lane = lax.broadcasted_iota(jnp.int32, (BLOCK, 128), 1)

    def grid(i, to):
        values = jnp.broadcast_to(table_ref[0, 4 * head + i : 4 * head + i + 1, :], (BLOCK, 128))
        values = pltpu.roll(values, 0, 1, stride=1, stride_axis=0)
        values = jnp.where((row < CELLS) & (lane < CELLS), values, 0.0)
        return pltpu.roll(values, to, 1) if to else values

    none = jnp.zeros((BLOCK, 128), F32)
    far = jnp.where((lane >= PAGE_AT) & (lane < PAGE_AT + PAGES) & (lane - PAGE_AT != row) & (row < PAGES), -MASKED, 0.0)
    left = [grid(0, HEAD if head == 0 else 0), none, none, none[:8]]
    right = [grid(2, CELLS), grid(1, 0) + grid(3, 2 * CELLS), far, none[:8]]
    return jnp.concatenate([jnp.concatenate(left, axis=0), jnp.concatenate(right, axis=0)], axis=1).astype(BF)


def split3(value):
    high = value.astype(BF).astype(F32)
    middle = (value - high).astype(BF).astype(F32)
    return high, middle, value - high - middle


def lanes_of(rows):
    return lax.broadcasted_iota(jnp.int32, (rows, PAIR), 1)


def attn_fwd_kernel(hot_ref, map_ref, q_ref, ko_ref, kp_ref, vo_ref, vp_ref, key_ref,
                    o_ref, rest_ref, inv_ref, w_ref, kx_ref, vx_ref):
    rows = q_ref.shape[0]
    lane = lanes_of(rows)
    for head in range(2):
        mine = (lane < HEAD) if head == 0 else (lane >= HEAD)
        one_at = HEAD if head == 0 else 0
        table = table_map(map_ref, head)
        kx, vx = kx_ref.at[head], vx_ref.at[head]
        kx[:, PAIR:] = key_ref[:, PAIR:]
        for part, (k_ref, v_ref) in enumerate(((ko_ref, vo_ref), (kp_ref, vp_ref))):
            at = pl.ds(part * rows, rows)
            kx[at, :PAIR] = jnp.where(mine, k_ref[...], key_ref[at, :PAIR])
            vx[at, :] = jnp.where(mine, v_ref[...], jnp.where(lane == one_at, 1.0, 0.0).astype(BF))
        feats = dot(hot_ref[...], table).astype(BF)
        query = jnp.concatenate([jnp.where(mine, q_ref[...], feats[:, :PAIR]), feats[:, PAIR:]], axis=1)
        scores = dot_nt(kx[...], query)
        weights = jnp.exp2(scores - jnp.max(scores, axis=0, keepdims=True)).astype(BF)
        w_ref[head] = weights
        mixed = dot_tn(vx[...], weights).T
        inv = 1.0 / mixed[:, one_at : one_at + 1]
        out = mixed * inv
        high = out.astype(BF)
        rest = (out - high.astype(F32)).astype(BF)
        inv = jnp.broadcast_to(inv, out.shape)
        if head == 0:
            o_ref[...], rest_ref[...], inv_ref[...] = high, rest, inv
        else:
            o_ref[...] = jnp.where(mine, high, o_ref[...])
            rest_ref[...] = jnp.where(mine, rest, rest_ref[...])
            inv_ref[...] = jnp.where(mine, inv, inv_ref[...])


def attn_forward(hot, maps, project, partner, keys, first, count):
    rows, width = project.shape[0], project.shape[1] // 3
    pairs = width // PAIR
    col = lambda off: pl.BlockSpec((rows, PAIR), lambda g: (0, off + first + g))
    out = pl.BlockSpec((rows, PAIR), lambda g: (0, g))
    return pl.pallas_call(
        attn_fwd_kernel,
        grid=(count,),
        in_specs=[
            whole((rows, 128)),
            pl.BlockSpec((1, 8, 128), lambda g: (first + g, 0, 0)),
            col(0),
            col(pairs),
            col(0),
            col(2 * pairs),
            col(pairs),
            whole((2 * rows, 256)),
        ],
        out_specs=[out, out, out, pl.BlockSpec((2, 2 * rows, rows), lambda g: (g, 0, 0))],
        out_shape=[
            jax.ShapeDtypeStruct((rows, count * PAIR), BF),
            jax.ShapeDtypeStruct((rows, count * PAIR), BF),
            jax.ShapeDtypeStruct((rows, count * PAIR), F32),
            jax.ShapeDtypeStruct((2 * count, 2 * rows, rows), BF),
        ],
        scratch_shapes=[pltpu.VMEM((2, 2 * rows, 256), BF), pltpu.VMEM((2, 2 * rows, PAIR), BF)],
        compiler_params=params_for(56),
        cost_estimate=cost(26),
        name="attn_fwd",
    )(hot, maps, project, project, partner, project, partner, keys)


def attn_bwd_kernel(hot_ref, w_ref, q_ref, ko_ref, kp_ref, vo_ref, vp_ref, key_ref, do_ref, o_ref, rest_ref, inv_ref,
                    dq_ref, mine_ref, other_ref, gt_ref, kx_ref, vx_ref, ds_ref):
    rows = q_ref.shape[0]
    lane = lanes_of(rows)
    scaled = (do_ref[...].astype(F32) * inv_ref[...]).astype(BF)
    product = scaled.astype(F32) * (o_ref[...].astype(F32) + rest_ref[...].astype(F32))
    for head in range(2):
        mine = (lane < HEAD) if head == 0 else (lane >= HEAD)
        spot = lane - (HEAD if head == 0 else 0)
        kx, vx, ds = kx_ref.at[head], vx_ref.at[head], ds_ref.at[head]
        kx[:, PAIR:] = key_ref[:, PAIR:]
        ones = jnp.where((spot >= 0) & (spot < 3), 1.0, 0.0).astype(BF)
        for part, (k_ref, v_ref) in enumerate(((ko_ref, vo_ref), (kp_ref, vp_ref))):
            at = pl.ds(part * rows, rows)
            kx[at, :PAIR] = jnp.where(mine, k_ref[...], key_ref[at, :PAIR])
            vx[at, :] = jnp.where(mine, v_ref[...], ones)
        delta = jnp.sum(jnp.where(mine, product, 0.0), axis=1, keepdims=True)
        high, middle, low = split3(delta)
        spread = jnp.where(spot == 0, -high, jnp.where(spot == 1, -middle, jnp.where(spot == 2, -low, 0.0)))
        d_out = jnp.where(mine, scaled, spread.astype(BF))
        for part, out_ref in enumerate((mine_ref, other_ref)):
            at = pl.ds(part * rows, rows)
            weights = w_ref[head, at, :]
            d_scores = (weights.astype(F32) * dot_nt(vx[at, :], d_out)).astype(BF)
            ds[at, :] = d_scores
            d_value = dot(weights, scaled).astype(BF)
            d_key = (dot(d_scores, q_ref[...]) * LN2).astype(BF)
            if head == 0:
                out_ref[1], out_ref[0] = d_value, d_key
            else:
                out_ref[1] = jnp.where(mine, d_value, out_ref[1])
                out_ref[0] = jnp.where(mine, d_key, out_ref[0])
        d_query = dot_tn(ds[...], kx[...])
        high_q = d_query.astype(BF)
        low_q = (d_query - high_q.astype(F32)).astype(BF)
        grid = dot_tn(hot_ref[...], high_q) + dot_tn(hot_ref[...], low_q)
        row = lax.broadcasted_iota(jnp.int32, (BLOCK, 128), 0)
        column = lax.broadcasted_iota(jnp.int32, (BLOCK, 128), 1)
        for axis in range(2):
            part = grid[axis * BLOCK : (axis + 1) * BLOCK, axis * 128 : (axis + 1) * 128]
            part = pltpu.roll(part, HEAD, 1) if axis == 0 and head == 0 else part
            part = jnp.where((row < CELLS) & (column < CELLS), part, 0.0)
            along = pltpu.roll(part, 0, 1, stride=1, stride_axis=0)
            gt_ref[0, 2 * head + axis : 2 * head + axis + 1, :] = jnp.sum(along, axis=0, keepdims=True)
        d_query = (d_query[:, :PAIR] * HEAD**-0.5).astype(BF)
        dq_ref[...] = d_query if head == 0 else jnp.where(mine, d_query, dq_ref[...])
    gt_ref[0, 4:8, :] = jnp.zeros((4, 128), F32)


def attn_backward(hot, weights, project, partner, keys, d_context, outcome, first, count):
    rows, width = project.shape[0], project.shape[1] // 3
    pairs = width // PAIR
    col = lambda off: pl.BlockSpec((rows, PAIR), lambda g: (0, off + first + g))
    out = pl.BlockSpec((rows, PAIR), lambda g: (0, g))
    both = pl.BlockSpec((2, rows, PAIR), lambda g: (0, 0, g))
    return pl.pallas_call(
        attn_bwd_kernel,
        grid=(count,),
        in_specs=[
            whole((rows, 128)),
            pl.BlockSpec((2, 2 * rows, rows), lambda g: (g, 0, 0)),
            col(0),
            col(pairs),
            col(0),
            col(2 * pairs),
            col(pairs),
            whole((2 * rows, 256)),
            col(0),
            out,
            out,
            out,
        ],
        out_specs=[out, both, both, pl.BlockSpec((1, 8, 128), lambda g: (g, 0, 0))],
        out_shape=[
            jax.ShapeDtypeStruct((rows, count * PAIR), BF),
            jax.ShapeDtypeStruct((2, rows, count * PAIR), BF),
            jax.ShapeDtypeStruct((2, rows, count * PAIR), BF),
            jax.ShapeDtypeStruct((count, 8, 128), F32),
        ],
        scratch_shapes=[
            pltpu.VMEM((2, 2 * rows, 256), BF),
            pltpu.VMEM((2, 2 * rows, PAIR), BF),
            pltpu.VMEM((2, 2 * rows, rows), BF),
        ],
        compiler_params=params_for(56),
        cost_estimate=cost(6 * count),
        name="attn_bwd",
    )(hot, weights, project, project, partner, project, partner, keys, d_context, *outcome)


def centred(values):
    values = values - jnp.mean(values, axis=-1, keepdims=True)
    inv = lax.rsqrt(jnp.mean(values * values, axis=-1, keepdims=True) + EPSILON)
    return values * inv, inv


def start_first(info_ref, kind, cols, far_cols, refs, dst, sem):
    own, near, far_own, far_other = refs
    local, core = info_ref[0] == 1, info_ref[1]
    part = far_own.shape[0]

    @pl.when(local & (core == kind))
    def _():
        pltpu.make_async_copy(own.at[:, cols], dst, sem).start()

    @pl.when(local & (core != kind))
    def _():
        pltpu.make_async_copy(near.at[:, cols], dst, sem).start()

    @pl.when(jnp.logical_not(local))
    def _():
        if part == dst.shape[0]:
            pltpu.make_async_copy(far_own, dst, sem).start()
            return
        pltpu.make_async_copy(far_own.at[:, far_cols], dst.at[pl.ds(core * part, part)], sem).start()
        pltpu.make_async_copy(far_other.at[:, far_cols], dst.at[pl.ds((1 - core) * part, part)], sem).start()


def start_down(info_ref, refs, dst, sem):
    own, near, far_own, far_other = refs
    local, core = info_ref[0] == 1, info_ref[1]
    part = own.shape[0]
    for here, mine, other in ((local, own, near), (jnp.logical_not(local), far_own, far_other)):

        @pl.when(here)
        def _(mine=mine, other=other):
            pltpu.make_async_copy(mine, dst.at[pl.ds(core * part, part)], sem).start()
            pltpu.make_async_copy(other, dst.at[pl.ds((1 - core) * part, part)], sem).start()


def wait_for(dst, sem):
    pltpu.make_async_copy(dst, dst, sem).wait()


EARLY = True
SMEM = pl.BlockSpec(memory_space=pltpu.SMEM)
ANY = pl.BlockSpec(memory_space=pl.ANY)


def whole(shape):
    return pl.BlockSpec(shape, lambda *g: (0,) * len(shape))


def params_for(mib):
    return pltpu.CompilerParams(vmem_limit_bytes=mib * 2**20)


def cost(us):
    return pl.CostEstimate(flops=int(us * 2e7), bytes_accessed=1000, transcendentals=0)


def project_kernel(info_ref, x_ref, p_ref, own, near, far_own, far_other, normed_ref, out_ref, w_ref, sem):
    width = x_ref.shape[1]
    start_first(info_ref, 0, pl.ds(0, 3 * width), pl.ds(0, 3 * width), (own, near, far_own, far_other), w_ref, sem)
    nhat, _ = centred(x_ref[...].astype(F32))
    normed = (nhat * p_ref[0:1, :] + p_ref[1:2, :]).astype(BF)
    normed_ref[...] = normed
    wait_for(w_ref, sem)
    for j in range(3):
        at = pl.ds(j * width, width)
        value = dot(normed, w_ref[:, at])
        if j == 0:
            value = value * (HEAD**-0.5 * LOG2E)
        out_ref[:, at] = value.astype(BF)


def project(info, x, p, first_refs):
    rows, width = x.shape
    return pl.pallas_call(
        project_kernel,
        in_specs=[SMEM, whole(x.shape), whole(p.shape)] + [ANY] * 4,
        out_specs=[whole((rows, width)), whole((rows, 3 * width))],
        out_shape=[jax.ShapeDtypeStruct((rows, width), BF), jax.ShapeDtypeStruct((rows, 3 * width), BF)],
        scratch_shapes=[pltpu.VMEM((width, 3 * width), BF), pltpu.SemaphoreType.DMA],
        compiler_params=params_for(40),
        cost_estimate=cost(5),
        name="project",
    )(info, x, p, *first_refs)


def block_out_kernel(info_ref, x_ref, ctx_a, ctx_b, p0_ref, p1_ref, *refs):
    att, up, refs = refs[:4], refs[:2] + refs[4:6], refs[6:]
    down, refs = refs[:4], refs[4:]
    b0_ref, x1_ref, n1_ref, slope_ref, hid_ref, b1_ref, x2_ref, mine_ref, other_ref, wo_ref, wu_ref, wd_ref, slopes, hiddens, sems, out_sems = refs
    width = x_ref.shape[1]
    start_first(info_ref, 0, pl.ds(3 * width, width), pl.ds(0, width), att, wo_ref, sems.at[0])
    for j in range(4):
        start_first(info_ref, 1, pl.ds(j * width, width), pl.ds(j * width, width), up, wu_ref.at[j], sems.at[1 + j])
    start_down(info_ref, down, wd_ref, sems.at[5])
    wait_for(wo_ref, sems.at[0])
    half = width // 2
    branch = dot(ctx_a[...], wo_ref[:half]) + dot(ctx_b[...], wo_ref[half:])
    b0_ref[...] = branch.astype(BF)
    x1 = (x_ref[...].astype(F32) + p0_ref[2:3, :] * branch).astype(BF)
    x1_ref[...] = x1
    x1 = x1.astype(F32)
    nhat, _ = centred(x1)
    normed = (nhat * p1_ref[0:1, :] + p1_ref[1:2, :]).astype(BF)
    n1_ref[...] = normed
    for j in range(4):
        wait_for(wu_ref.at[j], sems.at[1 + j])
    wait_for(wd_ref, sems.at[5])
    total = jnp.zeros(x1.shape, F32)
    for j in range(4):
        at = pl.ds(j * width, width)
        v = dot(normed, wu_ref[j])
        square = v * v
        bend = jnp.tanh(v * (0.7978845608028654 + (0.7978845608028654 * 0.044715) * square))
        up_half = 0.5 + 0.5 * bend
        along = v * (2 * 0.7978845608028654 + (6 * 0.7978845608028654 * 0.044715) * square)
        slopes[j] = (up_half + along * (up_half * (1.0 - up_half))).astype(BF)
        hiddens[j] = (v * up_half).astype(BF)
        if EARLY:
            pltpu.make_async_copy(slopes.at[j], slope_ref.at[:, at], out_sems.at[0, j]).start()
            pltpu.make_async_copy(hiddens.at[j], hid_ref.at[:, at], out_sems.at[1, j]).start()
        total = total + dot(hiddens[j], wd_ref[at, :])
    b1_ref[...] = total.astype(BF)
    x2 = (x1 + p1_ref[2:3, :] * total).astype(BF)
    x2_ref[...] = x2
    first = info_ref[1] == 0
    mine_ref[...] = jnp.where(first, x1_ref[...], x2)
    other_ref[...] = jnp.where(first, x2, x1_ref[...])
    if not EARLY:
        for j in range(4):
            at = pl.ds(j * width, width)
            pltpu.make_async_copy(slopes.at[j], slope_ref.at[:, at], out_sems.at[0, j]).start()
            pltpu.make_async_copy(hiddens.at[j], hid_ref.at[:, at], out_sems.at[1, j]).start()
    for j in range(4):
        wait_for(slopes.at[j], out_sems.at[0, j])
        wait_for(hiddens.at[j], out_sems.at[1, j])


def block_out(info, x, context, p0, p1, more_refs, up_refs, down_refs):
    rows, width = x.shape
    one = whole((rows, width))
    shape = lambda n: jax.ShapeDtypeStruct((rows, n), BF)
    widths = [width, width, width, 4 * width, 4 * width, width, width, width, width]
    refs = (*more_refs, *up_refs[2:], *down_refs)
    return pl.pallas_call(
        block_out_kernel,
        grid=(1,),
        in_specs=[SMEM, one, *[whole(c.shape) for c in context], whole(p0.shape), whole(p1.shape)] + [ANY] * len(refs),
        out_specs=[one if n == width else ANY for n in widths],
        out_shape=[shape(n) for n in widths],
        scratch_shapes=[
            pltpu.VMEM((width, width), BF),
            pltpu.VMEM((4, width, width), BF),
            pltpu.VMEM((4 * width, width), BF),
            pltpu.VMEM((4, rows, width), BF),
            pltpu.VMEM((4, rows, width), BF),
            pltpu.SemaphoreType.DMA((6,)),
            pltpu.SemaphoreType.DMA((2, 4)),
        ],
        compiler_params=params_for(58),
        cost_estimate=cost(12),
        name="block_out",
    )(info, x, *context, p0, p1, *refs)


def norm_back(x, gain, d_normed, gy):
    nhat, inv = centred(x)
    inner = d_normed * gain
    shift = jnp.mean(inner, axis=-1, keepdims=True)
    along = jnp.mean(inner * nhat, axis=-1, keepdims=True)
    total = lambda v: jnp.sum(v, axis=0, keepdims=True)
    return gy + inv * (inner - shift - nhat * along), total(nhat * d_normed), total(d_normed)


def block_back_kernel(info_ref, gy_ref, x1_ref, slope_ref, b1_ref, b0_ref, p0_ref, p1_ref, *refs):
    att, up, refs = refs[:4], refs[:2] + refs[4:6], refs[6:]
    down, refs = refs[:4], refs[4:]
    db1_ref, dpre_ref, gx_ref, db0_ref, dctx_ref, vec_ref, wo_ref, wu_ref, wd_ref, slopes, given, sems, more_sems = refs
    width = gy_ref.shape[1]
    start_down(info_ref, down, wd_ref, sems.at[5])
    for j in range(4):
        at = pl.ds(j * width, width)
        start_first(info_ref, 1, at, at, up, wu_ref.at[j], sems.at[1 + j])
        pltpu.make_async_copy(slope_ref.at[:, at], slopes.at[j], more_sems.at[0, j]).start()
    start_first(info_ref, 0, pl.ds(3 * width, width), pl.ds(0, width), att, wo_ref, sems.at[0])
    total = lambda v: jnp.sum(v, axis=0, keepdims=True)
    gy = gy_ref[...].astype(F32)
    d_branch = (gy * p1_ref[2:3, :]).astype(BF)
    db1_ref[...] = d_branch
    vec_ref[2:3, :] = total(b1_ref[...].astype(F32) * gy)
    vec_ref[4:, :] = jnp.zeros((4, width), F32)
    d_normed = jnp.zeros(gy.shape, F32)
    wait_for(wd_ref, sems.at[5])
    for j in range(4):
        wait_for(slopes.at[j], more_sems.at[0, j])
        wait_for(wu_ref.at[j], sems.at[1 + j])
    for j in range(4):
        at = pl.ds(j * width, width)
        d_hidden = dot_nt(d_branch, wd_ref[at, :])
        given[j] = (d_hidden * slopes[j].astype(F32)).astype(BF)
        if EARLY:
            pltpu.make_async_copy(given.at[j], dpre_ref.at[:, at], more_sems.at[1, j]).start()
        d_normed = d_normed + dot_nt(given[j], wu_ref[j])
    if not EARLY:
        for j in range(4):
            pltpu.make_async_copy(given.at[j], dpre_ref.at[:, pl.ds(j * width, width)], more_sems.at[1, j]).start()
    gx, g_gain, g_shift = norm_back(x1_ref[...].astype(F32), p1_ref[0:1, :], d_normed, gy)
    vec_ref[0:1, :] = g_gain
    vec_ref[1:2, :] = g_shift
    gx = gx.astype(BF)
    gx_ref[...] = gx
    gx = gx.astype(F32)
    d_att = (gx * p0_ref[2:3, :]).astype(BF)
    db0_ref[...] = d_att
    vec_ref[3:4, :] = total(b0_ref[...].astype(F32) * gx)
    wait_for(wo_ref, sems.at[0])
    dctx_ref[...] = dot_nt(d_att, wo_ref[...]).astype(BF)
    for j in range(4):
        wait_for(given.at[j], more_sems.at[1, j])


def block_back(info, gy, x1, slope, b1, b0, p0, p1, more_refs, up_refs, down_refs):
    rows, width = gy.shape
    one = whole((rows, width))
    shape = lambda n: jax.ShapeDtypeStruct((rows, n), BF)
    widths = [width, 4 * width, width, width, width]
    refs = (*more_refs, *up_refs[2:], *down_refs)
    return pl.pallas_call(
        block_back_kernel,
        grid=(1,),
        in_specs=[SMEM, one, one, ANY, one, one, whole(p0.shape), whole(p1.shape)] + [ANY] * len(refs),
        out_specs=[one if n == width else ANY for n in widths] + [whole((8, width))],
        out_shape=[shape(n) for n in widths] + [jax.ShapeDtypeStruct((8, width), F32)],
        scratch_shapes=[
            pltpu.VMEM((width, width), BF),
            pltpu.VMEM((4, width, width), BF),
            pltpu.VMEM((4 * width, width), BF),
            pltpu.VMEM((4, rows, width), BF),
            pltpu.VMEM((4, rows, width), BF),
            pltpu.SemaphoreType.DMA((6,)),
            pltpu.SemaphoreType.DMA((2, 4)),
        ],
        compiler_params=params_for(58),
        cost_estimate=cost(14),
        name="block_back",
    )(info, gy, x1, slope, b1, b0, p0, p1, *refs)


def project_back_kernel(info_ref, gy_ref, x_ref, p_ref, dqa, dqb, mya, myb, gota, gotb, own, near, far_own, far_other,
                        dproj_ref, gx_ref, vec_ref, w_ref, sem):
    width = x_ref.shape[1]
    start_first(info_ref, 0, pl.ds(0, 3 * width), pl.ds(0, 3 * width), (own, near, far_own, far_other), w_ref, sem)
    half = width // 2
    for i, (dq, my, got) in enumerate(((dqa, mya, gota), (dqb, myb, gotb))):
        dproj_ref[:, i * half : (i + 1) * half] = dq[...]
        for j in range(2):
            at = pl.ds((1 + j) * width + i * half, half)
            dproj_ref[:, at] = (my[j].astype(F32) + got[j].astype(F32)).astype(BF)
    wait_for(w_ref, sem)
    d_normed = dot_nt(dproj_ref[:, :width], w_ref[:, :width])
    for j in (1, 2):
        at = pl.ds(j * width, width)
        d_normed = d_normed + dot_nt(dproj_ref[:, at], w_ref[:, at])
    gx, g_gain, g_shift = norm_back(x_ref[...].astype(F32), p_ref[0:1, :], d_normed, gy_ref[...].astype(F32))
    gx_ref[...] = gx.astype(BF)
    vec_ref[0:1, :] = g_gain
    vec_ref[1:2, :] = g_shift
    vec_ref[2:, :] = jnp.zeros((6, width), F32)


def project_back(info, gy, x, p, parts, first_refs):
    rows, width = x.shape
    one = whole((rows, width))
    return pl.pallas_call(
        project_back_kernel,
        in_specs=[SMEM, one, one, whole(p.shape)] + [whole(v.shape) for v in parts] + [ANY] * 4,
        out_specs=[whole((rows, 3 * width)), one, whole((8, width))],
        out_shape=[
            jax.ShapeDtypeStruct((rows, 3 * width), BF),
            jax.ShapeDtypeStruct((rows, width), BF),
            jax.ShapeDtypeStruct((8, width), F32),
        ],
        grid=(1,),
        scratch_shapes=[pltpu.VMEM((width, 3 * width), BF), pltpu.SemaphoreType.DMA],
        compiler_params=params_for(48),
        cost_estimate=cost(7),
        name="project_back",
    )(info, gy, x, p, *parts, *first_refs)


def gather_kernel(info_ref, mine, by_x, by_z, diag_x, diag_z, out_ref, sem):
    quarter = mine.shape[0]
    part = quarter // 2
    q = info_ref[0]
    at = lambda i: pl.multiple_of(i * quarter, part)
    pltpu.make_async_copy(mine, out_ref.at[pl.ds(at(q), quarter)], sem).start()
    pltpu.make_async_copy(by_x, out_ref.at[pl.ds(at(info_ref[1]), quarter)], sem).start()
    pltpu.make_async_copy(by_z, out_ref.at[pl.ds(at(info_ref[2]), quarter)], sem).start()
    pltpu.make_async_copy(diag_x, out_ref.at[pl.ds(at(info_ref[3]), part)], sem).start()
    pltpu.make_async_copy(diag_z, out_ref.at[pl.ds(at(info_ref[3]) + part, part)], sem).start()
    wait_for(out_ref, sem)


def dp_swap(value, bit):
    return lax.ppermute(value, "dp", [(i, i ^ bit) for i in range(lax.axis_size("dp"))])


def tie(value, *deps):
    return lax.optimization_barrier((value, deps))[0]


def hold(values, count):
    state = values[-1]
    if not isinstance(state, list):
        return lax.optimization_barrier(values)
    arrays = [part[:2] for part in state]
    *values, arrays = lax.optimization_barrier((*values[:count], arrays))
    return (*values, [(*part, names) for part, (_, _, names) in zip(arrays, state)])


def together(values):
    return lax.optimization_barrier(values)


def quad_start(mine):
    return mine, dp_swap(mine, 1), dp_swap(mine, 2)


def quad_end(mine, by_x, by_z):
    part = mine.shape[0] // 2
    return mine, by_x, by_z, dp_swap(by_z[:part], 1), dp_swap(by_x[part:], 2)


def quad_place(mine, *others):
    quarter = mine.shape[0]
    q = lax.axis_index("dp") % 4
    spots = jnp.stack([q, q ^ 1, q ^ 2, q ^ 3]).astype(jnp.int32)
    return pl.pallas_call(
        gather_kernel,
        in_specs=[SMEM] + [ANY] * 5,
        out_specs=whole((4 * quarter, *mine.shape[1:])),
        out_shape=jax.ShapeDtypeStruct((4 * quarter, *mine.shape[1:]), mine.dtype),
        scratch_shapes=[pltpu.SemaphoreType.DMA],
        compiler_params=params_for(16),
        cost_estimate=cost(3),
        name="assemble",
    )(spots, mine, *others)


def put_rows(values, slot, tmp_ref, keep_ref, send_ref, core, for_d, at, sems):
    tmp = tmp_ref.at[slot].reshape(values.shape)
    tmp[...] = values
    pltpu.make_async_copy(tmp.at[:, core], keep_ref.at[for_d, at], sems.at[slot, 0]).start()
    pltpu.make_async_copy(tmp.at[:, 1 - core], send_ref.at[for_d, at], sems.at[slot, 1]).start()


def mlp_grads_kernel(core_ref, n_ref, pre_ref, hid_ref, db_ref, keep_ref, send_ref, tmp_ref, sems):
    core, j = core_ref[0], pl.program_id(0)
    width = n_ref.shape[1]
    size = keep_ref.shape[0]
    short, long = width // (2 * size), 2 * width // (2 * size)

    def finish(slot, long_rows):
        for i, ref in enumerate((keep_ref, send_ref)):
            to = ref.at[pl.ds(0, size // 2), pl.ds(0, long)] if long_rows else ref.at[:, pl.ds(0, short)]
            pltpu.make_async_copy(to, to, sems.at[slot, i]).wait()

    @pl.when(j > 0)
    def _():
        finish(0, False)
    up = dot_tn(n_ref[...], pre_ref[...]).astype(BF).reshape(size, 2, short, width)
    put_rows(up, 0, tmp_ref, keep_ref, send_ref, core, pl.ds(0, size), pl.ds(j * short, short), sems)

    @pl.when(j > 0)
    def _():
        finish(1, True)
    down = dot_tn(hid_ref[...], db_ref[...]).astype(BF).reshape(size // 2, 2, long, width)
    at = pl.ds(4 * short + (j // 2) * long, long)
    put_rows(down, 1, tmp_ref, keep_ref, send_ref, core, pl.ds((j % 2) * (size // 2), size // 2), at, sems)

    @pl.when(j == pl.num_programs(0) - 1)
    def _():
        finish(0, False)
        finish(1, True)


def att_grads_kernel(core_ref, n_ref, dproj_ref, ctx_a, ctx_b, db_ref, keep_ref, send_ref, tmp_ref, sems):
    core, j = core_ref[0], pl.program_id(0)
    width = n_ref.shape[1]
    size = keep_ref.shape[0]
    short = width // (2 * size)
    slot = lax.rem(j, 2)
    tmp = tmp_ref.at[slot].reshape(size, 2, short, width)

    def finish(at):
        for i, ref in enumerate((keep_ref, send_ref)):
            to = ref.at[:, pl.ds(0, short)]
            pltpu.make_async_copy(to, to, sems.at[at, i]).wait()

    @pl.when(j > 1)
    def _():
        finish(slot)

    @pl.when(j < 3)
    def _():
        tmp[...] = dot_tn(n_ref[...], dproj_ref[...]).astype(BF).reshape(tmp.shape)

    @pl.when(j == 3)
    def _():
        for i, ctx_ref in enumerate((ctx_a, ctx_b)):
            grad = dot_tn(ctx_ref[...], db_ref[...]).astype(BF)
            tmp[pl.ds(i * (size // 2), size // 2)] = grad.reshape(size // 2, 2, short, width)

    at = pl.ds(j * short, short)
    pltpu.make_async_copy(tmp.at[:, core], keep_ref.at[:, at], sems.at[slot, 0]).start()
    pltpu.make_async_copy(tmp.at[:, 1 - core], send_ref.at[:, at], sems.at[slot, 1]).start()

    @pl.when(j == 3)
    def _():
        finish(0)
        finish(1)


def plain_grads(att, core, shape, a, b, c, d):
    size, _, width = shape
    cut = lambda grad: [grad[:, j * width : (j + 1) * width].reshape(size, 2, -1, width) for j in range(grad.shape[1] // width)]
    parts = cut(dot_tn(a, b).astype(BF))
    if att:
        parts += cut(dot_tn(c, d).astype(BF))
    else:
        parts += [half.reshape(size, 2, -1, width) for half in jnp.split(dot_tn(c, d).astype(BF), 2, axis=0)]
    both = jnp.concatenate(parts, axis=2)
    at = lambda i: lax.dynamic_index_in_dim(both, i, 1, keepdims=False)
    return at(core), at(1 - core)


def weight_grads(kernel, core, size, us, a, b, c, d):
    rows, width = a.shape
    att = kernel is att_grads_kernel
    shape = (size, (2 * width if att else 4 * width) // size, width)
    if width // (2 * size) % 16:
        return plain_grads(att, core, shape, a, b, jnp.concatenate(c, axis=1), d)
    col = pl.BlockSpec((rows, width), lambda j: (0, jnp.minimum(j, 2 if att else 3)))
    return pl.pallas_call(
        kernel,
        grid=(4,),
        in_specs=[SMEM, whole(a.shape), col, *([whole(v.shape) for v in c] if att else [col]), whole(d.shape)],
        out_specs=[ANY] * 2,
        out_shape=[jax.ShapeDtypeStruct(shape, BF)] * 2,
        scratch_shapes=[pltpu.VMEM((2, width, width), BF), pltpu.SemaphoreType.DMA((2, 2))],
        compiler_params=params_for(48),
        cost_estimate=cost(us),
        name=kernel.__name__[:-7],
    )(core.astype(jnp.int32).reshape(1), a, b, *c, d)


def send(value, pairs):
    return lax.ppermute(value, "pipe", pairs)


def swap(value, bit):
    return send(value, [(i, i ^ bit) for i in range(lax.axis_size("pipe"))])


def to_target(value, target, bit):
    return send(value, [(target ^ bit, target)])


def pick(core, mine_first, mine_second):
    return jnp.where(core == 0, mine_first, mine_second)


ORDERS = (("x", "y", "z2", "z4"), ("y", "z2", "x", "z4"), ("z2", "x", "y", "z4"))
AT = {"x": ("dp", 1), "z2": ("dp", 2), "z4": ("dp", 4), "y": ("pipe", 2)}


def cube_start(parts):
    size, rows, width = parts.shape
    if size != 8:
        return parts
    parts = parts.reshape(2, 2, 2, 2, rows // 2, width)
    share = width // len(ORDERS)
    return [(parts[..., i * share : (i + 1) * share], None, ["z4", "z2", "x", "y"]) for i in range(len(ORDERS))]


def settled(part, got):
    return part if got is None else part + got


def halve(part, names, axis):
    name, bit = AT[axis]
    i = names.index(axis)
    me = (lax.axis_index(name) // bit) % 2
    at = lambda j: lax.dynamic_index_in_dim(part, j, i, keepdims=False)
    give = at(1 - me)
    got = lax.ppermute(give, name, [(k, k ^ bit) for k in range(lax.axis_size(name))])
    return at(me), got, [n for n in names if n != axis], give


def cube_step(state, step):
    if not isinstance(state, list):
        return state, state
    done = [halve(settled(part, got), names, order[step]) for (part, got, names), order in zip(state, ORDERS)]
    return [d[:3] for d in done], [d[3] for d in done]


def cube_end(state):
    if not isinstance(state, list):
        plane = lax.axis_index("pipe") // 2
        parts = state.reshape(state.shape[0], 2, -1, state.shape[2])
        at = lambda i: lax.dynamic_index_in_dim(parts, i, 1, keepdims=False)
        return (lax.psum_scatter(at(plane) + swap(at(1 - plane), 2), "dp", scatter_dimension=0), None), state
    whole_part = jnp.concatenate([settled(part, got) for part, got, _ in state], axis=-1)
    mine, got, _, give = halve(whole_part, ["z4"], "z4")
    return (mine, got), give


def line_start(parts):
    return lax.psum_scatter(parts, "dp", scatter_dimension=0)


def line_end(mlp, att):
    plane = lax.axis_index("pipe") // 2
    cut = lambda v, i: lax.dynamic_index_in_dim(v.reshape(2, -1, v.shape[1]), i, 0, keepdims=False)
    got = swap(jnp.concatenate([cut(mlp, 1 - plane), cut(att, 1 - plane)], axis=0), 2)
    rows = mlp.shape[0] // 2
    return cut(mlp, plane) + got[:rows], cut(att, plane) + got[rows:]


def by_sender(layer, even, odd, core, bits):
    targets = (2 * layer, 2 * layer + 1)
    mine, other = pick(core, even, odd), pick(core, odd, even)
    return [send(mine if bit == 2 else other, [(t ^ bit, t) for t in targets]) for bit in bits]


def from_pipe(value, target, sources):
    return [value if i == target else send(value, [(i, target)]) for i in sources]


def att_result(got):
    rows = got[0].shape[0] // 2
    cols = []
    for j in range(4):
        cols.append(jnp.concatenate([got[(j // 2) * 2 + c][(j % 2) * rows : (j % 2 + 1) * rows] for c in range(2)], axis=0))
    return jnp.concatenate(cols, axis=1)


def up_result(up):
    rows = up[0].shape[0] // 4
    return jnp.concatenate([jnp.concatenate([v[j * rows : (j + 1) * rows] for v in up], axis=0) for j in range(4)], axis=1)


def choose(place, options):
    result = options[-1]
    for s in range(len(options) - 2, -1, -1):
        result = jnp.where(place == s, options[s], result)
    return result


def small_sum(value, step):
    if lax.axis_size("dp") != 8:
        return lax.psum(value, ("dp", "pipe")) if step == 0 else value
    if step == 2:
        return value + dp_swap(value, 4)
    move = swap if step == 0 else dp_swap
    return (value + move(value, 1)) + (move(value, 2) + move(value, 3))


def local(
    inputs, out_grad, page_side, norm_gain, norm_shift, layer_scale, w_first, w_half, rel_table
):
    place = lax.axis_index("pipe")
    sections = lax.axis_size("pipe")
    dp_size, dp_place = lax.axis_size("dp"), lax.axis_index("dp")
    micro_count, slot_rows, width = inputs.shape
    halves = sections // micro_count
    assert halves == 2 and sections == 4
    rows = slot_rows // halves
    plane, core = place // 2, place % 2
    layers, heads = rel_table.shape[:2]

    own_params = jnp.stack([norm_gain[0], norm_shift[0], layer_scale[0]])
    seen = [own_params] + [swap(own_params, bit) for bit in (1, 2, 3)]
    params = [choose(place, [seen[s ^ p] for p in range(sections)]) for s in range(sections)]

    own_first, own_half = w_first[0], w_half[0]
    count = own_first.shape[0] // 2
    quarter = count // 4
    q = dp_place % 4
    infos = [jnp.stack([(plane == layer).astype(jnp.int32), core.astype(jnp.int32)]) for layer in range(layers)]

    micro, half = plane, core
    side = lax.dynamic_index_in_dim(page_side, micro, 0, keepdims=False)[0]
    own_rows = lambda x: lax.dynamic_slice(x, (micro, half * rows, 0), (1, rows, width))[0]
    key_ids = (jnp.arange(slot_rows, dtype=jnp.int32) + half * rows) % slot_rows
    layout = geometry(side, key_ids, slot_rows)
    own_layout = [c[:rows] for c in layout]
    hot, hot_back = row_features(*own_layout, True), row_features(*own_layout, False)
    keys = key_features(*layout)
    maps = table_rows(rel_table)

    current = own_rows(inputs)
    qkv = own_first[:, : 3 * width]
    far_qkv = (send(qkv[:count], [(0, 2), (2, 0)]), send(qkv[count:], [(0, 3), (2, 1)]))
    share = [lax.dynamic_slice_in_dim(own_first, c * count + q * quarter, quarter, 0) for c in range(2)]
    half_rows = own_half.shape[0] // 4
    share_half = lax.dynamic_slice_in_dim(own_half, q * half_rows, half_rows, 0)
    own_out = own_first[:, 3 * width :]
    last_grad = own_rows(out_grad)
    ready = (far_qkv, params, infos, current, last_grad, hot, hot_back, keys, maps, share, share_half, own_out)
    far_qkv, params, infos, current, last_grad, hot, hot_back, keys, maps, share, share_half, own_out = together(ready)
    far_qkv = pick(core, *far_qkv)
    qkv_refs = (own_first, swap(own_first, 1), far_qkv, swap(far_qkv, 1))
    mine_up = (send(share[0], [(1, 2), (3, 0)]), send(share[1], [(1, 3), (3, 1)]))
    mine_half = swap(share_half, 2)

    def shared(mine, other, layer):
        inside = [(2 * layer, 2 * layer + 1), (2 * layer + 1, 2 * layer)]
        straight = [(p ^ 2, p) for p in (2 * layer, 2 * layer + 1)]
        across = [(p ^ 3, p) for p in (2 * layer, 2 * layer + 1)]
        return [mine, send(other, inside), send(mine, straight), send(other, across)]

    def to_one(value, s):
        return [value] + [to_target(value, s, bit) for bit in (1, 2, 3)]

    def collected(parts):
        return choose(place, [jnp.stack([parts[s][i ^ s] for i in range(sections)]) for s in range(sections)])

    kept, outs = [], {}
    cut = heads // 4
    for layer in range(layers):
        p0, p1, info = params[2 * layer], params[2 * layer + 1], infos[layer]
        normed, proj = project(info, current, p0, qkv_refs)
        if layer == 0:
            own_out = tie(own_out, normed)
        partner = swap(proj[:, width:], 1)
        front = lambda keys, i: attn_forward(hot, maps[layer], proj, partner, keys, i * cut, cut)
        if layer == 0:
            partner, own_out, mine_up = together((partner, own_out, mine_up))
            some_up = quad_start(pick(core, *mine_up))
            far_out = send(own_out, [(0, 2), (2, 0)])
        part_a = front(keys, 0)
        if layer == 0:
            part_a, some_up, mine_half = together((part_a, some_up, mine_half))
            some_half = quad_start(mine_half)
            all_up = quad_end(*some_up)
        part_b = front(tie(keys, part_a[0]), 1)
        if layer == 0:
            part_b, all_up, some_half, far_out = together((part_b, all_up, some_half, far_out))
            near_out, all_half = swap(far_out, 1), quad_end(*some_half)
            far_up, far_half = quad_place(*all_up), quad_place(*all_half)
            far_out = pick(core, far_out, near_out)
            near_half = swap(tie(own_half, far_qkv), 1)
            more_refs = (qkv_refs[0], qkv_refs[1], far_out, far_out)
            up_refs = (qkv_refs[0], qkv_refs[1], far_up, swap(far_up, 1))
            down_refs = (own_half, near_half, far_half, swap(far_half, 1))
        else:
            part_b = tie(part_b, outs[0][2])
        context = (part_a[0], part_b[0])
        b0, x1, n1, slope, hidden, b1, x2, mine, other = block_out(info, current, context, p0, p1, more_refs, up_refs, down_refs)
        if layer == 1:
            b0, x1, n1, slope, hidden, b1, x2, mine, other = tie((b0, x1, n1, slope, hidden, b1, x2, mine, other), outs[0])
        kept.append((current, normed, proj, partner, (part_a, part_b), b0, x1, n1, slope, hidden, b1))
        outs[2 * layer] = outs[2 * layer + 1] = shared(mine, other, layer)
        current = x2

    tables, vecs, grads = {}, {}, {}
    core_id = core.astype(jnp.int32)

    x, normed, proj, partner, outcome, b0, x1, n1, slope, hidden, b1 = kept[1]
    p0, p1, info = params[2], params[3], infos[1]
    grad = tie(last_grad, current)
    db1, d_pre, gx1, db0, d_context, vec1 = block_back(info, grad, x1, slope, b1, b0, p0, p1, more_refs, up_refs, down_refs)
    db1, d_pre, gx1, db0, d_context, vec1 = tie((db1, d_pre, gx1, db0, d_context, vec1), outs[2][2])
    keep, other = weight_grads(mlp_grads_kernel, core, dp_size, 15, n1, d_pre, (hidden,), db1)
    keep, other = tie((keep, other), outs[2])
    got = swap(other, 1)
    back = lambda d_ctx, i: attn_backward(hot_back, outcome[i][3], proj, partner, keys, d_ctx, outcome[i][:3], i * cut, cut)
    dqa, mya, oa, ta = back(tie(d_context, keep), 0)
    dqa, mya, oa, ta, got = together((dqa, mya, oa, ta, got))
    mlp_b = keep + got
    gota = swap(oa, 1)
    dqb, myb, ob, tb = back(tie(d_context, mlp_b, oa), 1)
    dqb, myb, ob, tb, gota = together((dqb, myb, ob, tb, gota))
    gotb = swap(ob, 1)
    mlp_b = line_start(mlp_b)
    d_proj, gx0, vec0 = project_back(info, gx1, x, p0, (dqa, dqb, mya, myb, gota, gotb), qkv_refs)
    keep, other = weight_grads(att_grads_kernel, core, dp_size, 9, normed, d_proj, [part[0] for part in outcome], db0)
    got = swap(other, 1)
    grads[2] = grads[3] = shared(pick(core, gx0, gx1), pick(core, gx1, gx0), 1)
    tables[1] = (ta, tb)
    vecs[3], vecs[2] = vec1[:3], jnp.concatenate([vec0[:2], vec1[3:4]])

    x, normed, proj, partner, outcome, b0, x1, n1, slope, hidden, b1 = kept[0]
    p0, p1, info = params[0], params[1], infos[0]
    db1, d_pre, gx1, db0, d_context, vec1 = block_back(info, tie(gx0, keep), x1, slope, b1, b0, p0, p1, more_refs, up_refs, down_refs)
    db1, d_pre, gx1, db0, d_context, vec1, got = tie((db1, d_pre, gx1, db0, d_context, vec1, got), grads[2][2])
    att_b = keep + got
    d_pre = tie(d_pre, att_b)
    att_b = line_start(att_b)
    keep, other = weight_grads(mlp_grads_kernel, core, dp_size, 15, n1, d_pre, (hidden,), db1)
    keep, other = tie((keep, other), grads[2])
    got = swap(other, 1)
    grads[1] = to_one(gx1, 1)
    dqa, mya, oa, ta = back(tie(d_context, keep), 0)
    dqa, mya, oa, ta, got, mlp_b = tie((dqa, mya, oa, ta, got, mlp_b), grads[1])
    mlp_a = cube_start(keep + got)
    gota = swap(oa, 1)
    mlp_a, given = cube_step(mlp_a, 0)
    dqb, myb, ob, tb = back(tie(d_context, given, oa), 1)
    dqb, myb, ob, tb, gota, mlp_a = hold((dqb, myb, ob, tb, gota, mlp_a), 5)
    gotb = swap(ob, 1)
    mlp_a, given = cube_step(mlp_a, 1)
    gotb = tie(gotb, given)
    d_proj, gx0, vec0 = project_back(info, gx1, x, p0, (dqa, dqb, mya, myb, gota, gotb), qkv_refs)
    d_proj, gx0, vec0, mlp_a = hold((d_proj, gx0, vec0, mlp_a), 3)
    grads[0] = to_one(gx0, 0)
    keep, other = weight_grads(att_grads_kernel, core, dp_size, 9, normed, d_proj, [part[0] for part in outcome], db0)
    keep, other, att_b, grads[0][1] = together((keep, other, att_b, grads[0][1]))
    got = swap(other, 1)
    att_sum = keep + got
    att_a = line_start(att_sum)
    tables = [(ta, tb), tables[1]]
    att_sum, tables, vec0, mlp_b, att_b, outs, mlp_a = hold((att_sum, tables, vec0, mlp_b, att_b, outs, mlp_a), 6)
    vecs[1], vecs[0] = vec1[:3], jnp.concatenate([vec0[:2], vec1[3:4]])
    stack = lambda parts: jnp.stack([parts[s] for s in range(sections)])
    table_all = [jnp.concatenate(tables[layer])[:, :4].reshape(heads, 2, 128)[..., : 2 * SIDE_L + 1] for layer in range(layers)]
    small = jnp.concatenate([stack(vecs).reshape(-1), jnp.stack(table_all).reshape(-1)])
    mlp_a, _ = cube_step(mlp_a, 2)
    mlp_b, att_b = line_end(mlp_b, att_b)
    section_out = collected(outs).reshape(1, micro_count, slot_rows, width)
    small, section_out, mlp_b, att_b, grads[0], mlp_a = hold((small, section_out, mlp_b, att_b, grads[0], mlp_a), 5)
    mlp_a, given = cube_end(mlp_a)
    mlp_b, att_b, small = tie((mlp_b, att_b, small), given)
    small = small_sum(small, 0)
    even = jnp.concatenate([att_b, mlp_b[: att_b.shape[0]]], axis=0)
    own_b = pick(core, even, mlp_b)
    got_b = by_sender(1, even, mlp_b, core, (1, 2, 3))
    small, got_b, own_b, mlp_a = together((small, got_b, own_b, mlp_a))
    mlp_a = settled(*mlp_a)
    low, high = jnp.split(mlp_a, 2, axis=0)
    small = small_sum(small, 1)
    ups = [mlp_a, send(mlp_a, [(0, 1)])]
    downs = by_sender(0, low, high, core, (2, 3))
    grads = tie(grads, own_b)
    in_grads = collected({s: [part.astype(F32) for part in grads[s]] for s in range(sections)}).reshape(1, micro_count, slot_rows, width)
    small, ups, downs, in_grads, att_a = together((small, ups, downs, in_grads, att_a))
    small = small_sum(small, 2)
    got_a = from_pipe(att_a, 0, range(4))

    first_grads, half_grads = {}, {}
    rows_a = [(got_a[c].astype(F32) + got_a[2 + c].astype(F32)).reshape(4, -1, width) for c in range(2)]
    first_grads[0] = jnp.concatenate([jnp.concatenate([v[j] for v in rows_a], axis=0) for j in range(4)], axis=1)
    first_grads[1] = up_result([ups[1], ups[0]])
    half_grads[0] = jnp.concatenate(downs, axis=0)
    half_grads[1] = jnp.concatenate(downs[::-1], axis=0)
    by_bit = [own_b, *got_b]
    on = lambda target: [by_bit[p ^ target] for p in range(sections)]
    piece = att_b.shape[0]
    first_grads[2] = att_result([v[:piece] for v in on(2)])
    half_grads[2] = jnp.concatenate([v[piece:] for v in on(2)[2:]], axis=0)
    first_grads[3] = up_result(on(3)[:2])
    half_grads[3] = jnp.concatenate([v[piece:] for v in on(3)[2:]], axis=0)

    g_first = choose(place, [first_grads[s].astype(F32) for s in range(sections)])[None]
    g_half = choose(place, [half_grads[s].astype(F32) for s in range(sections)])[None]
    vec_size = sections * 3 * width
    vec_all = small[:vec_size].reshape(sections, 3, width)
    g_table = small[vec_size:].reshape(rel_table.shape)
    cols = width // dp_size
    mine = lax.dynamic_slice(vec_all, (place, 0, dp_place * cols), (1, 3, cols))
    return (section_out, in_grads, g_first, g_half, mine[:, 0], mine[:, 1], mine[:, 2], g_table)


def solution(mesh):
    in_specs = (
        P(None, "dp", None),
        P(None, "dp", None),
        P(None, "dp"),
        P("pipe", None),
        P("pipe", None),
        P("pipe", None),
        P("pipe", None, None),
        P("pipe", None, None),
        P(),
    )
    out_specs = (
        P("pipe", None, "dp", None),
        P("pipe", None, "dp", None),
        P("pipe", "dp", None),
        P("pipe", "dp", None),
        P("pipe", "dp"),
        P("pipe", "dp"),
        P("pipe", "dp"),
        P(),
    )
    return jax.shard_map(local, mesh=mesh, in_specs=in_specs, out_specs=out_specs, check_vma=False)
```
